32 devices in a mesh: dp: 4 (over y, x), sp: 8 (over z, core).
Axes of the slice: x: 2, y: 2, z: 4, core: 2. Of those that a mesh axis runs over, the one named last changes fastest.
Arguments:
- hidden_in: bfloat16 [8, 1024, 1536], P('dp', 'sp'), may hold values from -6 to 6
- w_zx: bfloat16 [1536, 6144], P(('dp', 'sp')), may hold values from -0.15625 to 0.15625
- w_bc: bfloat16 [1536, 256], P(('dp', 'sp')), may hold values from -0.15625 to 0.15625
- w_dt: bfloat16 [1536, 48], P(('dp', 'sp')), may hold values from -0.15625 to 0.15625
- norm_gain: bfloat16 [1536], P(('dp', 'sp')), may hold values from 0.5 to 1.5
- conv_bc_weight: bfloat16 [256, 4], P(('dp', 'sp')), may hold values from -3 to 3
- conv_bc_bias: bfloat16 [256], P(('dp', 'sp')), may hold values from -3 to 3
- conv_x_weight: bfloat16 [3072, 4], P('sp'), may hold values from -3 to 3
- conv_x_bias: bfloat16 [3072], P('sp'), may hold values from -3 to 3
- dt_bias: bfloat16 [48], P('sp'), may hold values from -5 to -2.296875
- a_log: bfloat16 [48], P('sp'), may hold values from 0 to 2.796875
- d_skip: bfloat16 [48], P('sp'), may hold values from 0.5 to 1.5
- gate_gain: bfloat16 [3072], P(('dp', 'sp')), may hold values from 0.5 to 1.5
- w_out: bfloat16 [3072, 1536], P(('dp', 'sp')), may hold values from -0.109375 to 0.109375
- cotangent: bfloat16 [8, 1024, 1536], P('dp', 'sp'), may hold values from -6 to 6
Outputs:
- hidden_out: bfloat16 [8, 1024, 1536], P('dp', 'sp')
- grad_hidden: bfloat16 [8, 1024, 1536], P('dp', 'sp')
- grad_w_zx: float32 [1536, 6144], P(('dp', 'sp'))
- grad_w_bc: float32 [1536, 256], P(('dp', 'sp'))
- grad_w_dt: float32 [1536, 48], P(('dp', 'sp'))
- grad_norm_gain: float32 [1536], P(('dp', 'sp'))
- grad_conv_bc_weight: float32 [256, 4], P(('dp', 'sp'))
- grad_conv_bc_bias: float32 [256], P(('dp', 'sp'))
- grad_conv_x_weight: float32 [3072, 4], P('sp')
- grad_conv_x_bias: float32 [3072], P('sp')
- grad_dt_bias: float32 [48], P('sp')
- grad_a_log: float32 [48], P('sp')
- grad_d_skip: float32 [48], P('sp')
- grad_gate_gain: float32 [3072], P(('dp', 'sp'))
- grad_w_out: float32 [3072, 1536], P(('dp', 'sp'))
The draws below stay inside these ranges and needn't reach their ends.
All inputs are finite; a program needn't handle non-finite values.
Results may differ from the reference program's by a relative error of at most 0.009.
The reference program's roundings to bfloat16 on the way count: a program that leaves them out, or rounds other values in their place, can miss the bound.
Values may be sent and summed in bfloat16 or wider, within the bound.
A program may use at most 256 MiB of HBM per device.

```python
import jax
import jax.numpy as jnp
from jax import lax

D = 1536
H = 48
P_SIZE = 64
N = 128
CONV = 4
SPAN = 256
LENGTH = 1024
INNER = 3072
SEQUENCES = 8


def shard_levels(own_key, shape, cuts, least, largest):
    loudness, own = 1.0, jax.random.fold_in(own_key, 6)
    for position, parts in cuts:
        heights = jnp.exp(jax.random.uniform(jax.random.fold_in(own, position), (parts,), jnp.float32, least / len(cuts), largest / len(cuts)))
        loudness = loudness * jnp.repeat(heights, shape[position] // parts).reshape([-1 if axis == position else 1 for axis in range(len(shape))])
    return loudness


def centred(stream_key, shape, scale, limit, cuts=(), held_as=jnp.bfloat16):
    result = scale * jax.random.normal(stream_key, shape, jnp.float32)
    if cuts:
        result = result * shard_levels(stream_key, shape, cuts, -0.22, 0.18)
    return jnp.clip(result, -limit, limit).astype(held_as)


def setup_inputs(seed: int = 0) -> dict:
    seeds = jax.random.split(jax.random.key(seed), 16)
    hidden_in = centred(seeds[0], (SEQUENCES, LENGTH, D), 1.0, 6.0, ((0, 4), (1, 8)))
    w_zx = centred(seeds[1], (D, 2 * INNER), D ** -0.5, 0.15625, ((0, 32),))
    w_bc = centred(seeds[2], (D, 2 * N), D ** -0.5, 0.15625, ((0, 32),))
    w_dt = centred(seeds[3], (D, H), D ** -0.5, 0.15625, ((0, 32),))
    norm_gain = jnp.clip(1.0 + 0.1 * jax.random.normal(seeds[4], (D,), jnp.float32), 0.5, 1.5).astype(jnp.bfloat16)
    conv_bc_weight = centred(seeds[5], (2 * N, CONV), CONV ** -0.5, 3.0, ((0, 32),))
    conv_bc_bias = centred(seeds[6], (2 * N,), 0.5, 3.0, ((0, 32),))
    conv_x_weight = centred(seeds[7], (INNER, CONV), CONV ** -0.5, 3.0, ((0, 8),))
    conv_x_bias = centred(seeds[8], (INNER,), 0.5, 3.0, ((0, 8),))
    dt_bias = jnp.clip(-5.0 + 2.703125 * jax.random.uniform(seeds[9], (H,), jnp.float32) ** shard_levels(seeds[9], (H,), ((0, 8),), -0.2, 0.2), -5.0, -2.296875).astype(jnp.bfloat16)
    a_log = jnp.clip(2.796875 * jax.random.uniform(seeds[10], (H,), jnp.float32) ** shard_levels(seeds[10], (H,), ((0, 8),), -0.2, 0.2), 0.0, 2.796875).astype(jnp.bfloat16)
    d_skip = jnp.clip(0.5 + 1.0 * jax.random.uniform(seeds[11], (H,), jnp.float32) ** shard_levels(seeds[11], (H,), ((0, 8),), -0.2, 0.2), 0.5, 1.5).astype(jnp.bfloat16)
    gate_gain = jnp.clip(1.0 + 0.1 * jax.random.normal(seeds[12], (INNER,), jnp.float32), 0.5, 1.5).astype(jnp.bfloat16)
    w_out = centred(seeds[13], (INNER, D), INNER ** -0.5, 0.109375, ((0, 32),))
    cotangent = centred(seeds[14], (SEQUENCES, LENGTH, D), 1.0, 6.0, ((0, 4), (1, 8)))
    return {"hidden_in": hidden_in, "w_zx": w_zx, "w_bc": w_bc, "w_dt": w_dt, "norm_gain": norm_gain, "conv_bc_weight": conv_bc_weight, "conv_bc_bias": conv_bc_bias, "conv_x_weight": conv_x_weight, "conv_x_bias": conv_x_bias, "dt_bias": dt_bias, "a_log": a_log, "d_skip": d_skip, "gate_gain": gate_gain, "w_out": w_out, "cotangent": cotangent}


EPS = 1e-05
HIGH = lax.Precision.HIGHEST

@jax.custom_vjp
def low(v):
    return lax.optimization_barrier(v.astype(jnp.bfloat16)).astype(jnp.float32)

@jax.custom_vjp
def low_back(v):
    return v

def low_keep(v):
    return (low(v), None)

def low_pass(kept, grad):
    return (grad,)

def back_keep(v):
    return (v, None)

def back_low(kept, grad):
    return (low(grad),)
low.defvjp(low_keep, low_pass)
low_back.defvjp(back_keep, back_low)

def matmul(left, right):
    return jnp.dot(left, right, precision=HIGH, preferred_element_type=jnp.float32)

def conv_silu(values, weight, bias):
    taps = weight.shape[1]
    length = values.shape[0]
    padded = jnp.pad(values, ((taps - 1, 0), (0, 0)))
    total = bias[None, :]
    for offset in range(taps):
        total = total + weight[:, offset][None, :] * padded[offset:offset + length, :]
    return jax.nn.silu(total)

def scan_heads(heads_x, steps, rates, bmat, cmat):
    length, heads, width = heads_x.shape
    count = length // SPAN
    states_n = bmat.shape[-1]
    x_blocks = heads_x.reshape(count, SPAN, heads, width)
    dt_blocks = steps.reshape(count, SPAN, heads)
    logs = dt_blocks * (-rates)[None, None, :]
    b_blocks = bmat.reshape(count, SPAN, states_n)
    c_blocks = cmat.reshape(count, SPAN, states_n)
    cumul = jnp.cumsum(logs, axis=1)
    differ = cumul[:, :, None, :] - cumul[:, None, :, :]
    causal = jnp.tril(jnp.ones((SPAN, SPAN), dtype=bool))
    decays = jnp.where(causal[None, :, :, None], jnp.exp(jnp.minimum(differ, 0.0)), 0.0)
    scores = jnp.einsum('cin,cjn->cij', c_blocks, b_blocks, precision=HIGH)
    weights = scores[..., None] * decays * dt_blocks[:, None, :, :]
    inside = jnp.einsum('cijh,cjhp->cihp', weights, x_blocks, precision=HIGH)
    to_end = jnp.exp(cumul[:, -1:, :] - cumul) * dt_blocks
    states = jnp.einsum('cjn,cjh,cjhp->chnp', b_blocks, to_end, x_blocks, precision=HIGH)
    factors = jnp.exp(cumul[:, -1, :])

    def advance(carry, pieces):
        state, factor = pieces
        return (carry * factor[:, None, None] + state, carry)
    start = jnp.zeros((heads, states_n, width), dtype=jnp.float32)
    _, entering = lax.scan(advance, start, (states, factors))
    across = jnp.einsum('cin,cih,chnp->cihp', c_blocks, jnp.exp(cumul), entering, precision=HIGH)
    return (inside + across).reshape(length, heads, width)

def layer(params, hidden):
    w_zx, w_bc, w_dt, norm_gain, conv_bc_weight, conv_bc_bias, conv_x_weight, conv_x_bias, dt_bias, a_log, d_skip, gate_gain, w_out = params
    inner = H * P_SIZE
    length = hidden.shape[0]
    scale_in = lax.rsqrt(lax.optimization_barrier(jnp.mean(hidden * hidden, axis=-1, keepdims=True)) + EPS)
    normed = low(hidden * scale_in * norm_gain)
    proj_zx = matmul(normed, w_zx)
    gate = low_back(low(proj_zx[:, :inner]))
    inner_x = low_back(low(proj_zx[:, inner:]))
    bc_proj = low_back(low(matmul(normed, w_bc)))
    dt_raw = low_back(low(matmul(normed, w_dt)))
    x_conv = low(conv_silu(inner_x, conv_x_weight, conv_x_bias))
    bc_conv = low(conv_silu(bc_proj, conv_bc_weight, conv_bc_bias))
    steps = jax.nn.softplus(dt_raw + dt_bias[None, :])
    rates = jnp.exp(a_log)
    heads_x = x_conv.reshape(length, H, P_SIZE)
    mixed = scan_heads(heads_x, steps, rates, bc_conv[:, :N], bc_conv[:, N:])
    mixed = mixed + d_skip[None, :, None] * heads_x
    mixed = low_back(low(mixed.reshape(length, inner)))
    gated_in = mixed * jax.nn.silu(gate)
    scale_out = lax.rsqrt(lax.optimization_barrier(jnp.mean(gated_in * gated_in, axis=-1, keepdims=True)) + EPS)
    gated = low(gated_in * scale_out * gate_gain)
    return hidden + matmul(gated, w_out)

def reference(hidden_in, w_zx, w_bc, w_dt, norm_gain, conv_bc_weight, conv_bc_bias, conv_x_weight, conv_x_bias, dt_bias, a_log, d_skip, gate_gain, w_out, cotangent):
    params = tuple((value.astype(jnp.float32) for value in (w_zx, w_bc, w_dt, norm_gain, conv_bc_weight, conv_bc_bias, conv_x_weight, conv_x_bias, dt_bias, a_log, d_skip, gate_gain, w_out)))
    hidden = hidden_in.astype(jnp.float32)

    def forward(weights, inputs):

        def single(sequence):
            return layer(weights, sequence)
        return lax.map(jax.checkpoint(single), inputs)
    output, pullback = jax.vjp(forward, params, hidden)
    grad_params, grad_input = pullback(cotangent.astype(jnp.float32))
    return (output.astype(jnp.bfloat16), grad_input.astype(jnp.bfloat16), grad_params[0], grad_params[1], grad_params[2], grad_params[3], grad_params[4], grad_params[5], grad_params[6], grad_params[7], grad_params[8], grad_params[9], grad_params[10], grad_params[11], grad_params[12])
```

```python
import functools

import jax
import jax.numpy as jnp
from jax import lax
from jax.experimental import pallas as pl
from jax.experimental.pallas import tpu as pltpu
from jax.sharding import PartitionSpec as P

P_SIZE = 64
EPS = 1e-05
F32 = jnp.float32
BF16 = jnp.bfloat16
HIGH = lax.Precision.HIGHEST
LANES = 128
VMEM_LIMIT = 48 * 1024 * 1024


def dot(left, right, dims=((1,), (0,)), precision=None):
    return lax.dot_general(
        left, right, (dims, ((), ())), precision=precision, preferred_element_type=F32
    )


def iota(shape, axis):
    return lax.broadcasted_iota(jnp.int32, shape, axis)


def spread(cols, pair, low_half):
    return jnp.where(low_half, cols[:, 2 * pair : 2 * pair + 1], cols[:, 2 * pair + 1 : 2 * pair + 2])


def spread_all(cols, pairs, low_half):
    return jnp.concatenate([spread(cols, pair, low_half) for pair in range(pairs)], axis=1)


def stack_heads(values, low_half):
    zero = jnp.zeros_like(values)
    return jnp.concatenate(
        [jnp.where(low_half, values, zero), jnp.where(low_half, zero, values)], axis=0
    )


def softplus(value):
    return jnp.maximum(value, 0.0) + jnp.log1p(jnp.exp(-jnp.abs(value)))


def conv_pre(ext, rows, taps):
    total = taps[4:5, :]
    for tap in range(4):
        total = total + taps[tap : tap + 1, :] * ext[pl.ds(5 + tap, rows), :]
    return total


def steps_of(dt_raw, head_ref):
    pre = dt_raw.astype(F32) + head_ref[0:1, :]
    steps = softplus(pre)
    return pre, steps, -steps * head_ref[1:2, :]


def scan_forward(wide, chans, zx, taps, heads, skip, mixed, enter, ext, halo, state):
    chunk, seq = pl.program_id(0), pl.program_id(1)
    rows = zx.shape[0]
    pairs = chans // LANES
    low_half = iota((rows, LANES), 1) < P_SIZE

    @pl.when(chunk == 0)
    def _():
        halo[seq] = jnp.zeros(halo.shape[1:], F32)
        state[seq] = jnp.zeros(state.shape[1:], F32)

    raw = zx[:, chans : 2 * chans + wide].astype(F32)
    ext[0:8, :] = halo[seq]
    ext[8 : 8 + rows, :] = raw
    halo[seq] = raw[rows - 8 :, :]
    pre = conv_pre(ext, rows, taps)
    act = (pre * jax.nn.sigmoid(pre)).astype(BF16)
    half = wide // 2
    bmat = act[:, chans : chans + half]
    cmat = act[:, chans + half :]
    _, steps, logs = steps_of(zx[:, 2 * chans + wide :], heads)
    earlier = iota((rows, rows), 0) >= iota((rows, rows), 1)
    cumul = dot(earlier.astype(F32), logs, precision=HIGH)
    cumul_t = cumul.T
    last = cumul[rows - 1 :, :]
    scores = dot(cmat, bmat, ((1,), (1,)))
    grown = jnp.exp(cumul)
    to_end = steps * jnp.exp(last - cumul)
    final = jnp.exp(last)
    entering = state[seq]
    enter[...] = entering.astype(BF16)
    across = dot(cmat, entering.astype(BF16))
    for pair in range(pairs):
        lanes = slice(pair * LANES, (pair + 1) * LANES)
        weights = []
        for head in (2 * pair, 2 * pair + 1):
            differ = cumul[:, head : head + 1] - cumul_t[head : head + 1, :]
            decay = jnp.where(earlier, jnp.exp(jnp.minimum(differ, 0.0)), 0.0)
            weights.append((decay * scores).astype(BF16))
        values = act[:, lanes].astype(F32)
        scaled = (values * spread(steps, pair, low_half)).astype(BF16)
        total = dot(jnp.concatenate(weights, axis=1), stack_heads(scaled, low_half))
        total = total + spread(grown, pair, low_half) * across[:, lanes]
        total = total + skip[0:1, lanes] * values
        mixed[:, lanes] = total.astype(BF16)
        ending = (values * spread(to_end, pair, low_half)).astype(BF16)
        state[seq, :, lanes] = entering[:, lanes] * spread(
            final, pair, low_half[0:1, :]
        ) + dot(bmat, ending, ((0,), (0,)))


def scan_backward(
    wide, chans, inner,
    zx, before, taps, heads, skip, gain, mixed, enter, grads, sums,
    dz, dtaps, dheads, dskip,
    ext, gext, halo, dstate,
):
    step, seq = pl.program_id(0), pl.program_id(1)
    chunk = pl.num_programs(0) - 1 - step
    rows = zx.shape[0]
    pairs = chans // LANES
    half = wide // 2
    low_half = iota((rows, LANES), 1) < P_SIZE

    @pl.when(step == 0)
    def _():
        halo[seq] = jnp.zeros(halo.shape[1:], F32)
        dstate[seq] = jnp.zeros(dstate.shape[1:], F32)

    @pl.when((step == 0) & (seq == 0))
    def _():
        dtaps[...] = jnp.zeros_like(dtaps)
        dheads[...] = jnp.zeros_like(dheads)
        dskip[...] = jnp.zeros_like(dskip)

    gate = zx[:, :chans].astype(F32)
    sig = jax.nn.sigmoid(gate)
    silu = gate * sig
    mix = mixed[...].astype(F32)
    scale = lax.rsqrt(sums[:, 0:1] * (1.0 / inner) + EPS)
    mean = sums[:, 1:2] * scale * (1.0 / inner)
    back = scale * (grads[...] * gain[0:1, :] - mix * silu * (scale * mean))
    dy_half = (back * silu).astype(BF16)
    dz[:, :chans] = (back * mix * sig * (1.0 + gate * (1.0 - sig))).astype(BF16)
    dy = dy_half.astype(F32)

    raw = zx[:, chans : 2 * chans + wide].astype(F32)
    past = before[before.shape[0] - 8 :, chans : 2 * chans + wide].astype(F32)
    ext[0:8, :] = jnp.where(chunk == 0, 0.0, past)
    ext[8 : 8 + rows, :] = raw
    pre = conv_pre(ext, rows, taps)
    sig_pre = jax.nn.sigmoid(pre)
    act = (pre * sig_pre).astype(BF16)
    slope = sig_pre * (1.0 + pre * (1.0 - sig_pre))
    bmat = act[:, chans : chans + half]
    cmat = act[:, chans + half :]
    xmat = act[:, :chans]
    xval = xmat.astype(F32)
    dt_pre, steps, logs = steps_of(zx[:, 2 * chans + wide :], heads)
    row, col = iota((rows, rows), 0), iota((rows, rows), 1)
    cumul = dot((row >= col).astype(F32), logs, precision=HIGH)
    cumul_t = cumul.T
    last = cumul[rows - 1 :, :]
    later = row <= col
    scores = dot(bmat, cmat, ((1,), (1,)))
    grown = jnp.exp(cumul)
    shrunk = jnp.exp(last - cumul)
    final = jnp.exp(last)
    entering = enter[...]
    dleave = dstate[seq]
    dleave_half = dleave.astype(BF16)
    from_state = dot(bmat, dleave_half)
    across = dot(cmat, entering)
    grown_all = spread_all(grown, pairs, low_half)
    ending_all = spread_all(steps * shrunk, pairs, low_half)
    dy_grown = (dy * grown_all).astype(BF16)
    x_end = (xval * ending_all).astype(BF16)
    dstate[seq] = dleave * spread_all(final, pairs, low_half[0:1, :]) + dot(
        cmat, dy_grown, ((0,), (0,))
    )
    owner = (iota((chans, LANES), 0) // P_SIZE == iota((chans, LANES), 1)).astype(F32)
    near = dot(xval * from_state, owner, precision=HIGH) * shrunk
    reach = dot(dy * across, owner, precision=HIGH) * grown
    kept = jnp.sum(entering.astype(F32) * dleave, axis=0, keepdims=True)
    kept = dot(jnp.broadcast_to(kept, (8, chans)), owner, precision=HIGH)[0:1, :] * final
    pairs_sum = jnp.zeros((rows, rows), F32)
    head_lane = iota((rows, LANES), 1)
    col_sum = jnp.zeros((rows, LANES), F32)
    row_sums = []
    for pair in range(pairs):
        lanes = slice(pair * LANES, (pair + 1) * LANES)
        products = dot(stack_heads(xmat[:, lanes], low_half), dy_half[:, lanes], ((1,), (1,)))
        weights = []
        for place, head in enumerate((2 * pair, 2 * pair + 1)):
            product = products[place * rows : (place + 1) * rows, :]
            differ = cumul_t[head : head + 1, :] - cumul[:, head : head + 1]
            decay = jnp.where(later, jnp.exp(jnp.minimum(differ, 0.0)), 0.0)
            weight = decay * scores
            step_col = steps[:, head : head + 1]
            weights.append(weight.astype(BF16))
            pairs_sum = pairs_sum + decay * product * step_col
            terms = weight * product
            col_sum = jnp.where(head_lane == head, jnp.sum(terms, axis=1, keepdims=True), col_sum)
            row_sums.append(jnp.sum(terms * step_col, axis=0, keepdims=True))
        inside = dot(
            jnp.concatenate(weights, axis=1), stack_heads(dy_half[:, lanes], low_half)
        )
        dx = spread(steps, pair, low_half) * (
            inside + spread(shrunk, pair, low_half) * from_state[:, lanes]
        )
        dx = dx + skip[0:1, lanes] * dy[:, lanes]
        gext[0:rows, lanes] = dx * slope[:, lanes]
    pairs_half = pairs_sum.astype(BF16)
    d_b = dot(pairs_half, cmat) + dot(x_end, dleave_half, ((1,), (1,)))
    d_c = dot(pairs_half, bmat, ((0,), (0,))) + dot(dy_grown, entering, ((1,), (1,)))
    gext[0:rows, chans : chans + half] = d_b * slope[:, chans : chans + half]
    gext[0:rows, chans + half :] = d_c * slope[:, chans + half :]

    row_sum = jnp.concatenate(
        row_sums + [jnp.zeros((LANES - 2 * pairs, rows), F32)], axis=0
    ).T
    d_logs = dot((row <= col).astype(F32), row_sum - steps * col_sum + reach, precision=HIGH)
    d_logs = d_logs + dot((row > col).astype(F32), steps * near, precision=HIGH) + kept
    d_steps = col_sum + near - heads[1:2, :] * d_logs
    d_pre = d_steps * jax.nn.sigmoid(dt_pre)
    dz[:, 2 * chans + wide :] = d_pre.astype(BF16)
    dheads[0:1, :] += jnp.sum(d_pre, axis=0, keepdims=True)
    dheads[1:2, :] += jnp.sum(d_logs * logs, axis=0, keepdims=True)
    dskip[0:1, :] += jnp.sum(dy * xval, axis=0, keepdims=True)

    gext[rows : rows + 8, :] = halo[seq]
    g = gext[0:rows, :]
    halo[seq] = g[0:8, :]
    d_in = jnp.zeros((rows, chans + wide), F32)
    for tap in range(4):
        d_in = d_in + taps[tap : tap + 1, :] * gext[pl.ds(3 - tap, rows), :]
        dtaps[tap : tap + 1, :] += jnp.sum(g * ext[pl.ds(5 + tap, rows), :], axis=0, keepdims=True)
    dtaps[4:5, :] += jnp.sum(g, axis=0, keepdims=True)
    dz[:, chans : 2 * chans + wide] = d_in.astype(BF16)


def run_forward(zx, taps, heads, skip, chans, wide):
    blocks, seqs, rows, cols = zx.shape
    states = wide // 2
    block = lambda n: pl.BlockSpec((None, None, rows, n), lambda i, j: (i, j, 0, 0))
    whole = lambda a: pl.BlockSpec(a.shape, lambda i, j: (0,) * a.ndim)
    return pl.pallas_call(
        functools.partial(scan_forward, wide, chans),
        grid=(blocks, seqs),
        in_specs=[block(cols), whole(taps), whole(heads), whole(skip)],
        out_specs=[
            block(chans),
            pl.BlockSpec((None, None, states, chans), lambda i, j: (i, j, 0, 0)),
        ],
        out_shape=[
            jax.ShapeDtypeStruct((blocks, seqs, rows, chans), BF16),
            jax.ShapeDtypeStruct((blocks, seqs, states, chans), BF16),
        ],
        scratch_shapes=[
            pltpu.VMEM((rows + 8, chans + wide), F32),
            pltpu.VMEM((seqs, 8, chans + wide), F32),
            pltpu.VMEM((seqs, states, chans), F32),
        ],
        compiler_params=pltpu.CompilerParams(vmem_limit_bytes=VMEM_LIMIT),
        name="scan_forward",
    )(zx, taps, heads, skip)


def run_backward(zx, taps, heads, skip, gain, mixed, enter, grads, sums, chans, wide, inner):
    blocks, seqs, rows, cols = zx.shape
    states = wide // 2
    back = lambda i: blocks - 1 - i
    block = lambda n: pl.BlockSpec((None, None, rows, n), lambda i, j: (back(i), j, 0, 0))
    whole = lambda a: pl.BlockSpec(a.shape, lambda i, j: (0,) * a.ndim)
    before = pl.BlockSpec(
        (None, None, 16, cols),
        lambda i, j: (jnp.maximum(back(i) - 1, 0), j, rows // 16 - 1, 0),
    )
    fixed = lambda n: pl.BlockSpec((8, n), lambda i, j: (0, 0))
    return pl.pallas_call(
        functools.partial(scan_backward, wide, chans, inner),
        grid=(blocks, seqs),
        in_specs=[
            block(cols), before, whole(taps), whole(heads), whole(skip), whole(gain),
            block(chans),
            pl.BlockSpec((None, None, states, chans), lambda i, j: (back(i), j, 0, 0)),
            block(chans), block(2),
        ],
        out_specs=[block(cols), fixed(chans + wide), fixed(LANES), fixed(chans)],
        out_shape=[
            jax.ShapeDtypeStruct(zx.shape, BF16),
            jax.ShapeDtypeStruct((8, chans + wide), F32),
            jax.ShapeDtypeStruct((8, LANES), F32),
            jax.ShapeDtypeStruct((8, chans), F32),
        ],
        scratch_shapes=[
            pltpu.VMEM((rows + 8, chans + wide), F32),
            pltpu.VMEM((rows + 8, chans + wide), F32),
            pltpu.VMEM((seqs, 8, chans + wide), F32),
            pltpu.VMEM((seqs, states, chans), F32),
        ],
        compiler_params=pltpu.CompilerParams(vmem_limit_bytes=VMEM_LIMIT),
        name="scan_backward",
    )(zx, zx, taps, heads, skip, gain, mixed, enter, grads, sums)


def pad_last(value, size):
    return jnp.pad(value, [(0, 0)] * (value.ndim - 1) + [(0, size - value.shape[-1])])


def eight_rows(*rows):
    stacked = jnp.stack(rows, axis=0)
    return jnp.pad(stacked, ((0, 8 - stacked.shape[0]), (0, 0)))


def on_device(
    dp, sp,
    hidden_in, w_zx, w_bc, w_dt, norm_gain, conv_bc_weight, conv_bc_bias,
    conv_x_weight, conv_x_bias, dt_bias, a_log, d_skip, gate_gain, w_out, cotangent,
):
    both = ("dp", "sp")
    me_dp, me_sp = lax.axis_index("dp"), lax.axis_index("sp")
    seqs, block, width = hidden_in.shape
    rows = sp * seqs * block
    wide = w_bc.shape[1]
    heads = w_dt.shape[1]
    own_heads = dt_bias.shape[0]
    inner = heads * P_SIZE
    own = own_heads * P_SIZE
    chans = -(-own // LANES) * LANES
    share = w_zx.shape[0]
    taps_n = conv_x_weight.shape[1]

    hidden_all = lax.all_gather(hidden_in, "sp", axis=0, tiled=False)
    cot_all = lax.all_gather(cotangent, "sp", axis=0, tiled=False)
    zx_parts = jnp.transpose(w_zx.reshape(share, 2, sp, own), (2, 0, 1, 3))
    zx_mine = lax.all_to_all(zx_parts, "sp", split_axis=0, concat_axis=0, tiled=True)
    zx_mine = lax.all_gather(zx_mine, "dp", axis=0, tiled=False).reshape(width, 2, own)
    bcdt = lax.all_gather(jnp.concatenate([w_bc, w_dt], axis=1), both, axis=0, tiled=True)
    dt_cols = lax.dynamic_slice_in_dim(bcdt, wide + me_sp * own_heads, own_heads, axis=1)
    weights = jnp.concatenate(
        [pad_last(zx_mine, chans).reshape(width, 2 * chans), bcdt[:, :wide], pad_last(dt_cols, LANES)],
        axis=1,
    )
    pieces = dp * sp
    to_group = [(src, (src % dp) * sp + src // dp) for src in range(pieces)]
    to_owner = [(dst, src) for src, dst in to_group]
    out_mine = lax.all_gather(
        lax.ppermute(w_out, both, to_group), "dp", axis=0, tiled=True
    )
    small = jnp.concatenate(
        [
            norm_gain.reshape(-1),
            gate_gain.reshape(-1),
            jnp.concatenate([conv_bc_weight, conv_bc_bias[:, None]], axis=1).reshape(-1),
        ]
    )
    small_all = lax.all_gather(small, both, axis=0, tiled=False)
    gate_share = gate_gain.shape[0]
    bc_share = conv_bc_bias.shape[0]
    norm_all = small_all[:, :share].reshape(width).astype(F32)
    gate_all = small_all[:, share : share + gate_share].reshape(inner)
    gate_mine = lax.dynamic_slice_in_dim(gate_all, me_sp * own, own).astype(F32)
    bc_all = small_all[:, share + gate_share :].reshape(wide, taps_n + 1).astype(F32)

    x_taps = pad_last(conv_x_weight.astype(F32).T, chans)
    x_bias = pad_last(conv_x_bias.astype(F32), chans)
    taps = jnp.concatenate(
        [
            eight_rows(*[x_taps[k] for k in range(taps_n)], x_bias),
            eight_rows(*[bc_all[:, k] for k in range(taps_n + 1)]),
        ],
        axis=1,
    )
    head_rows = eight_rows(
        pad_last(dt_bias.astype(F32), LANES), pad_last(jnp.exp(a_log.astype(F32)), LANES)
    )
    skip = eight_rows(pad_last(jnp.repeat(d_skip.astype(F32), P_SIZE), chans))
    gain = eight_rows(pad_last(gate_mine, chans))

    hidden = hidden_all.reshape(rows, width).astype(F32)
    scale_in = lax.rsqrt(jnp.mean(hidden * hidden, axis=-1, keepdims=True) + EPS)
    normed = (hidden * scale_in * norm_all).astype(BF16)
    zx = dot(normed, weights).astype(BF16)
    zx_blocks = zx.reshape(sp, seqs, block, -1)
    mixed, entering = run_forward(zx_blocks, taps, head_rows, skip, chans, wide)

    cot_rows = cot_all.reshape(rows, width)
    out_rows = jnp.pad(out_mine, ((0, chans - own), (0, 0)))
    d_gated = dot(cot_rows, out_rows, ((1,), (1,)))
    gate = zx[:, :chans].astype(F32)
    gated_in = mixed.reshape(rows, chans).astype(F32) * gate * jax.nn.sigmoid(gate)
    sums = jnp.stack(
        [
            jnp.sum(gated_in * gated_in, axis=1),
            jnp.sum(gated_in * d_gated * gain[0:1, :], axis=1),
        ],
        axis=1,
    )
    sums = lax.psum(sums, "sp")
    scale_out = lax.rsqrt(sums[:, 0:1] * (1.0 / inner) + EPS)
    gated = (gated_in * scale_out * gain[0:1, :]).astype(BF16)
    out_part = dot(gated, out_rows).astype(BF16).reshape(sp, seqs * block, width)
    out_sum = lax.psum_scatter(out_part, "sp", scatter_dimension=0, tiled=False)
    hidden_out = (
        hidden_in.astype(F32) + out_sum.astype(F32).reshape(hidden_in.shape)
    ).astype(BF16)
    out_terms = dot(gated, cot_rows, ((0,), (0,)))[:own].astype(BF16)
    out_grad = lax.psum_scatter(out_terms, "dp", scatter_dimension=0, tiled=True)
    grad_w_out = lax.ppermute(out_grad, both, to_owner).astype(F32)
    grad_gate_gain = jnp.sum(grad_w_out * w_out.astype(F32), axis=1) / gate_gain.astype(F32)

    dz, dtaps, dheads, dskip = run_backward(
        zx_blocks, taps, head_rows, skip, gain, mixed, entering,
        d_gated.reshape(sp, seqs, block, chans), sums.reshape(sp, seqs, block, 2),
        chans, wide, inner,
    )
    dz = dz.reshape(rows, -1)
    d_part = dot(dz, weights, ((1,), (1,))).astype(BF16).reshape(sp, seqs * block, width)
    d_normed = lax.psum_scatter(d_part, "sp", scatter_dimension=0, tiled=False).astype(F32)
    terms = dot(normed, dz, ((0,), (0,)))
    terms = jnp.concatenate(
        [terms[:, :own], terms[:, chans : chans + own], terms[:, 2 * chans : 2 * chans + wide + own_heads]],
        axis=1,
    ).astype(BF16)
    terms = lax.psum_scatter(terms, "dp", scatter_dimension=0, tiled=True)
    terms = terms.reshape(sp, share, -1)
    terms = lax.all_to_all(terms, "sp", split_axis=0, concat_axis=0, tiled=True).astype(F32)
    grad_w_zx = jnp.transpose(
        terms[:, :, : 2 * own].reshape(sp, share, 2, own), (1, 2, 0, 3)
    ).reshape(share, 2 * inner)
    grad_w_bc = jnp.sum(terms[:, :, 2 * own : 2 * own + wide], axis=0)
    grad_w_dt = jnp.transpose(terms[:, :, 2 * own + wide :], (1, 0, 2)).reshape(share, heads)
    grad_norm_gain = (
        jnp.sum(grad_w_zx * w_zx.astype(F32), axis=1)
        + jnp.sum(grad_w_bc * w_bc.astype(F32), axis=1)
        + jnp.sum(grad_w_dt * w_dt.astype(F32), axis=1)
    ) / norm_gain.astype(F32)

    hid = hidden_in.reshape(seqs * block, width).astype(F32)
    scale_own = lax.rsqrt(jnp.mean(hid * hid, axis=-1, keepdims=True) + EPS)
    unit_own = hid * scale_own
    weighted = d_normed * norm_all
    grad_rows = cotangent.reshape(seqs * block, width).astype(F32) + scale_own * (
        weighted - unit_own * jnp.mean(weighted * unit_own, axis=-1, keepdims=True)
    )
    grad_hidden = grad_rows.astype(BF16).reshape(hidden_in.shape)

    per_head = jnp.sum(dskip[0, :own].reshape(own_heads, P_SIZE), axis=1)
    g_x, g_dt, g_log, g_skip = lax.psum(
        (dtaps[:5, :own], dheads[0, :own_heads], dheads[1, :own_heads], per_head), "dp"
    )
    g_bc = lax.psum(dtaps[:5, chans:], both)
    mine = (me_dp * sp + me_sp) * bc_share
    g_bc = lax.dynamic_slice_in_dim(g_bc, mine, bc_share, axis=1)
    return (
        hidden_out,
        grad_hidden,
        grad_w_zx,
        grad_w_bc,
        grad_w_dt,
        grad_norm_gain,
        g_bc[:taps_n].T,
        g_bc[taps_n],
        g_x[:taps_n].T,
        g_x[taps_n],
        g_dt,
        g_log,
        g_skip,
        grad_gate_gain,
        grad_w_out,
    )


def solution(mesh):
    both = P(("dp", "sp"))
    rows = P(("dp", "sp"), None)
    tokens = P("dp", "sp", None)
    return jax.shard_map(
        functools.partial(on_device, mesh.shape["dp"], mesh.shape["sp"]),
        mesh=mesh,
        in_specs=(
            tokens, rows, rows, rows, both, rows, both, P("sp", None), P("sp"), P("sp"),
            P("sp"), P("sp"), both, rows, tokens,
        ),
        out_specs=(
            tokens, tokens, rows, rows, rows, both, rows, both, P("sp", None), P("sp"),
            P("sp"), P("sp"), P("sp"), both, rows,
        ),
        check_vma=False,
    )
```

```python
import functools

import jax
import jax.numpy as jnp
from jax import lax
from jax.experimental import pallas as pl
from jax.experimental.pallas import tpu as pltpu
from jax.sharding import PartitionSpec as P

P_SIZE = 64
EPS = 1e-05
F32 = jnp.float32
BF16 = jnp.bfloat16
HIGH = lax.Precision.HIGHEST
LANES = 128
VMEM_LIMIT = 48 * 1024 * 1024


def dot(left, right, dims=((1,), (0,)), precision=None):
    return lax.dot_general(
        left, right, (dims, ((), ())), precision=precision, preferred_element_type=F32
    )


def iota(shape, axis):
    return lax.broadcasted_iota(jnp.int32, shape, axis)


def spread(cols, pair, low_half):
    return jnp.where(low_half, cols[:, 2 * pair : 2 * pair + 1], cols[:, 2 * pair + 1 : 2 * pair + 2])


def spread_all(cols, pairs, low_half):
    return jnp.concatenate([spread(cols, pair, low_half) for pair in range(pairs)], axis=1)


def stack_heads(values, low_half):
    zero = jnp.zeros_like(values)
    return jnp.concatenate(
        [jnp.where(low_half, values, zero), jnp.where(low_half, zero, values)], axis=0
    )


def softplus(value):
    return jnp.maximum(value, 0.0) + jnp.log1p(jnp.exp(-jnp.abs(value)))


def conv_pre(ext, rows, taps):
    total = taps[4:5, :]
    for tap in range(4):
        total = total + taps[tap : tap + 1, :] * ext[pl.ds(5 + tap, rows), :]
    return total


def steps_of(dt_raw, head_ref):
    pre = dt_raw.astype(F32) + head_ref[0:1, :]
    steps = softplus(pre)
    return pre, steps, -steps * head_ref[1:2, :]


def scan_forward(wide, chans, x, bd, taps, heads, skip, mixed, enter, ext, halo, state):
    rows = x.shape[0]
    pairs = chans // LANES
    low_half = iota((rows, LANES), 1) < P_SIZE

    @pl.when(pl.program_id(0) == 0)
    def _():
        halo[...] = jnp.zeros(halo.shape, F32)
        state[...] = jnp.zeros(state.shape, F32)

    ext[0:8, :] = halo[...]
    ext[8 : 8 + rows, :chans] = x[...].astype(F32)
    ext[8 : 8 + rows, chans:] = bd[:, :wide].astype(F32)
    halo[...] = ext[rows : rows + 8, :]
    pre = conv_pre(ext, rows, taps)
    act = (pre * jax.nn.sigmoid(pre)).astype(BF16)
    half = wide // 2
    bmat = act[:, chans : chans + half]
    cmat = act[:, chans + half :]
    _, steps, logs = steps_of(bd[:, wide:], heads)
    earlier = iota((rows, rows), 0) >= iota((rows, rows), 1)
    cumul = dot(earlier.astype(F32), logs, precision=HIGH)
    cumul_t = cumul.T
    last = cumul[rows - 1 :, :]
    scores = dot(cmat, bmat, ((1,), (1,)))
    grown = jnp.exp(cumul)
    to_end = steps * jnp.exp(last - cumul)
    final = jnp.exp(last)
    entering = state[...]
    enter[...] = entering.astype(BF16)
    across = dot(cmat, entering.astype(BF16))
    for pair in range(pairs):
        lanes = slice(pair * LANES, (pair + 1) * LANES)
        weights = []
        for head in (2 * pair, 2 * pair + 1):
            differ = cumul[:, head : head + 1] - cumul_t[head : head + 1, :]
            decay = jnp.where(earlier, jnp.exp(jnp.minimum(differ, 0.0)), 0.0)
            weights.append((decay * scores).astype(BF16))
        values = act[:, lanes].astype(F32)
        scaled = (values * spread(steps, pair, low_half)).astype(BF16)
        total = dot(jnp.concatenate(weights, axis=1), stack_heads(scaled, low_half))
        total = total + spread(grown, pair, low_half) * across[:, lanes]
        total = total + skip[0:1, lanes] * values
        mixed[:, lanes] = total.astype(BF16)
        ending = (values * spread(to_end, pair, low_half)).astype(BF16)
        state[:, lanes] = entering[:, lanes] * spread(final, pair, low_half[0:1, :]) + dot(
            bmat, ending, ((0,), (0,))
        )


def scan_backward(
    wide, chans, inner,
    gate_in, x, x_before, bd, bd_before, taps, heads, skip, gain, mixed, enter, grads, sums,
    dgate, dx_out, dbd, dtaps, dheads, dskip,
    ext, gext, halo, dstate,
):
    step = pl.program_id(0)
    chunk = pl.num_programs(0) - 1 - step
    rows = x.shape[0]
    pairs = chans // LANES
    half = wide // 2
    low_half = iota((rows, LANES), 1) < P_SIZE

    @pl.when(step == 0)
    def _():
        halo[...] = jnp.zeros(halo.shape, F32)
        dstate[...] = jnp.zeros(dstate.shape, F32)
        dtaps[...] = jnp.zeros_like(dtaps)
        dheads[...] = jnp.zeros_like(dheads)
        dskip[...] = jnp.zeros_like(dskip)

    gate = gate_in[...].astype(F32)
    sig = jax.nn.sigmoid(gate)
    silu = gate * sig
    mix = mixed[...].astype(F32)
    scale = lax.rsqrt(sums[:, 0:1] * (1.0 / inner) + EPS)
    mean = sums[:, 1:2] * scale * (1.0 / inner)
    back = scale * (grads[...] * gain[0:1, :] - mix * silu * (scale * mean))
    dy_half = (back * silu).astype(BF16)
    dgate[...] = (back * mix * sig * (1.0 + gate * (1.0 - sig))).astype(BF16)
    dy = dy_half.astype(F32)

    last_rows = x_before.shape[0] - 8
    past = jnp.concatenate(
        [x_before[last_rows:, :], bd_before[last_rows:, :wide]], axis=1
    ).astype(F32)
    ext[0:8, :] = jnp.where(chunk == 0, 0.0, past)
    ext[8 : 8 + rows, :chans] = x[...].astype(F32)
    ext[8 : 8 + rows, chans:] = bd[:, :wide].astype(F32)
    pre = conv_pre(ext, rows, taps)
    sig_pre = jax.nn.sigmoid(pre)
    act = (pre * sig_pre).astype(BF16)
    slope = sig_pre * (1.0 + pre * (1.0 - sig_pre))
    bmat = act[:, chans : chans + half]
    cmat = act[:, chans + half :]
    xmat = act[:, :chans]
    xval = xmat.astype(F32)
    dt_pre, steps, logs = steps_of(bd[:, wide:], heads)
    row, col = iota((rows, rows), 0), iota((rows, rows), 1)
    cumul = dot((row >= col).astype(F32), logs, precision=HIGH)
    cumul_t = cumul.T
    last = cumul[rows - 1 :, :]
    later = row <= col
    scores = dot(bmat, cmat, ((1,), (1,)))
    grown = jnp.exp(cumul)
    shrunk = jnp.exp(last - cumul)
    final = jnp.exp(last)
    entering = enter[...]
    dleave = dstate[...]
    dleave_half = dleave.astype(BF16)
    from_state = dot(bmat, dleave_half)
    across = dot(cmat, entering)
    grown_all = spread_all(grown, pairs, low_half)
    ending_all = spread_all(steps * shrunk, pairs, low_half)
    dy_grown = (dy * grown_all).astype(BF16)
    x_end = (xval * ending_all).astype(BF16)
    dstate[...] = dleave * spread_all(final, pairs, low_half[0:1, :]) + dot(
        cmat, dy_grown, ((0,), (0,))
    )
    owner = (iota((chans, LANES), 0) // P_SIZE == iota((chans, LANES), 1)).astype(F32)
    near = dot(xval * from_state, owner, precision=HIGH) * shrunk
    reach = dot(dy * across, owner, precision=HIGH) * grown
    kept = jnp.sum(entering.astype(F32) * dleave, axis=0, keepdims=True)
    kept = dot(jnp.broadcast_to(kept, (8, chans)), owner, precision=HIGH)[0:1, :] * final
    pairs_sum = jnp.zeros((rows, rows), F32)
    head_lane = iota((rows, LANES), 1)
    col_sum = jnp.zeros((rows, LANES), F32)
    row_sums = []
    for pair in range(pairs):
        lanes = slice(pair * LANES, (pair + 1) * LANES)
        products = dot(stack_heads(xmat[:, lanes], low_half), dy_half[:, lanes], ((1,), (1,)))
        weights = []
        for place, head in enumerate((2 * pair, 2 * pair + 1)):
            product = products[place * rows : (place + 1) * rows, :]
            differ = cumul_t[head : head + 1, :] - cumul[:, head : head + 1]
            decay = jnp.where(later, jnp.exp(jnp.minimum(differ, 0.0)), 0.0)
            weight = decay * scores
            step_col = steps[:, head : head + 1]
            weights.append(weight.astype(BF16))
            pairs_sum = pairs_sum + decay * product * step_col
            terms = weight * product
            col_sum = jnp.where(head_lane == head, jnp.sum(terms, axis=1, keepdims=True), col_sum)
            row_sums.append(jnp.sum(terms * step_col, axis=0, keepdims=True))
        inside = dot(
            jnp.concatenate(weights, axis=1), stack_heads(dy_half[:, lanes], low_half)
        )
        dx = spread(steps, pair, low_half) * (
            inside + spread(shrunk, pair, low_half) * from_state[:, lanes]
        )
        dx = dx + skip[0:1, lanes] * dy[:, lanes]
        gext[0:rows, lanes] = dx * slope[:, lanes]
    pairs_half = pairs_sum.astype(BF16)
    d_b = dot(pairs_half, cmat) + dot(x_end, dleave_half, ((1,), (1,)))
    d_c = dot(pairs_half, bmat, ((0,), (0,))) + dot(dy_grown, entering, ((1,), (1,)))
    gext[0:rows, chans : chans + half] = d_b * slope[:, chans : chans + half]
    gext[0:rows, chans + half :] = d_c * slope[:, chans + half :]

    row_sum = jnp.concatenate(
        row_sums + [jnp.zeros((LANES - 2 * pairs, rows), F32)], axis=0
    ).T
    d_logs = dot((row <= col).astype(F32), row_sum - steps * col_sum + reach, precision=HIGH)
    d_logs = d_logs + dot((row > col).astype(F32), steps * near, precision=HIGH) + kept
    d_steps = col_sum + near - heads[1:2, :] * d_logs
    d_pre = d_steps * jax.nn.sigmoid(dt_pre)
    dbd[:, wide:] = d_pre.astype(BF16)
    dheads[0:1, :] += jnp.sum(d_pre, axis=0, keepdims=True)
    dheads[1:2, :] += jnp.sum(d_logs * logs, axis=0, keepdims=True)
    dskip[0:1, :] += jnp.sum(dy * xval, axis=0, keepdims=True)

    gext[rows : rows + 8, :] = halo[...]
    g = gext[0:rows, :]
    halo[...] = g[0:8, :]
    d_in = jnp.zeros((rows, chans + wide), F32)
    for tap in range(4):
        d_in = d_in + taps[tap : tap + 1, :] * gext[pl.ds(3 - tap, rows), :]
        dtaps[tap : tap + 1, :] += jnp.sum(g * ext[pl.ds(5 + tap, rows), :], axis=0, keepdims=True)
    dtaps[4:5, :] += jnp.sum(g, axis=0, keepdims=True)
    dx_out[...] = d_in[:, :chans].astype(BF16)
    dbd[:, :wide] = d_in[:, chans:].astype(BF16)


def run_forward(x, bd, taps, heads, skip, wide):
    blocks, rows, chans = x.shape
    states = wide // 2
    block = lambda n: pl.BlockSpec((None, rows, n), lambda i: (i, 0, 0))
    whole = lambda a: pl.BlockSpec(a.shape, lambda i: (0,) * a.ndim)
    return pl.pallas_call(
        functools.partial(scan_forward, wide, chans),
        grid=(blocks,),
        in_specs=[block(chans), block(bd.shape[2]), whole(taps), whole(heads), whole(skip)],
        out_specs=[block(chans), pl.BlockSpec((None, states, chans), lambda i: (i, 0, 0))],
        out_shape=[
            jax.ShapeDtypeStruct((blocks, rows, chans), BF16),
            jax.ShapeDtypeStruct((blocks, states, chans), BF16),
        ],
        scratch_shapes=[
            pltpu.VMEM((rows + 8, chans + wide), F32),
            pltpu.VMEM((8, chans + wide), F32),
            pltpu.VMEM((states, chans), F32),
        ],
        compiler_params=pltpu.CompilerParams(vmem_limit_bytes=VMEM_LIMIT),
        name="scan_forward",
    )(x, bd, taps, heads, skip)


def run_backward(gate, x, bd, taps, heads, skip, gain, mixed, enter, grads, sums, wide, inner):
    blocks, rows, chans = x.shape
    states = wide // 2
    back = lambda i: blocks - 1 - i
    block = lambda n: pl.BlockSpec((None, rows, n), lambda i: (back(i), 0, 0))
    whole = lambda a: pl.BlockSpec(a.shape, lambda i: (0,) * a.ndim)
    before = lambda n: pl.BlockSpec(
        (None, 16, n), lambda i: (jnp.maximum(back(i) - 1, 0), rows // 16 - 1, 0)
    )
    fixed = lambda n: pl.BlockSpec((8, n), lambda i: (0, 0))
    cols = bd.shape[2]
    return pl.pallas_call(
        functools.partial(scan_backward, wide, chans, inner),
        grid=(blocks,),
        in_specs=[
            block(chans), block(chans), before(chans), block(cols), before(cols),
            whole(taps), whole(heads), whole(skip), whole(gain), block(chans),
            pl.BlockSpec((None, states, chans), lambda i: (back(i), 0, 0)),
            block(chans), block(2),
        ],
        out_specs=[
            block(chans), block(chans), block(cols), fixed(chans + wide), fixed(LANES),
            fixed(chans),
        ],
        out_shape=[
            jax.ShapeDtypeStruct(x.shape, BF16),
            jax.ShapeDtypeStruct(x.shape, BF16),
            jax.ShapeDtypeStruct(bd.shape, BF16),
            jax.ShapeDtypeStruct((8, chans + wide), F32),
            jax.ShapeDtypeStruct((8, LANES), F32),
            jax.ShapeDtypeStruct((8, chans), F32),
        ],
        scratch_shapes=[
            pltpu.VMEM((rows + 8, chans + wide), F32),
            pltpu.VMEM((rows + 8, chans + wide), F32),
            pltpu.VMEM((8, chans + wide), F32),
            pltpu.VMEM((states, chans), F32),
        ],
        compiler_params=pltpu.CompilerParams(vmem_limit_bytes=VMEM_LIMIT),
        name="scan_backward",
    )(gate, x, x, bd, bd, taps, heads, skip, gain, mixed, enter, grads, sums)


MESH = pl.DeviceIdType.MESH
ANY = pl.BlockSpec(memory_space=pl.ANY)


class Place:
    def __init__(self, dp, sp, seqs):
        self.dp, self.sp, self.seqs = dp, sp, seqs
        self.groups = sp // seqs
        self.chips = sp // 2
        self.per = self.groups // 2
        self.p = lax.axis_index("dp")
        self.s = lax.axis_index("sp")
        self.chip = self.s // 2
        self.core = lax.rem(self.s, 2)
        self.seq = self.s // self.groups
        self.group = lax.rem(self.s, self.groups)
        self.low = self.seq * self.per
        self.high = self.low + self.per - 1
        self.bits = [1 << i for i in range(dp.bit_length() - 1)]

    def along_sp(self, other):
        return (self.p, other)

    def along_dp(self, other):
        return (other, self.s)

    def flip(self, bit):
        return self.p + bit - 2 * bit * lax.rem(self.p // bit, 2)

    def masked(self, mask):
        other = self.p
        for bit in self.bits:
            if mask & bit:
                other = other + bit - 2 * bit * lax.rem(self.p // bit, 2)
        return other

    def sp_peer(self, step):
        return lax.rem(self.s + step, self.sp)

    def meet(self, sp_peers=True, dp_peers=True, group_peers=False):
        barrier = pltpu.get_barrier_semaphore()
        peers = []
        if sp_peers:
            peers += [self.along_sp(self.sp_peer(i)) for i in range(1, self.sp)]
        if group_peers:
            peers += [self.along_sp(self.group_peer(i)) for i in range(1, self.groups)]
        if dp_peers:
            peers += [self.along_dp(self.masked(m)) for m in range(1, self.dp)]
        for peer in peers:
            pl.semaphore_signal(barrier, inc=1, device_id=peer, device_id_type=MESH)
        pl.semaphore_wait(barrier, len(peers))

    def group_peer(self, step):
        return self.seq * self.groups + lax.rem(self.group + step, self.groups)


def remote(src, dst, send, recv, device):
    return pltpu.make_async_remote_copy(
        src_ref=src, dst_ref=dst, send_sem=send, recv_sem=recv, device_id=device,
        device_id_type=MESH,
    )


def dma(*shape):
    return pltpu.SemaphoreType.DMA(shape)


class SequenceGather:
    @staticmethod
    def scratch(dp, sp, seqs):
        chips = sp // 2
        return [dma(6, chips), dma(seqs + 1)]

    def __init__(self, place, x, out, sems, more):
        self.at, self.x, self.out = place, x, out
        self.own, self.other, self.up, self.down, self.cross = (sems.at[i] for i in range(5))
        self.far, self.local = more, more.at[place.seqs]

    def copy(self, src, k, chip, core, send, recv):
        at = self.at
        return remote(src, self.out.at[k * 2 + at.core], send, recv, at.along_sp(chip * 2 + core))

    def passes(self, k, src):
        at = self.at
        return (
            ((k <= at.chip) & (at.chip < at.high),
             self.copy(src, k, at.chip + 1, at.core, self.up.at[k], self.own.at[k])),
            ((k >= at.chip) & (at.chip > at.low),
             self.copy(src, k, at.chip - 1, at.core, self.down.at[k], self.own.at[k])),
        )

    def crossing(self, k, src):
        at = self.at
        return self.copy(src, k, at.chip, 1 - at.core, self.cross.at[k], self.other.at[k])

    def far_copies(self):
        at = self.at
        for target in range(at.seqs):
            low = target * at.per
            entry = jnp.where(at.chip < low, low, low + at.per - 1)
            yield target != at.seq, self.copy(
                self.x.at[target], at.chip, entry, at.core, self.far.at[target],
                self.own.at[at.chip],
            )

    def keep(self):
        return pltpu.make_async_copy(self.x.at[self.at.seq], self.out.at[self.at.s], self.local)

    def start(self):
        for needed, copy in self.far_copies():
            pl.when(needed)(copy.start)
        for needed, copy in self.passes(self.at.chip, self.x.at[self.at.seq]):
            pl.when(needed)(copy.start)
        self.crossing(self.at.chip, self.x.at[self.at.seq]).start()
        self.keep().start()

    def step(self, i):
        at = self.at
        for k in (at.chip + i, at.chip - i):

            @pl.when((k >= 0) & (k < at.chips))
            def _():
                src = self.out.at[k * 2 + at.core]
                self.copy(src, k, at.chip, at.core, self.up.at[k], self.own.at[k]).wait_recv()
                for needed, copy in self.passes(k, src):
                    pl.when(needed)(copy.start)
                self.crossing(k, src).start()

    def finish(self):
        at = self.at
        for k in range(at.chips):
            dst = self.out.at[k * 2 + 1 - at.core]
            remote(dst, dst, self.cross.at[k], self.other.at[k], at.along_sp(at.s)).wait_recv()
        for k in range(at.chips):
            src = self.out.at[k * 2 + at.core]
            for needed, copy in self.passes(k, src):
                pl.when(needed)(copy.wait_send)
            self.crossing(k, src).wait_send()
        for needed, copy in self.far_copies():
            pl.when(needed)(copy.wait_send)
        self.keep().wait()


class ShardGather:
    @staticmethod
    def scratch(dp, sp, seqs):
        steps = dp.bit_length() - 1
        return [dma(2, sp), dma(sp, dp), dma(sp, dp, steps), dma(1)]

    def __init__(self, place, piece, out, along, recv, send, local):
        self.at, self.piece, self.out = place, piece, out
        self.along, self.recv, self.send, self.local = along, recv, send, local.at[0]

    def order(self, slot_parity):
        return self.at.bits if slot_parity == 0 else self.at.bits[::-1]

    def sp_copy(self, i):
        at = self.at
        target = at.sp_peer(i)
        return remote(
            self.piece(lax.rem(target, at.groups)), self.out.at[at.p, at.s],
            self.along.at[0, i], self.along.at[1, i], at.along_sp(target),
        )

    def keep(self):
        at = self.at
        return pltpu.make_async_copy(self.piece(at.group), self.out.at[at.p, at.s], self.local)

    def start(self):
        for i in range(1, self.at.sp):
            self.sp_copy(i).start()
        self.keep().start()

    def children(self, slot, parity, mask):
        at, order = self.at, self.order(parity)
        last = max([order.index(b) for b in order if mask & b], default=-1)
        src = self.out.at[at.masked(mask), slot]
        for bit in order[last + 1 :]:
            yield remote(
                src, src, self.send.at[slot, mask, at.bits.index(bit)],
                self.recv.at[slot, mask ^ bit], at.along_dp(at.flip(bit)),
            )

    def slot_of(self, i):
        at = self.at
        return lax.rem(at.s + at.sp - i, at.sp)

    def both(self, slot, fn):
        odd = lax.rem(slot, 2)
        pl.when(odd == 0)(lambda: fn(0))
        pl.when(odd == 1)(lambda: fn(1))

    def along_dp(self, i):
        at = self.at
        slot = self.slot_of(i)
        if i == 0:
            self.keep().wait()
        else:
            dst = self.out.at[at.p, slot]
            remote(dst, dst, self.along.at[0, i], self.along.at[1, i], at.along_sp(at.s)).wait_recv()
        self.both(slot, lambda odd: [copy.start() for copy in self.children(slot, odd, 0)] and None)

    def masks(self, odd):
        return [m for m in sorted(range(1, self.at.dp), key=lambda m: (bin(m).count("1"), m))]

    def forward(self, i):
        at = self.at
        slot = self.slot_of(i)

        def go(odd):
            for mask in self.masks(odd):
                dst = self.out.at[at.masked(mask), slot]
                remote(
                    dst, dst, self.send.at[slot, 0, 0], self.recv.at[slot, mask],
                    at.along_dp(at.p),
                ).wait_recv()
                for copy in self.children(slot, odd, mask):
                    copy.start()

        self.both(slot, go)

    def finish(self):
        for i in range(1, self.at.sp):
            self.sp_copy(i).wait_send()
        for slot in range(self.at.sp):
            for mask in range(self.at.dp):
                for copy in self.children(slot, slot % 2, mask):
                    copy.wait_send()


class OutGather:
    @staticmethod
    def scratch(dp, sp, seqs):
        steps = dp.bit_length() - 1
        return [dma(seqs), dma(sp), dma(2), dma(2, steps), dma(1)]

    def __init__(self, place, x, out, sent, got, recv, send, local):
        self.at, self.x, self.out = place, x, out
        self.sent, self.got, self.recv, self.send, self.local = sent, got, recv, send, local.at[0]
        self.root = place.group == place.p

    def sp_copies(self):
        at = self.at
        for target in range(at.seqs):
            device = target * at.groups + at.p
            yield device != at.s, remote(
                self.x, self.out.at[at.s], self.sent.at[target], self.got.at[at.s],
                at.along_sp(device),
            )

    def keep(self):
        return pltpu.make_async_copy(self.x, self.out.at[self.at.s], self.local)

    def start(self):
        for needed, copy in self.sp_copies():
            pl.when(needed)(copy.start)
        pl.when(self.root)(lambda: self.keep().start())

    def collect(self):
        at = self.at

        @pl.when(self.root)
        def _():
            self.keep().wait()
            for slot in range(at.sp):

                @pl.when(at.s != slot)
                def _():
                    dst = self.out.at[slot]
                    remote(dst, dst, self.sent.at[0], self.got.at[slot], at.along_sp(at.s)).wait_recv()

    def tree(self, odd):
        at = self.at
        order = at.bits if odd == 0 else at.bits[::-1]
        half = at.sp // 2
        part = self.out.at[pl.ds(odd * half, half)]
        digits = {b: (lax.rem(at.p // b, 2) != lax.rem(at.group // b, 2)) for b in at.bits}
        for place, bit in enumerate(order):
            later_clear = jnp.bool_(True)
            for b in order[place + 1 :]:
                later_clear = later_clear & jnp.logical_not(digits[b])
            copy = remote(
                part, part, self.send.at[odd, place], self.recv.at[odd], at.along_dp(at.flip(bit))
            )
            yield later_clear & jnp.logical_not(digits[bit]), later_clear & digits[bit], copy

    def spread(self):
        steps = [list(self.tree(0)), list(self.tree(1))]
        for place in range(len(steps[0])):
            for odd in range(2):
                sends, receives, copy = steps[odd][place]
                pl.when(receives)(copy.wait_recv)
                pl.when(sends)(copy.start)

    def finish(self):
        for needed, copy in self.sp_copies():
            pl.when(needed)(copy.wait_send)
        for odd in range(2):
            for sends, _, copy in self.tree(odd):
                pl.when(sends)(copy.wait_send)


class SequenceReduce:
    @staticmethod
    def scratch(dp, sp, seqs, rows, cols):
        chips = sp // 2
        return [
            pltpu.VMEM((4, chips, rows, cols), BF16),
            dma(7, chips), dma(2, seqs),
        ]

    def __init__(self, place, part, total, bufs, sems, ends):
        self.at, self.part, self.total = place, part, total
        self.acc, self.cross, self.from_low, self.from_high = (bufs.at[i] for i in range(4))
        (self.local, self.cross_send, self.cross_recv, self.chain_send, self.low_recv,
         self.high_recv, self.far_send) = (sems.at[i] for i in range(7))
        self.end_send, self.end_recv = ends.at[0], ends.at[1]

    def keep(self, k):
        at = self.at
        return pltpu.make_async_copy(self.part.at[k * 2 + at.core], self.acc.at[k], self.local.at[k])

    def crossing(self, k):
        at = self.at
        return remote(
            self.part.at[k * 2 + 1 - at.core], self.cross.at[k], self.cross_send.at[k],
            self.cross_recv.at[k], at.along_sp(at.chip * 2 + 1 - at.core),
        )

    def onward(self, k, up):
        at = self.at
        step = 1 if up else -1
        return remote(
            self.acc.at[k], (self.from_low if up else self.from_high).at[k], self.chain_send.at[k],
            (self.low_recv if up else self.high_recv).at[k],
            at.along_sp((at.chip + step) * 2 + at.core),
        )

    def ending(self, k):
        at = self.at
        return remote(
            self.acc.at[k], self.total.at[at.seq], self.far_send.at[k], self.end_recv.at[at.seq],
            at.along_sp(k * 2 + at.core),
        )

    def start(self):
        for k in range(self.at.chips):
            self.crossing(k).start()
            self.keep(k).start()

    def gather(self, k, exit_chip):
        at = self.at
        self.crossing(k).wait_recv()
        self.keep(k).wait()
        self.acc[k] = (self.acc[k].astype(F32) + self.cross[k].astype(F32)).astype(BF16)

        @pl.when((at.chip <= exit_chip) & (at.chip > at.low))
        def _():
            self.onward(k, True).wait_recv()
            self.acc[k] = (self.acc[k].astype(F32) + self.from_low[k].astype(F32)).astype(BF16)

        @pl.when((at.chip >= exit_chip) & (at.chip < at.high))
        def _():
            self.onward(k, False).wait_recv()
            self.acc[k] = (self.acc[k].astype(F32) + self.from_high[k].astype(F32)).astype(BF16)

    def exit_of(self, k):
        return jnp.clip(k, self.at.low, self.at.high)

    def run(self):
        at = self.at
        for i in range(at.chips - 1, 0, -1):
            for k in (at.chip + i, at.chip - i):

                @pl.when((k >= 0) & (k < at.chips))
                def _():
                    out = self.exit_of(k)

                    @pl.when(at.chip != out)
                    def _():
                        self.gather(k, out)
                        pl.when(at.chip < out)(lambda: self.onward(k, True).start())
                        pl.when(at.chip > out)(lambda: self.onward(k, False).start())

        for i in range(at.chips - 1, 0, -1):
            for k in (at.chip + i, at.chip - i):

                @pl.when((k >= 0) & (k < at.chips))
                def _():
                    out = self.exit_of(k)

                    @pl.when(at.chip == out)
                    def _():
                        self.gather(k, out)
                        self.ending(k).start()

        self.gather(at.chip, at.chip)
        self.total[at.seq] = self.acc[at.chip]

    def finish(self):
        at = self.at
        for target in range(at.seqs):

            @pl.when(target != at.seq)
            def _():
                dst = self.total.at[target]
                remote(dst, dst, self.end_send.at[0], self.end_recv.at[target], at.along_sp(at.s)).wait_recv()

        for k in range(at.chips):
            self.crossing(k).wait_send()
            out = self.exit_of(k)
            pl.when(at.chip < out)(lambda: self.onward(k, True).wait_send())
            pl.when(at.chip > out)(lambda: self.onward(k, False).wait_send())
            pl.when((at.chip == out) & (at.chip != k))(lambda: self.ending(k).wait_send())


class ShardReduce:
    @staticmethod
    def scratch(dp, sp, shape):
        return [
            pltpu.VMEM((dp, sp) + shape, BF16),
            dma(2, dp), dma(2, sp), dma(1),
        ]

    def __init__(self, place, terms, out, buf, along_dp, along_sp, local):
        self.at, self.terms, self.out, self.buf = place, terms, out, buf
        self.dp_sems, self.sp_sems, self.local = along_dp, along_sp, local.at[0]

    def dp_copy(self, mask):
        at = self.at
        return remote(
            self.terms.at[at.masked(mask)], self.buf.at[mask], self.dp_sems.at[0, mask],
            self.dp_sems.at[1, mask], at.along_dp(at.masked(mask)),
        )

    def keep(self):
        return pltpu.make_async_copy(self.terms.at[self.at.p], self.buf.at[0], self.local)

    def sp_copy(self, i):
        at = self.at
        target = at.sp_peer(i)
        return remote(
            self.buf.at[0, target], self.out.at[at.s], self.sp_sems.at[0, i], self.sp_sems.at[1, i],
            at.along_sp(target),
        )

    def back(self):
        at = self.at
        return pltpu.make_async_copy(self.buf.at[0, at.s], self.out.at[at.s], self.local)

    def start(self):
        for mask in range(1, self.at.dp):
            self.dp_copy(mask).start()
        self.keep().start()

    def add(self):
        at = self.at
        self.keep().wait()
        for mask in range(1, at.dp):
            self.dp_copy(mask).wait_recv()
        for i in list(range(1, at.sp)) + [0]:
            slot = at.sp_peer(i)
            total = self.buf[0, slot].astype(F32)
            for mask in range(1, at.dp):
                total = total + self.buf[mask, slot].astype(F32)
            self.buf[0, slot] = total.astype(BF16)
            if i:
                self.sp_copy(i).start()
            else:
                self.back().start()

    def finish(self):
        at = self.at
        for mask in range(1, at.dp):
            self.dp_copy(mask).wait_send()
        for i in range(1, at.sp):
            dst = self.out.at[lax.rem(at.s + at.sp - i, at.sp)]
            remote(dst, dst, self.sp_sems.at[0, i], self.sp_sems.at[1, i], at.along_sp(at.s)).wait_recv()
            self.sp_copy(i).wait_send()
        self.back().wait()


class OutReduce:
    @staticmethod
    def scratch(dp, sp, seqs, shape):
        return [pltpu.VMEM((dp, sp) + shape, BF16), dma(2, dp), dma(2, sp), dma(1 + seqs)]

    def __init__(self, place, terms, out, buf, dp_sems, sp_sems, local):
        self.at, self.terms, self.out, self.buf = place, terms, out, buf
        self.dp_sems, self.sp_sems, self.local = dp_sems, sp_sems, local
        self.root = place.group == place.p

    def dp_copy(self):
        at = self.at
        return remote(
            self.terms, self.buf.at[at.p], self.dp_sems.at[0, 0], self.dp_sems.at[1, at.p],
            at.along_dp(at.group),
        )

    def keep(self):
        return pltpu.make_async_copy(self.terms, self.buf.at[self.at.p], self.local.at[0])

    def start(self):
        pl.when(self.root)(lambda: self.keep().start())
        pl.when(jnp.logical_not(self.root))(lambda: self.dp_copy().start())

    def sp_copy(self, slot):
        at = self.at
        return remote(
            self.buf.at[at.p, slot], self.out.at[at.seq], self.sp_sems.at[0, slot],
            self.sp_sems.at[1, at.seq], at.along_sp(slot),
        )

    def add(self):
        at = self.at

        @pl.when(self.root)
        def _():
            self.keep().wait()
            for mask in range(1, at.dp):
                other = at.masked(mask)
                dst = self.buf.at[other]
                remote(
                    self.terms, dst, self.dp_sems.at[0, 0], self.dp_sems.at[1, other], at.along_dp(other)
                ).wait_recv()
            for slot in range(at.sp):
                total = self.buf[0, slot].astype(F32)
                for other in range(1, at.dp):
                    total = total + self.buf[other, slot].astype(F32)
                total = total.astype(BF16)

                @pl.when(at.s == slot)
                def _():
                    self.out[at.seq] = total

                @pl.when(at.s != slot)
                def _():
                    self.buf[at.p, slot] = total
                    self.sp_copy(slot).start()

    def finish(self):
        at = self.at
        pl.when(jnp.logical_not(self.root))(lambda: self.dp_copy().wait_send())

        @pl.when(self.root)
        def _():
            for slot in range(at.sp):
                pl.when(at.s != slot)(lambda: self.sp_copy(slot).wait_send())

        for seq in range(at.seqs):
            sender = seq * at.groups + at.p

            @pl.when(sender != at.s)
            def _():
                dst = self.out.at[seq]
                remote(dst, dst, self.sp_sems.at[0, 0], self.sp_sems.at[1, seq], at.along_sp(sender)).wait_recv()


class SmallReduce:
    @staticmethod
    def scratch(dp, sp, seqs, shape):
        return [pltpu.VMEM((dp,) + shape, F32), dma(2, dp), dma(2, sp)]

    def __init__(self, place, x, out, buf, dp_sems, sp_sems):
        self.at, self.x, self.out, self.buf = place, x, out, buf
        self.dp_sems, self.sp_sems = dp_sems, sp_sems

    def dp_copy(self, mask):
        at = self.at
        return remote(
            self.x, self.buf.at[mask], self.dp_sems.at[0, mask], self.dp_sems.at[1, mask],
            at.along_dp(at.masked(mask)),
        )

    def sp_copy(self, i):
        at = self.at
        return remote(
            self.buf.at[0], self.out.at[at.s], self.sp_sems.at[0, i], self.sp_sems.at[1, i],
            at.along_sp(at.sp_peer(i)),
        )

    def start(self):
        for mask in range(1, self.at.dp):
            self.dp_copy(mask).start()

    def add(self):
        at = self.at
        total = self.x[...]
        for mask in range(1, at.dp):
            self.dp_copy(mask).wait_recv()
            total = total + self.buf[mask]
        self.buf[0] = total
        self.out[at.s] = total
        for i in range(1, at.sp):
            self.sp_copy(i).start()

    def finish(self):
        at = self.at
        for mask in range(1, at.dp):
            self.dp_copy(mask).wait_send()
        for i in range(1, at.sp):
            dst = self.out.at[lax.rem(at.s + at.sp - i, at.sp)]
            remote(dst, dst, self.sp_sems.at[0, i], self.sp_sems.at[1, i], at.along_sp(at.s)).wait_recv()
            self.sp_copy(i).wait_send()


def comm_params(number):
    return pltpu.CompilerParams(
        collective_id=number, has_side_effects=True, vmem_limit_bytes=VMEM_LIMIT
    )


def first_kernel(dp, sp, seqs, chans, w_ref, misc_ref, hid_ref, wx_out, misc_out, hid_out, *sems):
    place = Place(dp, sp, seqs)
    inner = w_ref.shape[1] // 2
    columns = lambda g: w_ref.at[:, pl.ds(pl.multiple_of(inner + g * chans, LANES), chans)]
    wx = ShardGather(place, columns, wx_out, *sems[:4])
    misc = ShardGather(place, lambda g: misc_ref, misc_out, *sems[4:8])
    hid = SequenceGather(place, hid_ref, hid_out, *sems[8:])
    place.meet()
    misc.start()
    wx.start()
    hid.start()
    for i in range(sp):
        misc.along_dp(i)
        wx.along_dp(i)
    steps = place.chips - 1
    for i in range(1, steps + 1):
        hid.step(i)
        for slot in range((i - 1) * sp // steps, i * sp // steps):
            misc.forward(slot)
            wx.forward(slot)
    hid.finish()
    misc.finish()
    wx.finish()


def run_first(dp, sp, seqs, chans, w_zx, misc, hidden):
    share = w_zx.shape[0]
    _, rows, cols = hidden.shape
    shards = ShardGather.scratch(dp, sp, seqs)
    return pl.pallas_call(
        functools.partial(first_kernel, dp, sp, seqs, chans),
        in_specs=[ANY] * 3,
        out_specs=[ANY] * 3,
        out_shape=[
            jax.ShapeDtypeStruct((dp, sp, share, chans), BF16),
            jax.ShapeDtypeStruct((dp, sp) + misc.shape, BF16),
            jax.ShapeDtypeStruct((sp, rows, cols), BF16),
        ],
        scratch_shapes=shards + shards + SequenceGather.scratch(dp, sp, seqs),
        compiler_params=comm_params(1),
        name="first_gather",
    )(w_zx, misc, hidden)


def second_kernel(dp, sp, seqs, chans, w_ref, o_ref, cot_ref, wg_out, o_out, cot_out, *sems):
    place = Place(dp, sp, seqs)
    columns = lambda g: w_ref.at[:, pl.ds(pl.multiple_of(g * chans, LANES), chans)]
    wg = ShardGather(place, columns, wg_out, *sems[:4])
    out = OutGather(place, o_ref, o_out, *sems[4:9])
    cot = SequenceGather(place, cot_ref, cot_out, *sems[9:])
    place.meet()
    out.start()
    wg.start()
    cot.start()
    out.collect()
    out.spread()
    for i in range(sp):
        wg.along_dp(i)
    steps = place.chips - 1
    for i in range(1, steps + 1):
        cot.step(i)
        for slot in range((i - 1) * sp // steps, i * sp // steps):
            wg.forward(slot)
    cot.finish()
    out.finish()
    wg.finish()


def run_second(dp, sp, seqs, chans, w_zx, w_out, cotangent):
    share = w_zx.shape[0]
    _, rows, cols = cotangent.shape
    return pl.pallas_call(
        functools.partial(second_kernel, dp, sp, seqs, chans),
        in_specs=[ANY] * 3,
        out_specs=[ANY] * 3,
        out_shape=[
            jax.ShapeDtypeStruct((dp, sp, share, chans), BF16),
            jax.ShapeDtypeStruct((sp,) + w_out.shape, BF16),
            jax.ShapeDtypeStruct((sp, rows, cols), BF16),
        ],
        scratch_shapes=ShardGather.scratch(dp, sp, seqs)
        + OutGather.scratch(dp, sp, seqs)
        + SequenceGather.scratch(dp, sp, seqs),
        compiler_params=comm_params(2),
        name="second_gather",
    )(w_zx, w_out, cotangent)


def sums_kernel(dp, sp, seqs, own, total, got, sems):
    place = Place(dp, sp, seqs)
    place.meet(sp_peers=False, dp_peers=False, group_peers=True)
    copies = []
    for i in range(1, place.groups):
        copies.append(
            remote(
                own, got.at[i], sems.at[0, i], sems.at[1, i], place.along_sp(place.group_peer(i))
            )
        )
        copies[-1].start()
    value = own[...]
    for i, copy in enumerate(copies):
        copy.wait_recv()
        value = value + got[i + 1]
    total[...] = value
    for copy in copies:
        copy.wait_send()


def run_sums(dp, sp, seqs, own):
    groups = sp // seqs
    return pl.pallas_call(
        functools.partial(sums_kernel, dp, sp, seqs),
        in_specs=[pl.BlockSpec(memory_space=pltpu.VMEM)],
        out_specs=pl.BlockSpec(memory_space=pltpu.VMEM),
        out_shape=jax.ShapeDtypeStruct(own.shape, F32),
        scratch_shapes=[pltpu.VMEM((groups,) + own.shape, F32), dma(2, groups)],
        compiler_params=comm_params(3),
        name="norm_sums",
    )(own)


def out_reduce_kernel(dp, sp, seqs, part, total, *scratch):
    place = Place(dp, sp, seqs)
    reduce = SequenceReduce(place, part, total, *scratch)
    place.meet(dp_peers=False)
    reduce.start()
    reduce.run()
    reduce.finish()


def run_out_reduce(dp, sp, seqs, part):
    _, rows, cols = part.shape
    return pl.pallas_call(
        functools.partial(out_reduce_kernel, dp, sp, seqs),
        in_specs=[ANY],
        out_specs=pl.BlockSpec(memory_space=pltpu.VMEM),
        out_shape=jax.ShapeDtypeStruct((seqs, rows, cols), BF16),
        scratch_shapes=SequenceReduce.scratch(dp, sp, seqs, rows, cols),
        compiler_params=comm_params(4),
        name="out_reduce",
    )(part)


def last_kernel(dp, sp, seqs, part, tg, tx, tb, to, small, total, og, ox, ob, oo, osmall, *scratch):
    place = Place(dp, sp, seqs)
    reduce = SequenceReduce(place, part, total, *scratch[:3])
    shards = []
    rest = scratch[3:]
    for terms, out in ((tx, ox), (tb, ob), (tg, og)):
        shards.append(ShardReduce(place, terms, out, *rest[:4]))
        rest = rest[4:]
    outs = OutReduce(place, to, oo, *rest[:4])
    few = SmallReduce(place, small, osmall, *rest[4:])
    place.meet()
    for shard in shards:
        shard.start()
    few.start()
    outs.start()
    reduce.start()
    reduce.run()
    for shard in shards:
        shard.add()
    outs.add()
    few.add()
    reduce.finish()
    for shard in shards:
        shard.finish()
    outs.finish()
    few.finish()


def run_last(dp, sp, seqs, part, terms_gate, terms_x, terms_bd, terms_out, small):
    _, rows, cols = part.shape
    args = (part, terms_gate, terms_x, terms_bd, terms_out, small)
    scratch = SequenceReduce.scratch(dp, sp, seqs, rows, cols)
    for terms in (terms_x, terms_bd, terms_gate):
        scratch += ShardReduce.scratch(dp, sp, terms.shape[2:])
    scratch += OutReduce.scratch(dp, sp, seqs, terms_out.shape[1:])
    scratch += SmallReduce.scratch(dp, sp, seqs, small.shape)
    return pl.pallas_call(
        functools.partial(last_kernel, dp, sp, seqs),
        in_specs=[ANY] * 5 + [pl.BlockSpec(memory_space=pltpu.VMEM)],
        out_specs=[pl.BlockSpec(memory_space=pltpu.VMEM)]
        + [ANY] * 3
        + [pl.BlockSpec(memory_space=pltpu.VMEM)] * 2,
        out_shape=[
            jax.ShapeDtypeStruct((seqs, rows, cols), BF16),
            jax.ShapeDtypeStruct((sp,) + terms_gate.shape[2:], BF16),
            jax.ShapeDtypeStruct((sp,) + terms_x.shape[2:], BF16),
            jax.ShapeDtypeStruct((sp,) + terms_bd.shape[2:], BF16),
            jax.ShapeDtypeStruct((seqs,) + terms_out.shape[1:], BF16),
            jax.ShapeDtypeStruct((sp,) + small.shape, F32),
        ],
        scratch_shapes=scratch,
        compiler_params=comm_params(5),
        name="last_reduce",
    )(*args)


def pad_last(value, size):
    return jnp.pad(value, [(0, 0)] * (value.ndim - 1) + [(0, size - value.shape[-1])])


def eight_rows(*rows):
    stacked = jnp.stack(rows, axis=0)
    return jnp.pad(stacked, ((0, 8 - stacked.shape[0]), (0, 0)))


def on_device(
    dp, sp,
    hidden_in, w_zx, w_bc, w_dt, norm_gain, conv_bc_weight, conv_bc_bias,
    conv_x_weight, conv_x_bias, dt_bias, a_log, d_skip, gate_gain, w_out, cotangent,
):
    me_dp, me_sp = lax.axis_index("dp"), lax.axis_index("sp")
    seqs, block, width = hidden_in.shape
    groups = sp // seqs
    group = lax.rem(me_sp, groups)
    rows = sp * block
    wide, heads = w_bc.shape[1], w_dt.shape[1]
    share, taps_n = w_zx.shape[0], conv_x_weight.shape[1]
    inner = heads * P_SIZE
    chans = inner // groups
    own_heads = heads // groups
    gate_share, bc_share = gate_gain.shape[0], conv_bc_bias.shape[0]
    x_share, head_share = conv_x_bias.shape[0], dt_bias.shape[0]
    cols = wide + LANES

    small = jnp.concatenate(
        [
            norm_gain,
            gate_gain,
            jnp.concatenate([conv_bc_weight, conv_bc_bias[:, None]], axis=1).reshape(-1),
            jnp.concatenate([conv_x_weight, conv_x_bias[:, None]], axis=1).reshape(-1),
            dt_bias,
            a_log,
            d_skip,
        ]
    )
    high = -(-share // 16) * 16
    lines = -(-small.shape[0] // (16 * cols)) * 16
    misc = jnp.concatenate(
        [
            jnp.pad(jnp.concatenate([w_bc, w_dt], axis=1), ((0, high - share), (0, LANES - heads))),
            pad_last(small, lines * cols).reshape(lines, cols),
        ],
        axis=0,
    )
    wx, misc_all, hidden_all = run_first(dp, sp, seqs, chans, w_zx, misc, hidden_in)
    wg, out_mine, cot_all = run_second(dp, sp, seqs, chans, w_zx, w_out, cotangent)

    wx = wx.reshape(width, chans)
    bd_all = misc_all[:, :, :share, :].reshape(width, cols)
    dt_cols = lax.dynamic_slice_in_dim(bd_all[:, wide:], group * own_heads, own_heads, axis=1)
    wb = jnp.concatenate([bd_all[:, :wide], pad_last(dt_cols, LANES)], axis=1)
    few = misc_all[:, :, high:, :].reshape(dp, sp, lines * cols)
    ends = []
    for size in (share, gate_share, bc_share * (taps_n + 1), x_share * (taps_n + 1)) + (head_share,) * 3:
        ends.append(size + (ends[-1] if ends else 0))
    piece = lambda i: few[:, :, (ends[i - 1] if i else 0) : ends[i]]
    mine = lambda i: lax.dynamic_slice_in_dim(piece(i)[0], group * seqs, seqs, axis=0).astype(F32)
    norm_all = piece(0).reshape(width).astype(F32)
    gate_mine = lax.dynamic_slice_in_dim(
        piece(1).reshape(inner), group * chans, chans
    ).astype(F32)
    bc_all = piece(2).reshape(wide, taps_n + 1).astype(F32)
    x_all = mine(3).reshape(chans, taps_n + 1)
    taps = jnp.concatenate([x_all, bc_all], axis=0).T
    taps = jnp.pad(taps, ((0, 8 - taps.shape[0]), (0, 0)))
    head_rows = eight_rows(
        pad_last(mine(4).reshape(own_heads), LANES),
        pad_last(jnp.exp(mine(5).reshape(own_heads)), LANES),
    )
    skip = eight_rows(jnp.repeat(mine(6).reshape(own_heads), P_SIZE))
    gain = eight_rows(gate_mine)

    hidden = hidden_all.reshape(rows, width).astype(F32)
    scale_in = lax.rsqrt(jnp.mean(hidden * hidden, axis=-1, keepdims=True) + EPS)
    normed = (hidden * scale_in * norm_all).astype(BF16)
    x = dot(normed, wx).astype(BF16)
    bd = dot(normed, wb).astype(BF16)
    x_blocks, bd_blocks = x.reshape(sp, block, chans), bd.reshape(sp, block, cols)
    mixed, entering = run_forward(x_blocks, bd_blocks, taps, head_rows, skip, wide)

    gate = dot(normed, wg.reshape(width, chans)).astype(BF16)
    cot_rows = cot_all.reshape(rows, width)
    out_rows = out_mine.reshape(chans, width)
    d_gated = dot(cot_rows, out_rows, ((1,), (1,)))
    gate_f = gate.astype(F32)
    gated_in = mixed.reshape(rows, chans).astype(F32) * gate_f * jax.nn.sigmoid(gate_f)
    sums = jnp.stack(
        [
            jnp.sum(gated_in * gated_in, axis=1),
            jnp.sum(gated_in * d_gated * gain[0:1, :], axis=1),
        ],
        axis=0,
    )
    sums = run_sums(dp, sp, seqs, sums.reshape(2 * sp, block)).reshape(2, rows).T
    scale_out = lax.rsqrt(sums[:, 0:1] * (1.0 / inner) + EPS)
    gated = (gated_in * scale_out * gain[0:1, :]).astype(BF16)
    out_part = dot(gated, out_rows).astype(BF16).reshape(sp, block, width)
    out_sum = run_out_reduce(dp, sp, seqs, out_part)
    hidden_out = (hidden_in.astype(F32) + out_sum.astype(F32)).astype(BF16)
    terms_out = dot(gated, cot_rows, ((0,), (0,))).astype(BF16).reshape(sp, gate_share, width)

    dgate, dx, dbd, dtaps, dheads, dskip = run_backward(
        gate.reshape(sp, block, chans), x_blocks, bd_blocks, taps, head_rows, skip, gain, mixed,
        entering, d_gated.reshape(sp, block, chans), sums.reshape(sp, block, 2), wide, inner,
    )
    dgate, dx, dbd = (v.reshape(rows, -1) for v in (dgate, dx, dbd))
    d_part = (
        dot(dgate, wg.reshape(width, chans), ((1,), (1,)))
        + dot(dx, wx, ((1,), (1,)))
        + dot(dbd, wb, ((1,), (1,)))
    )
    d_part = d_part.astype(BF16).reshape(sp, block, width)
    terms = lambda v: dot(normed, v, ((0,), (0,))).astype(BF16).reshape(dp, sp, share, -1)
    small_terms = jnp.concatenate(
        [jnp.concatenate([dtaps[:5, :chans], dskip[0:1], dtaps[6:8, :chans]], axis=0),
         dtaps[:, chans:], dheads], axis=1,
    )
    d_normed, og, ox, ob, oo, osmall = run_last(
        dp, sp, seqs, d_part, terms(dgate), terms(dx), terms(dbd), terms_out, small_terms
    )
    spread_cols = lambda v: jnp.transpose(
        jnp.sum(v.astype(F32).reshape(seqs, groups, share, -1), axis=0), (1, 0, 2)
    ).reshape(share, -1)
    grad_w_zx = jnp.concatenate([spread_cols(og), spread_cols(ox)], axis=1)
    ob = ob.astype(F32)
    grad_w_bc = jnp.sum(ob[:, :, :wide], axis=0)
    grad_w_dt = spread_cols(ob[:, :, wide : wide + own_heads])
    grad_norm_gain = (
        jnp.sum(grad_w_zx * w_zx.astype(F32), axis=1)
        + jnp.sum(grad_w_bc * w_bc.astype(F32), axis=1)
        + jnp.sum(grad_w_dt * w_dt.astype(F32), axis=1)
    ) / norm_gain.astype(F32)
    grad_w_out = jnp.sum(oo.astype(F32), axis=0)
    grad_gate_gain = jnp.sum(grad_w_out * w_out.astype(F32), axis=1) / gate_gain.astype(F32)

    hid = hidden_in.reshape(seqs * block, width).astype(F32)
    scale_own = lax.rsqrt(jnp.mean(hid * hid, axis=-1, keepdims=True) + EPS)
    unit_own = hid * scale_own
    weighted = d_normed.reshape(seqs * block, width).astype(F32) * norm_all
    grad_rows = cotangent.reshape(seqs * block, width).astype(F32) + scale_own * (
        weighted - unit_own * jnp.mean(weighted * unit_own, axis=-1, keepdims=True)
    )
    grad_hidden = grad_rows.astype(BF16).reshape(hidden_in.shape)

    by_group = jnp.sum(osmall.reshape(seqs, groups, 8, -1), axis=0)
    from_group = lax.dynamic_index_in_dim(by_group, me_sp // seqs, axis=0, keepdims=False)
    part = lax.rem(me_sp, seqs)
    g_x = lax.dynamic_slice_in_dim(from_group[:, :chans], part * x_share, x_share, axis=1)
    g_heads = lax.dynamic_slice_in_dim(
        from_group[:, chans + wide :], part * head_share, head_share, axis=1
    )
    g_skip = jnp.sum(g_x[5].reshape(head_share, P_SIZE), axis=1)
    g_bc = jnp.sum(by_group[:, :, chans : chans + wide], axis=0)
    first = (me_dp * sp + me_sp) * bc_share
    g_bc = lax.dynamic_slice_in_dim(g_bc, first, bc_share, axis=1)
    return (
        hidden_out,
        grad_hidden,
        grad_w_zx,
        grad_w_bc,
        grad_w_dt,
        grad_norm_gain,
        g_bc[:taps_n].T,
        g_bc[taps_n],
        g_x[:taps_n].T,
        g_x[taps_n],
        g_heads[0],
        g_heads[1],
        g_skip,
        grad_gate_gain,
        grad_w_out,
    )


def solution(mesh):
    both = P(("dp", "sp"))
    rows = P(("dp", "sp"), None)
    tokens = P("dp", "sp", None)
    return jax.shard_map(
        functools.partial(on_device, mesh.shape["dp"], mesh.shape["sp"]),
        mesh=mesh,
        in_specs=(
            tokens, rows, rows, rows, both, rows, both, P("sp", None), P("sp"), P("sp"),
            P("sp"), P("sp"), both, rows, tokens,
        ),
        out_specs=(
            tokens, tokens, rows, rows, rows, both, rows, both, P("sp", None), P("sp"),
            P("sp"), P("sp"), P("sp"), both, rows,
        ),
        check_vma=False,
    )
```

```python
import functools

import jax
import jax.numpy as jnp
from jax import lax
from jax.experimental import pallas as pl
from jax.experimental.pallas import tpu as pltpu
from jax.sharding import PartitionSpec as P

P_SIZE = 64
EPS = 1e-05
F32 = jnp.float32
BF16 = jnp.bfloat16
HIGH = lax.Precision.HIGHEST
LANES = 128
VMEM_LIMIT = 58 * 1024 * 1024


def dot(left, right, dims=((1,), (0,)), precision=None):
    return lax.dot_general(
        left, right, (dims, ((), ())), precision=precision, preferred_element_type=F32
    )


def iota(shape, axis):
    return lax.broadcasted_iota(jnp.int32, shape, axis)


def spread(cols, pair, low_half):
    return jnp.where(low_half, cols[:, 2 * pair : 2 * pair + 1], cols[:, 2 * pair + 1 : 2 * pair + 2])


def spread_all(cols, pairs, low_half):
    return jnp.concatenate([spread(cols, pair, low_half) for pair in range(pairs)], axis=1)


def stack_heads(values, low_half):
    zero = jnp.zeros_like(values)
    return jnp.concatenate(
        [jnp.where(low_half, values, zero), jnp.where(low_half, zero, values)], axis=0
    )


def softplus(value):
    return jnp.maximum(value, 0.0) + jnp.log1p(jnp.exp(-jnp.abs(value)))


def conv_pre(ext, rows, taps):
    total = taps[4:5, :]
    for tap in range(4):
        total = total + taps[tap : tap + 1, :] * ext[pl.ds(5 + tap, rows), :]
    return total


def steps_of(dt_raw, head_ref):
    pre = dt_raw.astype(F32) + head_ref[0:1, :]
    steps = softplus(pre)
    return pre, steps, -steps * head_ref[1:2, :]


def scan_backward(
    wide, chans,
    dy_in, x, x_before, bd, bd_before, taps, heads, skip, enter,
    dx_out, dbd, dtaps, dheads, dskip,
    ext, gext, halo, dstate,
):
    step = pl.program_id(0)
    chunk = pl.num_programs(0) - 1 - step
    rows = x.shape[0]
    pairs = chans // LANES
    half = wide // 2
    low_half = iota((rows, LANES), 1) < P_SIZE

    @pl.when(step == 0)
    def _():
        halo[...] = jnp.zeros(halo.shape, F32)
        dstate[...] = jnp.zeros(dstate.shape, F32)
        dtaps[...] = jnp.zeros_like(dtaps)
        dheads[...] = jnp.zeros_like(dheads)
        dskip[...] = jnp.zeros_like(dskip)

    dy_half = dy_in[...]
    dy = dy_half.astype(F32)

    last_rows = x_before.shape[0] - 8
    past = jnp.concatenate(
        [x_before[last_rows:, :], bd_before[last_rows:, :wide]], axis=1
    ).astype(F32)
    ext[0:8, :] = jnp.where(chunk == 0, 0.0, past)
    ext[8 : 8 + rows, :chans] = x[...].astype(F32)
    ext[8 : 8 + rows, chans:] = bd[:, :wide].astype(F32)
    pre = conv_pre(ext, rows, taps)
    sig_pre = jax.nn.sigmoid(pre)
    act = (pre * sig_pre).astype(BF16)
    slope = sig_pre * (1.0 + pre * (1.0 - sig_pre))
    bmat = act[:, chans : chans + half]
    cmat = act[:, chans + half :]
    xmat = act[:, :chans]
    xval = xmat.astype(F32)
    dt_pre, steps, logs = steps_of(bd[:, wide:], heads)
    row, col = iota((rows, rows), 0), iota((rows, rows), 1)
    cumul = dot((row >= col).astype(F32), logs, precision=HIGH)
    cumul_t = cumul.T
    last = cumul[rows - 1 :, :]
    later = row <= col
    scores = dot(bmat, cmat, ((1,), (1,)))
    grown = jnp.exp(cumul)
    shrunk = jnp.exp(last - cumul)
    final = jnp.exp(last)
    entering = enter[...]
    dleave = dstate[...]
    dleave_half = dleave.astype(BF16)
    from_state = dot(bmat, dleave_half)
    across = dot(cmat, entering)
    grown_all = spread_all(grown, pairs, low_half)
    ending_all = spread_all(steps * shrunk, pairs, low_half)
    dy_grown = (dy * grown_all).astype(BF16)
    x_end = (xval * ending_all).astype(BF16)
    dstate[...] = dleave * spread_all(final, pairs, low_half[0:1, :]) + dot(
        cmat, dy_grown, ((0,), (0,))
    )
    owner = (iota((chans, LANES), 0) // P_SIZE == iota((chans, LANES), 1)).astype(F32)
    near = dot(xval * from_state, owner, precision=HIGH) * shrunk
    reach = dot(dy * across, owner, precision=HIGH) * grown
    kept = jnp.sum(entering.astype(F32) * dleave, axis=0, keepdims=True)
    kept = dot(jnp.broadcast_to(kept, (8, chans)), owner, precision=HIGH)[0:1, :] * final
    pairs_sum = jnp.zeros((rows, rows), F32)
    head_lane = iota((rows, LANES), 1)
    col_sum = jnp.zeros((rows, LANES), F32)
    row_sums = []
    for pair in range(pairs):
        lanes = slice(pair * LANES, (pair + 1) * LANES)
        products = dot(stack_heads(xmat[:, lanes], low_half), dy_half[:, lanes], ((1,), (1,)))
        weights = []
        for place, head in enumerate((2 * pair, 2 * pair + 1)):
            product = products[place * rows : (place + 1) * rows, :]
            differ = cumul_t[head : head + 1, :] - cumul[:, head : head + 1]
            decay = jnp.where(later, jnp.exp(jnp.minimum(differ, 0.0)), 0.0)
            weight = decay * scores
            step_col = steps[:, head : head + 1]
            weights.append(weight.astype(BF16))
            pairs_sum = pairs_sum + decay * product * step_col
            terms = weight * product
            col_sum = jnp.where(head_lane == head, jnp.sum(terms, axis=1, keepdims=True), col_sum)
            row_sums.append(jnp.sum(terms * step_col, axis=0, keepdims=True))
        inside = dot(
            jnp.concatenate(weights, axis=1), stack_heads(dy_half[:, lanes], low_half)
        )
        dx = spread(steps, pair, low_half) * (
            inside + spread(shrunk, pair, low_half) * from_state[:, lanes]
        )
        dx = dx + skip[0:1, lanes] * dy[:, lanes]
        gext[0:rows, lanes] = dx * slope[:, lanes]
    pairs_half = pairs_sum.astype(BF16)
    d_b = dot(pairs_half, cmat) + dot(x_end, dleave_half, ((1,), (1,)))
    d_c = dot(pairs_half, bmat, ((0,), (0,))) + dot(dy_grown, entering, ((1,), (1,)))
    gext[0:rows, chans : chans + half] = d_b * slope[:, chans : chans + half]
    gext[0:rows, chans + half :] = d_c * slope[:, chans + half :]

    row_sum = jnp.concatenate(
        row_sums + [jnp.zeros((LANES - 2 * pairs, rows), F32)], axis=0
    ).T
    d_logs = dot((row <= col).astype(F32), row_sum - steps * col_sum + reach, precision=HIGH)
    d_logs = d_logs + dot((row > col).astype(F32), steps * near, precision=HIGH) + kept
    d_steps = col_sum + near - heads[1:2, :] * d_logs
    d_pre = d_steps * jax.nn.sigmoid(dt_pre)
    dbd[:, wide:] = d_pre.astype(BF16)
    dheads[0:1, :] += jnp.sum(d_pre, axis=0, keepdims=True)
    dheads[1:2, :] += jnp.sum(d_logs * logs, axis=0, keepdims=True)
    dskip[0:1, :] += jnp.sum(dy * xval, axis=0, keepdims=True)

    gext[rows : rows + 8, :] = halo[...]
    g = gext[0:rows, :]
    halo[...] = g[0:8, :]
    d_in = jnp.zeros((rows, chans + wide), F32)
    for tap in range(4):
        d_in = d_in + taps[tap : tap + 1, :] * gext[pl.ds(3 - tap, rows), :]
        dtaps[tap : tap + 1, :] += jnp.sum(g * ext[pl.ds(5 + tap, rows), :], axis=0, keepdims=True)
    dtaps[4:5, :] += jnp.sum(g, axis=0, keepdims=True)
    dx_out[...] = d_in[:, :chans].astype(BF16)
    dbd[:, :wide] = d_in[:, chans:].astype(BF16)


MESH = pl.DeviceIdType.MESH
ANY = pl.BlockSpec(memory_space=pl.ANY)


class Place:
    def __init__(self, dp, sp, seqs):
        self.dp, self.sp, self.seqs = dp, sp, seqs
        self.groups = sp // seqs
        self.chips = sp // 2
        self.per = self.groups // 2
        self.p = lax.axis_index("dp")
        self.s = lax.axis_index("sp")
        self.chip = self.s // 2
        self.core = lax.rem(self.s, 2)
        self.seq = self.s // self.groups
        self.group = lax.rem(self.s, self.groups)
        self.low = self.seq * self.per
        self.high = self.low + self.per - 1
        self.bits = [1 << i for i in range(dp.bit_length() - 1)]

    def along_sp(self, other):
        return (self.p, other)

    def along_dp(self, other):
        return (other, self.s)

    def flip(self, bit):
        return self.p + bit - 2 * bit * lax.rem(self.p // bit, 2)

    def masked(self, mask):
        other = self.p
        for bit in self.bits:
            if mask & bit:
                other = other + bit - 2 * bit * lax.rem(self.p // bit, 2)
        return other

    def sp_peer(self, step):
        return lax.rem(self.s + step, self.sp)

    def meet(self, sp_peers=True, dp_peers=True, group_peers=False, more=0):
        barrier = pltpu.get_barrier_semaphore()
        peers = []
        if sp_peers:
            peers += [self.along_sp(self.sp_peer(i)) for i in range(1, self.sp)]
        if group_peers:
            peers += [self.along_sp(self.group_peer(i)) for i in range(1, self.groups)]
        if dp_peers:
            peers += [self.along_dp(self.masked(m)) for m in range(1, self.dp)]
        for peer in peers:
            pl.semaphore_signal(barrier, inc=1, device_id=peer, device_id_type=MESH)
        pl.semaphore_wait(barrier, len(peers) + more)

    def group_peer(self, step):
        return self.seq * self.groups + lax.rem(self.group + step, self.groups)


def remote(src, dst, send, recv, device):
    return pltpu.make_async_remote_copy(
        src_ref=src, dst_ref=dst, send_sem=send, recv_sem=recv, device_id=device,
        device_id_type=MESH,
    )


def dma(*shape):
    return pltpu.SemaphoreType.DMA(shape)


class DpTree:
    @staticmethod
    def scratch(dp):
        return [dma(2, dp), dma(2, dp, dp.bit_length() - 1)]

    def __init__(self, place, part, recv, send):
        self.at, self.part, self.recv, self.send = place, part, recv, send

    def children(self, odd, mask):
        at = self.at
        order = at.bits if odd == 0 else at.bits[::-1]
        last = max([order.index(b) for b in order if mask & b], default=-1)
        src = self.part(at.masked(mask), odd)
        return [
            remote(
                src, src, self.send.at[odd, mask, at.bits.index(bit)],
                self.recv.at[odd, mask ^ bit], at.along_dp(at.flip(bit)),
            )
            for bit in order[last + 1 :]
        ]

    def start(self, odd):
        for copy in self.children(odd, 0):
            copy.start()

    def forward(self, odd):
        at = self.at
        for mask in sorted(range(1, at.dp), key=lambda m: (bin(m).count("1"), m)):
            dst = self.part(at.masked(mask), odd)
            remote(dst, dst, self.send.at[odd, 0, 0], self.recv.at[odd, mask], at.along_dp(at.p)).wait_recv()
            for copy in self.children(odd, mask):
                copy.start()

    def finish(self):
        for odd in range(2):
            for mask in range(self.at.dp):
                for copy in self.children(odd, mask):
                    copy.wait_send()


class Owners:
    def __init__(self, place):
        self.at, self.each = place, place.sp // place.dp

    def holder(self, seq):
        at = self.at
        p, s = at.s // self.each, seq * at.groups + at.p
        return (p, s), (p == at.p) & (s == at.s)

    def owner(self, i):
        at = self.at
        p, s = at.group, at.p * self.each + i
        return (p, s), (p == at.p) & (s == at.s)

    def meet(self, spread):
        barrier = pltpu.get_barrier_semaphore()
        holders = [self.holder(seq) for seq in range(self.at.seqs)]
        owners = [self.owner(i) for i in range(self.each)]
        greet, wait = (owners, holders) if spread else (holders, owners)
        for device, mine in greet:

            @pl.when(jnp.logical_not(mine))
            def _():
                pl.semaphore_signal(barrier, inc=1, device_id=device, device_id_type=MESH)

        count = jnp.int32(0)
        for _, mine in wait:
            count = count + jnp.where(mine, 0, 1)
        return count


class OutGather:
    @staticmethod
    def scratch(dp, sp, seqs):
        return [dma(seqs), dma(sp), dma(1)] + DpTree.scratch(dp)

    def __init__(self, place, x, out, sent, got, local, *tree):
        self.at, self.x, self.out = place, x, out
        self.sent, self.got, self.local = sent, got, local.at[0]
        self.ways = Owners(place)
        each = self.ways.each
        size = each // 2
        part = lambda p, odd: out.at[pl.ds(p * each + odd * size, size)]
        self.tree = DpTree(place, part, *tree)

    def shard_copy(self, seq):
        at = self.at
        device, mine = self.ways.holder(seq)
        return jnp.logical_not(mine), remote(
            self.x, self.out.at[at.s], self.sent.at[seq], self.got.at[at.s], device
        )

    def keep(self):
        return pltpu.make_async_copy(self.x, self.out.at[self.at.s], self.local)

    def start(self):
        for seq in range(self.at.seqs):
            needed, copy = self.shard_copy(seq)
            pl.when(needed)(copy.start)
        for i in range(self.ways.each):
            pl.when(self.ways.owner(i)[1])(lambda: self.keep().start())

    def along_dp(self, odd):
        at, each = self.at, self.ways.each
        for i in range(odd * each // 2, (odd + 1) * each // 2):
            _, mine = self.ways.owner(i)
            slot = at.p * each + i
            pl.when(mine)(lambda: self.keep().wait())

            @pl.when(jnp.logical_not(mine))
            def _():
                dst = self.out.at[slot]
                remote(dst, dst, self.sent.at[0], self.got.at[slot], at.along_sp(at.s)).wait_recv()

        self.tree.start(odd)

    def forward(self, odd):
        self.tree.forward(odd)

    def finish(self):
        for seq in range(self.at.seqs):
            needed, copy = self.shard_copy(seq)
            pl.when(needed)(copy.wait_send)
        self.tree.finish()


class BlockReduce:
    @staticmethod
    def scratch(dp, sp, seqs, rows, cols, own):
        chips, sides = sp // 2, (2 if sp // seqs > 4 else 1)
        block = lambda *n: pltpu.VMEM(n + (rows, cols), BF16)
        return ([block(chips)] if own else []) + [
            block(chips), block(sides, chips), block(seqs), dma(7, chips), dma(2, seqs),
        ]

    def __init__(self, place, part, acc, cross, chain, total, sems, ends):
        self.at, self.part, self.acc = place, part, acc
        self.cross, self.chain, self.total = cross, chain, total
        (self.local, self.cross_send, self.cross_recv, self.chain_send, self.low_recv,
         self.high_recv, self.far_send) = (sems.at[i] for i in range(7))
        self.end_send, self.end_recv = ends.at[0], ends.at[1]

    def mine(self, k):
        return self.part.at[k * 2 + self.at.core] if self.acc is None else self.acc.at[k]

    def keep(self, k):
        return pltpu.make_async_copy(
            self.part.at[k * 2 + self.at.core], self.acc.at[k], self.local.at[k]
        )

    def crossing(self, k):
        at = self.at
        return remote(
            self.part.at[k * 2 + 1 - at.core], self.cross.at[k], self.cross_send.at[k],
            self.cross_recv.at[k], at.along_sp(at.chip * 2 + 1 - at.core),
        )

    def onward(self, k, up):
        at = self.at
        side = 0 if up else self.chain.shape[0] - 1
        return remote(
            self.mine(k), self.chain.at[side, k], self.chain_send.at[k],
            (self.low_recv if up else self.high_recv).at[k],
            at.along_sp((at.chip + (1 if up else -1)) * 2 + at.core),
        )

    def ending(self, k):
        at = self.at
        return remote(
            self.mine(k), self.total.at[at.seq], self.far_send.at[k], self.end_recv.at[at.seq],
            at.along_sp(k * 2 + at.core),
        )

    def exit_of(self, k):
        return jnp.clip(k, self.at.low, self.at.high)

    def add(self, k, other):
        mine = self.mine(k)
        mine[...] = (mine[...].astype(F32) + other[...].astype(F32)).astype(BF16)

    def start(self, k):
        self.crossing(k).start()
        if self.acc is not None:
            self.keep(k).start()

    def upstream(self, k, out):
        at = self.at

        @pl.when((at.chip <= out) & (at.chip > at.low))
        def _():
            self.onward(k, True).wait_recv()
            self.add(k, self.chain.at[0, k])

        @pl.when((at.chip >= out) & (at.chip < at.high))
        def _():
            self.onward(k, False).wait_recv()
            self.add(k, self.chain.at[self.chain.shape[0] - 1, k])

    def collect(self, k):
        at, out = self.at, self.exit_of(k)
        self.crossing(k).wait_recv()
        if self.acc is not None:
            self.keep(k).wait()
        self.add(k, self.cross.at[k])

        @pl.when(at.chip != out)
        def _():
            self.upstream(k, out)
            pl.when(at.chip < out)(lambda: self.onward(k, True).start())
            pl.when(at.chip > out)(lambda: self.onward(k, False).start())

    def settle(self, k):
        at, out = self.at, self.exit_of(k)

        @pl.when(at.chip == out)
        def _():
            self.upstream(k, out)

            @pl.when(k == at.chip)
            def _():
                self.total[at.seq] = self.mine(k)[...]

            @pl.when(k != at.chip)
            def _():
                self.ending(k).start()

    def finish(self):
        at = self.at
        for target in range(at.seqs):

            @pl.when(target != at.seq)
            def _():
                dst = self.total.at[target]
                remote(dst, dst, self.end_send.at[0], self.end_recv.at[target], at.along_sp(at.s)).wait_recv()

        for k in range(at.chips):
            out = self.exit_of(k)
            self.crossing(k).wait_send()
            pl.when(at.chip < out)(lambda: self.onward(k, True).wait_send())
            pl.when(at.chip > out)(lambda: self.onward(k, False).wait_send())
            pl.when((at.chip == out) & (at.chip != k))(lambda: self.ending(k).wait_send())


class ShardReduce:
    @staticmethod
    def scratch(dp, sp, shape):
        return [
            pltpu.VMEM((dp, sp) + shape, BF16),
            dma(2, dp), dma(2, sp), dma(1),
        ]

    def __init__(self, place, terms, out, buf, along_dp, along_sp, local):
        self.at, self.terms, self.out, self.buf = place, terms, out, buf
        self.dp_sems, self.sp_sems, self.local = along_dp, along_sp, local.at[0]

    def dp_copy(self, mask):
        at = self.at
        return remote(
            self.terms.at[at.masked(mask)], self.buf.at[mask], self.dp_sems.at[0, mask],
            self.dp_sems.at[1, mask], at.along_dp(at.masked(mask)),
        )

    def keep(self):
        return pltpu.make_async_copy(self.terms.at[self.at.p], self.buf.at[0], self.local)

    def sp_copy(self, i):
        at = self.at
        target = at.sp_peer(i)
        return remote(
            self.buf.at[0, target], self.out.at[at.s], self.sp_sems.at[0, i], self.sp_sems.at[1, i],
            at.along_sp(target),
        )

    def back(self):
        at = self.at
        return pltpu.make_async_copy(self.buf.at[0, at.s], self.out.at[at.s], self.local)

    def start(self):
        for mask in range(1, self.at.dp):
            self.dp_copy(mask).start()
        self.keep().start()

    def add(self, kept=True):
        at = self.at
        if kept:
            self.keep().wait()
        for mask in range(1, at.dp):
            self.dp_copy(mask).wait_recv()
        for i in list(range(1, at.sp)) + [0]:
            slot = at.sp_peer(i)
            total = self.buf[0, slot].astype(F32)
            for mask in range(1, at.dp):
                total = total + self.buf[mask, slot].astype(F32)
            self.buf[0, slot] = total.astype(BF16)
            if i:
                self.sp_copy(i).start()
            else:
                self.back().start()

    def finish(self):
        at = self.at
        for mask in range(1, at.dp):
            self.dp_copy(mask).wait_send()
        for i in range(1, at.sp):
            dst = self.out.at[lax.rem(at.s + at.sp - i, at.sp)]
            remote(dst, dst, self.sp_sems.at[0, i], self.sp_sems.at[1, i], at.along_sp(at.s)).wait_recv()
            self.sp_copy(i).wait_send()
        self.back().wait()


class OutReduce:
    @staticmethod
    def scratch(dp, sp, seqs, shape):
        each = sp // dp
        return [pltpu.VMEM((dp, each) + shape, BF16), dma(2, dp), dma(each), dma(seqs), dma(2)]

    def __init__(self, place, terms, out, buf, dp_sems, sent, got, local):
        self.at, self.terms, self.out, self.buf = place, terms, out, buf
        self.dp_sems, self.sent, self.got, self.local = dp_sems, sent, got, local
        self.ways = Owners(place)

    def shards(self, p):
        return self.terms.at[pl.ds(p * self.ways.each, self.ways.each)]

    def dp_copy(self, mask):
        at = self.at
        return remote(
            self.shards(at.masked(mask)), self.buf.at[mask], self.dp_sems.at[0, mask],
            self.dp_sems.at[1, mask], at.along_dp(at.masked(mask)),
        )

    def keep(self):
        return pltpu.make_async_copy(self.shards(self.at.p), self.buf.at[0], self.local.at[0])

    def start(self):
        for mask in range(1, self.at.dp):
            self.dp_copy(mask).start()
        self.keep().start()

    def shard_copy(self, i):
        at = self.at
        device, mine = self.ways.owner(i)
        return mine, remote(
            self.buf.at[0, i], self.out.at[at.seq], self.sent.at[i], self.got.at[at.seq], device
        )

    def back(self, i):
        return pltpu.make_async_copy(self.buf.at[0, i], self.out.at[self.at.seq], self.local.at[1])

    def add(self):
        at = self.at
        self.keep().wait()
        for mask in range(1, at.dp):
            self.dp_copy(mask).wait_recv()
        for i in range(self.ways.each):
            total = self.buf[0, i].astype(F32)
            for mask in range(1, at.dp):
                total = total + self.buf[mask, i].astype(F32)
            self.buf[0, i] = total.astype(BF16)
            mine, copy = self.shard_copy(i)
            pl.when(jnp.logical_not(mine))(copy.start)
            pl.when(mine)(lambda: self.back(i).start())

    def finish(self):
        at = self.at
        for mask in range(1, at.dp):
            self.dp_copy(mask).wait_send()
        for i in range(self.ways.each):
            mine, copy = self.shard_copy(i)
            pl.when(jnp.logical_not(mine))(copy.wait_send)
            pl.when(mine)(lambda: self.back(i).wait())
        for seq in range(at.seqs):
            _, mine = self.ways.holder(seq)

            @pl.when(jnp.logical_not(mine))
            def _():
                dst = self.out.at[seq]
                remote(dst, dst, self.sent.at[0], self.got.at[seq], at.along_sp(at.s)).wait_recv()


class SmallReduce:
    @staticmethod
    def scratch(dp, sp, seqs, shape):
        return [pltpu.VMEM((dp,) + shape, F32), dma(2, dp), dma(2, sp)]

    def __init__(self, place, x, out, buf, dp_sems, sp_sems):
        self.at, self.x, self.out, self.buf = place, x, out, buf
        self.dp_sems, self.sp_sems = dp_sems, sp_sems

    def dp_copy(self, mask):
        at = self.at
        return remote(
            self.x, self.buf.at[mask], self.dp_sems.at[0, mask], self.dp_sems.at[1, mask],
            at.along_dp(at.masked(mask)),
        )

    def sp_copy(self, i):
        at = self.at
        return remote(
            self.buf.at[0], self.out.at[at.s], self.sp_sems.at[0, i], self.sp_sems.at[1, i],
            at.along_sp(at.sp_peer(i)),
        )

    def start(self):
        for mask in range(1, self.at.dp):
            self.dp_copy(mask).start()

    def add(self):
        at = self.at
        total = self.x[...]
        for mask in range(1, at.dp):
            self.dp_copy(mask).wait_recv()
            total = total + self.buf[mask]
        self.buf[0] = total
        self.out[at.s] = total
        for i in range(1, at.sp):
            self.sp_copy(i).start()

    def finish(self):
        at = self.at
        for mask in range(1, at.dp):
            self.dp_copy(mask).wait_send()
        for i in range(1, at.sp):
            dst = self.out.at[lax.rem(at.s + at.sp - i, at.sp)]
            remote(dst, dst, self.sp_sems.at[0, i], self.sp_sems.at[1, i], at.along_sp(at.s)).wait_recv()
            self.sp_copy(i).wait_send()


def comm_params(number):
    return pltpu.CompilerParams(
        collective_id=number, has_side_effects=True, vmem_limit_bytes=VMEM_LIMIT
    )


class BlockGather:
    @staticmethod
    def scratch(dp, sp, seqs):
        return [dma(5, sp // 2)]

    def __init__(self, place, x, out, sems):
        self.at, self.x, self.out = place, x, out
        self.send, self.recv, self.cross_send, self.cross_recv, self.local = (
            sems.at[i] for i in range(5)
        )

    def chip_at(self, i):
        return lax.rem(self.at.chip + i, self.at.chips)

    def chip_copy(self, i):
        at = self.at
        chip = self.chip_at(i)
        return remote(
            self.x.at[chip // at.per], self.out.at[at.s], self.send.at[i], self.recv.at[at.chip],
            at.along_sp(chip * 2 + at.core),
        )

    def keep(self):
        return pltpu.make_async_copy(self.x.at[self.at.seq], self.out.at[self.at.s], self.local.at[0])

    def crossing(self, k, src):
        at = self.at
        return remote(
            src, self.out.at[k * 2 + at.core], self.cross_send.at[k], self.cross_recv.at[k],
            at.along_sp(at.chip * 2 + 1 - at.core),
        )

    def start(self):
        for i in range(1, self.at.chips):
            self.chip_copy(i).start()
        self.crossing(self.at.chip, self.x.at[self.at.seq]).start()
        self.keep().start()

    def arrive(self, i):
        at = self.at
        k = self.chip_at(i)
        dst = self.out.at[k * 2 + at.core]

        @pl.when(i == 0)
        def _():
            self.keep().wait()

        @pl.when(i != 0)
        def _():
            remote(dst, dst, self.send.at[0], self.recv.at[k], at.along_sp(at.s)).wait_recv()
            self.crossing(k, dst).start()

        return k * 2 + at.core

    def arrive_other(self, i):
        at = self.at
        k = self.chip_at(i)
        dst = self.out.at[k * 2 + 1 - at.core]
        remote(dst, dst, self.cross_send.at[0], self.cross_recv.at[k], at.along_sp(at.s)).wait_recv()
        return k * 2 + 1 - at.core

    def finish(self):
        for i in range(1, self.at.chips):
            self.chip_copy(i).wait_send()
        for k in range(self.at.chips):
            self.crossing(k, self.out.at[k * 2 + self.at.core]).wait_send()


class ColumnGather:
    @staticmethod
    def scratch(dp, sp, seqs):
        return [dma(2, sp), dma(1)] + DpTree.scratch(dp)

    def __init__(self, place, piece, out, along, local, *tree):
        self.at, self.piece, self.out = place, piece, out
        self.along, self.local = along, local.at[0]
        size = place.sp // 2
        self.tree = DpTree(place, lambda p, odd: out.at[p, pl.ds(odd * size, size)], *tree)

    def sp_copy(self, i):
        at = self.at
        target = at.sp_peer(i)
        return remote(
            self.piece(lax.rem(target, at.groups)), self.out.at[at.p, at.s],
            self.along.at[0, i], self.along.at[1, at.s], at.along_sp(target),
        )

    def keep(self):
        at = self.at
        return pltpu.make_async_copy(self.piece(at.group), self.out.at[at.p, at.s], self.local)

    def start(self):
        for i in range(1, self.at.sp):
            self.sp_copy(i).start()
        self.keep().start()

    def along_dp(self, odd):
        at = self.at
        size = at.sp // 2
        for slot in range(odd * size, (odd + 1) * size):

            @pl.when(at.s == slot)
            def _():
                self.keep().wait()

            @pl.when(at.s != slot)
            def _():
                dst = self.out.at[at.p, slot]
                remote(dst, dst, self.along.at[0, 0], self.along.at[1, slot], at.along_sp(at.s)).wait_recv()

        self.tree.start(odd)

    def forward(self, odd):
        self.tree.forward(odd)

    def finish(self):
        for i in range(1, self.at.sp):
            self.sp_copy(i).wait_send()
        self.tree.finish()


class CommonGather:
    @staticmethod
    def scratch(dp, sp, seqs):
        return [dma(2, sp // 2), dma(2, dp), dma(3)]

    def __init__(self, place, x, out, along, across, ends):
        self.at, self.x, self.out = place, x, out
        self.along, self.across, self.ends = along, across, ends

    def chip_copy(self, i):
        at = self.at
        chip = lax.rem(at.chip + i, at.chips)
        return remote(
            self.x, self.out.at[at.core, at.p, at.chip], self.along.at[0, i],
            self.along.at[1, at.chip], at.along_sp(chip * 2 + at.core),
        )

    def keep(self):
        at = self.at
        return pltpu.make_async_copy(self.x, self.out.at[at.core, at.p, at.chip], self.ends.at[0])

    def dp_copy(self, mask):
        at = self.at
        src = self.out.at[at.core, at.p]
        return remote(
            src, src, self.across.at[0, mask], self.across.at[1, mask], at.along_dp(at.masked(mask))
        )

    def crossing(self):
        at = self.at
        src = self.out.at[at.core]
        return remote(
            src, src, self.ends.at[1], self.ends.at[2], at.along_sp(at.chip * 2 + 1 - at.core)
        )

    def start(self):
        for i in range(1, self.at.chips):
            self.chip_copy(i).start()
        self.keep().start()

    def along_dp(self):
        at = self.at
        self.keep().wait()
        for i in range(1, at.chips):
            k = lax.rem(at.chip + i, at.chips)
            dst = self.out.at[at.core, at.p, k]
            remote(dst, dst, self.along.at[0, 0], self.along.at[1, k], at.along_sp(at.s)).wait_recv()
        for mask in range(1, at.dp):
            self.dp_copy(mask).start()

    def cross(self):
        at = self.at
        for mask in range(1, at.dp):
            dst = self.out.at[at.core, at.masked(mask)]
            remote(dst, dst, self.across.at[0, 0], self.across.at[1, mask], at.along_dp(at.p)).wait_recv()
        self.crossing().start()

    def finish(self):
        at = self.at
        dst = self.out.at[1 - at.core]
        remote(dst, dst, self.ends.at[1], self.ends.at[2], at.along_sp(at.s)).wait_recv()
        self.crossing().wait_send()
        for mask in range(1, at.dp):
            self.dp_copy(mask).wait_send()
        for i in range(1, at.chips):
            self.chip_copy(i).wait_send()


def first_kernel(dp, sp, seqs, chans, w_ref, misc_ref, hid_ref, wx_out, misc_out, hid_out, *sems):
    place = Place(dp, sp, seqs)
    inner = w_ref.shape[1] // 2
    columns = lambda g: w_ref.at[:, pl.ds(pl.multiple_of(inner + g * chans, LANES), chans)]
    wx = ColumnGather(place, columns, wx_out, *sems[:4])
    misc = CommonGather(place, misc_ref, misc_out, *sems[4:7])
    hid = BlockGather(place, hid_ref, hid_out, *sems[7:])
    place.meet()
    misc.start()
    wx.start()
    hid.start()
    misc.along_dp()
    wx.along_dp(0)
    wx.along_dp(1)
    misc.cross()
    hid.arrive(0)
    hid.arrive(1)
    wx.forward(0)
    wx.forward(1)
    for i in range(2, place.chips):
        hid.arrive(i)
    for i in range(place.chips):
        hid.arrive_other(i)
    misc.finish()
    wx.finish()
    hid.finish()


def run_first(dp, sp, seqs, chans, w_zx, misc, hidden):
    share = w_zx.shape[0]
    _, rows, cols = hidden.shape
    return pl.pallas_call(
        functools.partial(first_kernel, dp, sp, seqs, chans),
        in_specs=[ANY] * 3,
        out_specs=[ANY] * 3,
        out_shape=[
            jax.ShapeDtypeStruct((dp, sp, share, chans), BF16),
            jax.ShapeDtypeStruct((2, dp, sp // 2) + misc.shape, BF16),
            jax.ShapeDtypeStruct((sp, rows, cols), BF16),
        ],
        scratch_shapes=ColumnGather.scratch(dp, sp, seqs)
        + CommonGather.scratch(dp, sp, seqs)
        + BlockGather.scratch(dp, sp, seqs),
        compiler_params=comm_params(1),
        name="first_gather",
    )(w_zx, misc, hidden)


def scan_block(wide, chans, x, bd, taps, heads, skip, mixed, enter, ext, halo, state):
    rows = x.shape[0]
    pairs = chans // LANES
    low_half = iota((rows, LANES), 1) < P_SIZE
    ext[0:8, :] = halo[...]
    ext[8 : 8 + rows, :chans] = x.astype(F32)
    ext[8 : 8 + rows, chans:] = bd[:, :wide].astype(F32)
    halo[...] = ext[rows : rows + 8, :]
    pre = conv_pre(ext, rows, taps)
    act = (pre * jax.nn.sigmoid(pre)).astype(BF16)
    half = wide // 2
    bmat = act[:, chans : chans + half]
    cmat = act[:, chans + half :]
    _, steps, logs = steps_of(bd[:, wide:], heads)
    earlier = iota((rows, rows), 0) >= iota((rows, rows), 1)
    cumul = dot(earlier.astype(F32), logs, precision=HIGH)
    cumul_t = cumul.T
    last = cumul[rows - 1 :, :]
    scores = dot(cmat, bmat, ((1,), (1,)))
    grown = jnp.exp(cumul)
    to_end = steps * jnp.exp(last - cumul)
    final = jnp.exp(last)
    entering = state[...]
    entering_half = entering.astype(BF16)
    enter[...] = entering_half
    across = dot(cmat, entering_half)
    for pair in range(pairs):
        lanes = slice(pair * LANES, (pair + 1) * LANES)
        weights = []
        for head in (2 * pair, 2 * pair + 1):
            differ = cumul[:, head : head + 1] - cumul_t[head : head + 1, :]
            decay = jnp.where(earlier, jnp.exp(jnp.minimum(differ, 0.0)), 0.0)
            weights.append((decay * scores).astype(BF16))
        values = act[:, lanes].astype(F32)
        scaled = (values * spread(steps, pair, low_half)).astype(BF16)
        total = dot(jnp.concatenate(weights, axis=1), stack_heads(scaled, low_half))
        total = total + spread(grown, pair, low_half) * across[:, lanes]
        total = total + skip[0:1, lanes] * values
        mixed[:, lanes] = total.astype(BF16)
        ending = (values * spread(to_end, pair, low_half)).astype(BF16)
        state[:, lanes] = entering[:, lanes] * spread(final, pair, low_half[0:1, :]) + dot(
            bmat, ending, ((0,), (0,))
        )


def forward_kernel(
    dp, sp, seqs, wide, inner,
    w_ref, o_ref, cot_ref, hid_ref, wx_ref, wb_ref, norm, taps, heads, skip, gain,
    wg_out, o_out, cot_out, normed_out, x_out, bd_out, enter_out, gated_out, dgate_out, dy_out,
    hid, wx, wb, wg, rows_out, cot, normed, x, bd, mixed, enter, gate, d_gated, gated, dgate, dy,
    ext, halo, state, sums, got, saves, sum_sems, *sems,
):
    place = Place(dp, sp, seqs)
    chans = wx.shape[1]
    blocks, rows, width = hid.shape
    columns = lambda g: w_ref.at[:, pl.ds(pl.multiple_of(g * chans, LANES), chans)]
    wg_comm = ColumnGather(place, columns, wg, *sems[:4])
    out_comm = OutGather(place, o_ref, rows_out, *sems[4:9])
    cot_comm = BlockGather(place, cot_ref, cot, *sems[9:])
    loads = [
        pltpu.make_async_copy(src, dst, saves.at[7, i])
        for i, (src, dst) in enumerate(((hid_ref, hid), (wx_ref, wx), (wb_ref, wb)))
    ]
    for load in loads:
        load.start()
    place.meet(more=out_comm.ways.meet(True))
    out_comm.start()
    wg_comm.start()
    cot_comm.start()
    halo[...] = jnp.zeros(halo.shape, F32)
    state[...] = jnp.zeros(state.shape, F32)
    sums[...] = jnp.zeros(sums.shape, F32)
    for load in loads:
        load.wait()

    def save(src, dst, index, b):
        return pltpu.make_async_copy(src.at[b], dst.at[b], saves.at[index, b])

    early = ((normed, normed_out), (x, x_out), (bd, bd_out), (enter, enter_out))
    late = ((gated, gated_out), (dgate, dgate_out), (dy, dy_out))

    def first(b, carry):
        @pl.when(b == blocks // 2 - 1)
        def _():
            for odd in range(2):
                out_comm.along_dp(odd)

        @pl.when(b == blocks // 2)
        def _():
            for odd in range(2):
                wg_comm.along_dp(odd)

        @pl.when(b == blocks - 1)
        def _():
            for odd in range(2):
                out_comm.forward(odd)

        hidden = hid[b].astype(F32)
        scale = lax.rsqrt(jnp.mean(hidden * hidden, axis=-1, keepdims=True) + EPS)
        normed[b] = (hidden * scale * norm[0:1, :]).astype(BF16)
        x[b] = dot(normed[b], wx[...]).astype(BF16)
        bd[b] = dot(normed[b], wb[...]).astype(BF16)
        scan_block(
            wide, chans, x[b], bd[b], taps, heads, skip, mixed.at[b], enter.at[b], ext, halo, state
        )
        for index, (src, dst) in enumerate(early):
            save(src, dst, index, b).start()
        return carry

    lax.fori_loop(0, blocks, first, 0)
    wg_comm.forward(0)
    wg_comm.forward(1)
    lane = iota((rows, LANES), 1)

    def gates(b):
        gate[b] = dot(normed[b], wg[...].reshape(width, chans)).astype(BF16)

    def second(b):
        d_gated[b] = dot(cot[b], rows_out[...].reshape(chans, width), ((1,), (1,)))
        gate_f = gate[b].astype(F32)
        value = mixed[b].astype(F32) * gate_f * jax.nn.sigmoid(gate_f)
        square = jnp.sum(value * value, axis=1, keepdims=True)
        cross = jnp.sum(value * d_gated[b] * gain[0:1, :], axis=1, keepdims=True)
        sums[...] = sums[...] + jnp.where(lane == 2 * b, square, 0.0) + jnp.where(
            lane == 2 * b + 1, cross, 0.0
        )

    def gates_loop(b, carry):
        gates(b)
        return carry

    lax.fori_loop(0, blocks, gates_loop, 0)

    def own_core(i, carry):
        second(cot_comm.arrive(i))
        return carry

    def other_core(i, carry):
        second(cot_comm.arrive_other(i))
        return carry

    lax.fori_loop(0, place.chips, own_core, 0)
    lax.fori_loop(0, place.chips, other_core, 0)

    copies = [
        remote(sums, got.at[i], sum_sems.at[0, i], sum_sems.at[1, i], place.along_sp(place.group_peer(i)))
        for i in range(1, place.groups)
    ]
    for copy in copies:
        copy.start()
    keep_cot = pltpu.make_async_copy(cot, cot_out, saves.at[7, 0])
    keep_wg = pltpu.make_async_copy(wg, wg_out, saves.at[7, 1])
    keep_out = pltpu.make_async_copy(rows_out, o_out, saves.at[7, 2])
    for keep in (keep_cot, keep_wg, keep_out):
        keep.start()
    total = sums[...]
    for i, copy in enumerate(copies):
        copy.wait_recv()
        total = total + got[i + 1]
    got[0] = total

    def third(b, carry):
        total = got[0]
        square = jnp.sum(jnp.where(lane == 2 * b, total, 0.0), axis=1, keepdims=True)
        cross = jnp.sum(jnp.where(lane == 2 * b + 1, total, 0.0), axis=1, keepdims=True)
        scale = lax.rsqrt(square * (1.0 / inner) + EPS)
        mean = cross * scale * (1.0 / inner)
        gate_f = gate[b].astype(F32)
        sig = jax.nn.sigmoid(gate_f)
        silu = gate_f * sig
        mix = mixed[b].astype(F32)
        unit = mix * silu * scale
        gated[b] = (unit * gain[0:1, :]).astype(BF16)
        back = scale * (d_gated[b] * gain[0:1, :] - unit * mean)
        dy[b] = (back * silu).astype(BF16)
        dgate[b] = (back * mix * sig * (1.0 + gate_f * (1.0 - sig))).astype(BF16)
        for index, (src, dst) in enumerate(late):
            save(src, dst, 4 + index, b).start()
        return carry

    lax.fori_loop(0, blocks, third, 0)
    for copy in copies:
        copy.wait_send()
    cot_comm.finish()
    out_comm.finish()
    wg_comm.finish()
    for keep in (keep_cot, keep_wg, keep_out):
        keep.wait()
    for index, (src, dst) in enumerate(early + late):
        for b in range(blocks):
            save(src, dst, index, b).wait()


def run_middle(dp, sp, seqs, wide, inner, w_zx, w_out, cotangent, hidden, wx, wb, norm, taps, heads, skip, gain):
    share = w_zx.shape[0]
    blocks, rows, width = hidden.shape
    chans, cols = wx.shape[1], wb.shape[1]
    states = wide // 2
    shapes = [
        (dp, sp, share, chans), (sp,) + w_out.shape, hidden.shape, hidden.shape,
        (blocks, rows, chans), (blocks, rows, cols), (blocks, states, chans),
        (blocks, rows, chans), (blocks, rows, chans), (blocks, rows, chans),
    ]
    block = lambda n, kind: pltpu.VMEM((blocks, rows, n), kind)
    vmem = pl.BlockSpec(memory_space=pltpu.VMEM)
    return pl.pallas_call(
        functools.partial(forward_kernel, dp, sp, seqs, wide, inner),
        in_specs=[ANY] * 6 + [vmem] * 5,
        out_specs=[ANY] * len(shapes),
        out_shape=[jax.ShapeDtypeStruct(shape, BF16) for shape in shapes],
        scratch_shapes=[
            pltpu.VMEM(hidden.shape, BF16),
            pltpu.VMEM(wx.shape, BF16),
            pltpu.VMEM(wb.shape, BF16),
            pltpu.VMEM(shapes[0], BF16),
            pltpu.VMEM(shapes[1], BF16),
            pltpu.VMEM(shapes[2], BF16),
            block(width, BF16), block(chans, BF16), block(cols, BF16), block(chans, BF16),
            pltpu.VMEM(shapes[6], BF16),
            block(chans, BF16), block(chans, F32), block(chans, BF16), block(chans, BF16),
            block(chans, BF16),
            pltpu.VMEM((rows + 8, chans + wide), F32),
            pltpu.VMEM((8, chans + wide), F32),
            pltpu.VMEM((states, chans), F32),
            pltpu.VMEM((rows, LANES), F32),
            pltpu.VMEM((sp // seqs, rows, LANES), F32),
            dma(8, max(blocks, 3)),
            dma(2, sp // seqs),
        ]
        + ColumnGather.scratch(dp, sp, seqs)
        + OutGather.scratch(dp, sp, seqs)
        + BlockGather.scratch(dp, sp, seqs),
        compiler_params=comm_params(2),
        name="forward",
    )(w_zx, w_out, cotangent, hidden, wx, wb, norm, taps, heads, skip, gain)


def backward_kernel(
    dp, sp, seqs, wide, chans,
    dy, x, x_before, bd, bd_before, dgate, enter, taps, heads, skip, wg, wx, wb,
    normed_ref, out_part, terms_out, terms_gate,
    out_total, dn_total, og, ox, ob, oo, osmall,
    ext, gext, halo, dstate, dtaps, dheads, dskip, dx, dbd, normed, part, loads,
    tx, tb, small, landed, *scratch,
):
    step, steps = pl.program_id(0), pl.num_programs(0)
    chunk = steps - 1 - step
    place = Place(dp, sp, seqs)
    chips = place.chips
    blocks, rows, width = part.shape
    rest = list(scratch)

    def take(n):
        taken = rest[:n]
        del rest[:n]
        return taken

    out_red = BlockReduce(place, out_part, *take(6))
    dn_red = BlockReduce(place, part, None, *take(5))
    gate_red = ShardReduce(place, terms_gate, og, *take(4))
    x_red = ShardReduce(place, tx, ox, *take(4))
    b_red = ShardReduce(place, tb, ob, *take(4))
    out_grads = OutReduce(place, terms_out, oo, *take(5))
    few = SmallReduce(place, small, landed, *take(3))
    load = pltpu.make_async_copy(normed_ref, normed, loads.at[0])

    @pl.when(step == 0)
    def _():
        place.meet(more=out_grads.ways.meet(False))
        for k in range(chips):
            out_red.start(k)
        gate_red.start()
        out_grads.start()
        load.start()

    scan_backward(
        wide, chans, dy, x, x_before, bd, bd_before, taps, heads, skip, enter,
        dx.at[chunk], dbd.at[chunk], dtaps, dheads, dskip, ext, gext, halo, dstate,
    )
    across = ((1,), (1,))
    total = dot(dgate[...], wg[...], across) + dot(dx[chunk], wx[...], across)
    part[chunk] = (total + dot(dbd[chunk], wb[...], across)).astype(BF16)

    def both_ways(i, fn):
        for k in (place.chip + i, place.chip - i):
            pl.when((k >= 0) & (k < chips))(functools.partial(fn, k))

    @pl.when(step == 0)
    def _():
        for i in range(chips - 1, 0, -1):
            both_ways(i, out_red.collect)
        out_red.collect(place.chip)

    for i in range(chips - 1, -1, -1):

        @pl.when(step == steps - 1 - max(i, 0) * (steps - 3) // chips)
        def _():
            if i:
                both_ways(i, out_red.settle)
            else:
                out_red.settle(place.chip)

    @pl.when(lax.rem(step, 2) == 1)
    def _():
        dn_red.start(chunk // 2)

    @pl.when((lax.rem(step, 2) == 0) & (step >= 2))
    def _():
        dn_red.collect(chunk // 2 + 1)

    wait = 6

    @pl.when((lax.rem(step, 2) == 0) & (step >= wait))
    def _():
        dn_red.settle(chunk // 2 + wait // 2)

    @pl.when(step == steps - 1)
    def _():
        dn_red.collect(jnp.int32(0))
        load.wait()
        share_rows = tx.shape[1] * tx.shape[2]
        rows_all = blocks * rows
        small[:, : chans + wide] = dtaps[...]
        small[5:6, :chans] = dskip[0:1, :]
        small[:, chans + wide :] = dheads[...]
        few.start()
        turned = dx[...].reshape(rows_all, -1)
        turned_b = dbd[...].reshape(rows_all, -1)
        for mask in list(range(1, dp)) + [0]:
            other = place.masked(mask)
            first = pl.multiple_of(other * share_rows, LANES)
            columns = normed[:, :, pl.ds(first, share_rows)].reshape(rows_all, share_rows)
            for red, values in ((x_red, turned), (b_red, turned_b)):
                value = dot(columns, values, ((0,), (0,))).astype(BF16)
                value = value.reshape(red.terms.shape[1:])
                if mask:
                    red.terms[other] = value
                    red.dp_copy(mask).start()
                else:
                    red.buf[0] = value
        gate_red.add()
        out_grads.add()
        for k in range(chips - 1 - (steps - 1 - wait) // 2 - 1, -1, -1):
            dn_red.settle(jnp.int32(k))
        few.add()
        x_red.add(kept=False)
        b_red.add(kept=False)
        out_red.finish()
        out_total[...] = out_red.total[...]
        dn_red.finish()
        dn_total[...] = dn_red.total[...]
        gate_red.finish()
        out_grads.finish()
        few.finish()
        osmall[...] = landed[...]
        x_red.finish()
        b_red.finish()


def run_backward(
    dp, sp, seqs, dy, x, bd, dgate, enter, taps, heads, skip, wg, wx, wb,
    normed, out_part, terms_out, terms_gate, wide,
):
    blocks, rows, chans = x.shape
    states = wide // 2
    cols, width = bd.shape[2], normed.shape[2]
    share = terms_gate.shape[2]
    back = lambda i: blocks - 1 - i
    block = lambda n: pl.BlockSpec((None, rows, n), lambda i: (back(i), 0, 0))
    whole = lambda a: pl.BlockSpec(a.shape, lambda i: (0,) * a.ndim)
    before = lambda n: pl.BlockSpec(
        (None, 16, n), lambda i: (jnp.maximum(back(i) - 1, 0), rows // 16 - 1, 0)
    )
    fixed = lambda *shape: pl.BlockSpec(shape, lambda i: (0,) * len(shape))
    tokens = (seqs, rows, width)
    small = (8, chans + wide + LANES)
    reduce = lambda n: ShardReduce.scratch(dp, sp, (share, n))
    return pl.pallas_call(
        functools.partial(backward_kernel, dp, sp, seqs, wide, chans),
        grid=(blocks,),
        in_specs=[
            block(chans), block(chans), before(chans), block(cols), before(cols), block(chans),
            pl.BlockSpec((None, states, chans), lambda i: (back(i), 0, 0)),
            whole(taps), whole(heads), whole(skip), whole(wg), whole(wx), whole(wb),
        ]
        + [ANY] * 4,
        out_specs=[fixed(*tokens), fixed(*tokens)] + [ANY] * 3
        + [ANY, fixed(sp, *small)],
        out_shape=[
            jax.ShapeDtypeStruct(tokens, BF16),
            jax.ShapeDtypeStruct(tokens, BF16),
            jax.ShapeDtypeStruct((sp, share, chans), BF16),
            jax.ShapeDtypeStruct((sp, share, chans), BF16),
            jax.ShapeDtypeStruct((sp, share, cols), BF16),
            jax.ShapeDtypeStruct((seqs,) + terms_out.shape[1:], BF16),
            jax.ShapeDtypeStruct((sp,) + small, F32),
        ],
        scratch_shapes=[
            pltpu.VMEM((rows + 8, chans + wide), F32),
            pltpu.VMEM((rows + 8, chans + wide), F32),
            pltpu.VMEM((8, chans + wide), F32),
            pltpu.VMEM((states, chans), F32),
            pltpu.VMEM((8, chans + wide), F32),
            pltpu.VMEM((8, LANES), F32),
            pltpu.VMEM((8, chans), F32),
            pltpu.VMEM((blocks, rows, chans), BF16),
            pltpu.VMEM((blocks, rows, cols), BF16),
            pltpu.VMEM(normed.shape, BF16),
            pltpu.VMEM((blocks, rows, width), BF16),
            dma(1),
            pltpu.VMEM((dp, sp, share, chans), BF16),
            pltpu.VMEM((dp, sp, share, cols), BF16),
            pltpu.VMEM(small, F32),
            pltpu.VMEM((sp,) + small, F32),
        ]
        + BlockReduce.scratch(dp, sp, seqs, rows, width, True)
        + BlockReduce.scratch(dp, sp, seqs, rows, width, False)
        + reduce(chans) + reduce(chans) + reduce(cols)
        + OutReduce.scratch(dp, sp, seqs, terms_out.shape[1:])
        + SmallReduce.scratch(dp, sp, seqs, small),
        compiler_params=comm_params(4),
        name="backward",
    )(
        dy, x, x, bd, bd, dgate, enter, taps, heads, skip, wg, wx, wb,
        normed, out_part, terms_out, terms_gate,
    )


def pad_last(value, size):
    return jnp.pad(value, [(0, 0)] * (value.ndim - 1) + [(0, size - value.shape[-1])])


def eight_rows(*rows):
    stacked = jnp.stack(rows, axis=0)
    return jnp.pad(stacked, ((0, 8 - stacked.shape[0]), (0, 0)))


def on_device(
    dp, sp,
    hidden_in, w_zx, w_bc, w_dt, norm_gain, conv_bc_weight, conv_bc_bias,
    conv_x_weight, conv_x_bias, dt_bias, a_log, d_skip, gate_gain, w_out, cotangent,
):
    me_dp, me_sp = lax.axis_index("dp"), lax.axis_index("sp")
    seqs, block, width = hidden_in.shape
    groups = sp // seqs
    group = lax.rem(me_sp, groups)
    rows = sp * block
    wide, heads = w_bc.shape[1], w_dt.shape[1]
    share, taps_n = w_zx.shape[0], conv_x_weight.shape[1]
    inner = heads * P_SIZE
    chans = inner // groups
    own_heads = heads // groups
    gate_share, bc_share = gate_gain.shape[0], conv_bc_bias.shape[0]
    x_share, head_share = conv_x_bias.shape[0], dt_bias.shape[0]
    cols = wide + LANES

    small = jnp.concatenate(
        [
            norm_gain,
            gate_gain,
            jnp.concatenate([conv_bc_weight, conv_bc_bias[:, None]], axis=1).reshape(-1),
            jnp.concatenate([conv_x_weight, conv_x_bias[:, None]], axis=1).reshape(-1),
            dt_bias,
            a_log,
            d_skip,
        ]
    )
    spare = cols - wide - heads
    high = -(-max(share, -(-small.shape[0] // spare)) // 16) * 16
    tall = lambda v: jnp.pad(v, ((0, high - share), (0, 0)))
    misc = jnp.concatenate(
        [tall(w_bc), tall(w_dt), pad_last(small, high * spare).reshape(high, spare)], axis=1
    )
    wx, misc_all, hidden_all = run_first(dp, sp, seqs, chans, w_zx, misc, hidden_in)
    misc_all = jnp.transpose(misc_all, (1, 2, 0, 3, 4)).reshape((dp, sp) + misc.shape)

    wx = wx.reshape(width, chans)
    bd_all = misc_all[:, :, :share, :].reshape(width, cols)
    dt_cols = lax.dynamic_slice_in_dim(bd_all[:, wide : wide + heads], group * own_heads, own_heads, axis=1)
    wb = jnp.concatenate([bd_all[:, :wide], pad_last(dt_cols, LANES)], axis=1)
    few = misc_all[:, :, :, wide + heads :].reshape(dp, sp, high * spare)
    ends = []
    for size in (share, gate_share, bc_share * (taps_n + 1), x_share * (taps_n + 1)) + (head_share,) * 3:
        ends.append(size + (ends[-1] if ends else 0))
    piece = lambda i: few[:, :, (ends[i - 1] if i else 0) : ends[i]]
    mine = lambda i: lax.dynamic_slice_in_dim(piece(i)[0], group * seqs, seqs, axis=0).astype(F32)
    norm_all = piece(0).reshape(width).astype(F32)
    gate_mine = lax.dynamic_slice_in_dim(
        piece(1).reshape(inner), group * chans, chans
    ).astype(F32)
    bc_all = piece(2).reshape(wide, taps_n + 1).astype(F32)
    x_all = mine(3).reshape(chans, taps_n + 1)
    taps = jnp.concatenate([x_all, bc_all], axis=0).T
    taps = jnp.pad(taps, ((0, 8 - taps.shape[0]), (0, 0)))
    head_rows = eight_rows(
        pad_last(mine(4).reshape(own_heads), LANES),
        pad_last(jnp.exp(mine(5).reshape(own_heads)), LANES),
    )
    skip = eight_rows(jnp.repeat(mine(6).reshape(own_heads), P_SIZE))
    gain = eight_rows(gate_mine)

    wg, out_mine, cot_all, normed, x_blocks, bd_blocks, entering, gated, dgate, dy = run_middle(
        dp, sp, seqs, wide, inner, w_zx, w_out, cotangent, hidden_all, wx, wb,
        eight_rows(norm_all), taps, head_rows, skip, gain,
    )
    normed, gated, cot_rows = (v.reshape(rows, -1) for v in (normed, gated, cot_all))
    out_rows = out_mine.reshape(chans, width)
    out_part = dot(gated, out_rows).astype(BF16).reshape(sp, block, width)
    terms_out = dot(gated, cot_rows, ((0,), (0,))).astype(BF16).reshape(sp, gate_share, width)
    terms_gate = dot(normed, dgate.reshape(rows, chans), ((0,), (0,))).astype(BF16)
    out_sum, d_normed, og, ox, ob, oo, osmall = run_backward(
        dp, sp, seqs, dy, x_blocks, bd_blocks, dgate, entering, taps, head_rows, skip,
        wg.reshape(width, chans), wx, wb, normed.reshape(sp, block, width), out_part, terms_out,
        terms_gate.reshape(dp, sp, share, chans), wide,
    )
    hidden_out = (hidden_in.astype(F32) + out_sum.astype(F32)).astype(BF16)
    spread_cols = lambda v: jnp.transpose(
        jnp.sum(v.astype(F32).reshape(seqs, groups, share, -1), axis=0), (1, 0, 2)
    ).reshape(share, -1)
    grad_w_zx = jnp.concatenate([spread_cols(og), spread_cols(ox)], axis=1)
    ob = ob.astype(F32)
    grad_w_bc = jnp.sum(ob[:, :, :wide], axis=0)
    grad_w_dt = spread_cols(ob[:, :, wide : wide + own_heads])
    grad_norm_gain = (
        jnp.sum(grad_w_zx * w_zx.astype(F32), axis=1)
        + jnp.sum(grad_w_bc * w_bc.astype(F32), axis=1)
        + jnp.sum(grad_w_dt * w_dt.astype(F32), axis=1)
    ) / norm_gain.astype(F32)
    grad_w_out = jnp.sum(oo.astype(F32), axis=0)
    grad_gate_gain = jnp.sum(grad_w_out * w_out.astype(F32), axis=1) / gate_gain.astype(F32)

    hid = hidden_in.reshape(seqs * block, width).astype(F32)
    scale_own = lax.rsqrt(jnp.mean(hid * hid, axis=-1, keepdims=True) + EPS)
    unit_own = hid * scale_own
    weighted = d_normed.reshape(seqs * block, width).astype(F32) * norm_all
    grad_rows = cotangent.reshape(seqs * block, width).astype(F32) + scale_own * (
        weighted - unit_own * jnp.mean(weighted * unit_own, axis=-1, keepdims=True)
    )
    grad_hidden = grad_rows.astype(BF16).reshape(hidden_in.shape)

    by_group = jnp.sum(osmall.reshape(seqs, groups, 8, -1), axis=0)
    from_group = lax.dynamic_index_in_dim(by_group, me_sp // seqs, axis=0, keepdims=False)
    part = lax.rem(me_sp, seqs)
    g_x = lax.dynamic_slice_in_dim(from_group[:, :chans], part * x_share, x_share, axis=1)
    g_heads = lax.dynamic_slice_in_dim(
        from_group[:, chans + wide :], part * head_share, head_share, axis=1
    )
    g_skip = jnp.sum(g_x[5].reshape(head_share, P_SIZE), axis=1)
    g_bc = jnp.sum(by_group[:, :, chans : chans + wide], axis=0)
    first = (me_dp * sp + me_sp) * bc_share
    g_bc = lax.dynamic_slice_in_dim(g_bc, first, bc_share, axis=1)
    return (
        hidden_out,
        grad_hidden,
        grad_w_zx,
        grad_w_bc,
        grad_w_dt,
        grad_norm_gain,
        g_bc[:taps_n].T,
        g_bc[taps_n],
        g_x[:taps_n].T,
        g_x[taps_n],
        g_heads[0],
        g_heads[1],
        g_skip,
        grad_gate_gain,
        grad_w_out,
    )


def solution(mesh):
    both = P(("dp", "sp"))
    rows = P(("dp", "sp"), None)
    tokens = P("dp", "sp", None)
    return jax.shard_map(
        functools.partial(on_device, mesh.shape["dp"], mesh.shape["sp"]),
        mesh=mesh,
        in_specs=(
            tokens, rows, rows, rows, both, rows, both, P("sp", None), P("sp"), P("sp"),
            P("sp"), P("sp"), both, rows, tokens,
        ),
        out_specs=(
            tokens, tokens, rows, rows, rows, both, rows, both, P("sp", None), P("sp"),
            P("sp"), P("sp"), P("sp"), both, rows,
        ),
        check_vma=False,
    )
```

```python
import functools

import jax
import jax.numpy as jnp
from jax import lax
from jax.experimental import pallas as pl
from jax.experimental.pallas import tpu as pltpu
from jax.sharding import PartitionSpec as P

P_SIZE = 64
EPS = 1e-05
F32 = jnp.float32
BF16 = jnp.bfloat16
HIGH = lax.Precision.HIGHEST
LANES = 128
VMEM_LIMIT = 58 * 1024 * 1024


def dot(left, right, dims=((1,), (0,)), precision=None):
    return lax.dot_general(
        left, right, (dims, ((), ())), precision=precision, preferred_element_type=F32
    )


def iota(shape, axis):
    return lax.broadcasted_iota(jnp.int32, shape, axis)


def spread(cols, pair, low_half):
    return jnp.where(low_half, cols[:, 2 * pair : 2 * pair + 1], cols[:, 2 * pair + 1 : 2 * pair + 2])


def spread_all(cols, pairs, low_half):
    return jnp.concatenate([spread(cols, pair, low_half) for pair in range(pairs)], axis=1)


def stack_heads(values, low_half):
    zero = jnp.zeros_like(values)
    return jnp.concatenate(
        [jnp.where(low_half, values, zero), jnp.where(low_half, zero, values)], axis=0
    )


def softplus(value):
    return jnp.maximum(value, 0.0) + jnp.log1p(jnp.exp(-jnp.abs(value)))


def conv_pre(ext, rows, taps):
    total = taps[4:5, :]
    for tap in range(4):
        total = total + taps[tap : tap + 1, :] * ext[pl.ds(5 + tap, rows), :]
    return total


def steps_of(dt_raw, head_ref):
    pre = dt_raw.astype(F32) + head_ref[0:1, :]
    steps = softplus(pre)
    return pre, steps, -steps * head_ref[1:2, :]


def scan_backward(
    wide, chans,
    dy_in, x, x_before, bd, bd_before, taps, heads, skip, enter,
    dx_out, dbd, dtaps, dheads, dskip,
    ext, gext, halo, dstate,
):
    step = pl.program_id(0)
    chunk = pl.num_programs(0) - 1 - step
    rows = x.shape[0]
    pairs = chans // LANES
    half = wide // 2
    low_half = iota((rows, LANES), 1) < P_SIZE

    @pl.when(step == 0)
    def _():
        halo[...] = jnp.zeros(halo.shape, F32)
        dstate[...] = jnp.zeros(dstate.shape, F32)
        dtaps[...] = jnp.zeros_like(dtaps)
        dheads[...] = jnp.zeros_like(dheads)
        dskip[...] = jnp.zeros_like(dskip)

    dy_half = dy_in[...]
    dy = dy_half.astype(F32)

    last_rows = x_before.shape[0] - 8
    past = jnp.concatenate(
        [x_before[last_rows:, :], bd_before[last_rows:, :wide]], axis=1
    ).astype(F32)
    ext[0:8, :] = jnp.where(chunk == 0, 0.0, past)
    ext[8 : 8 + rows, :chans] = x[...].astype(F32)
    ext[8 : 8 + rows, chans:] = bd[:, :wide].astype(F32)
    pre = conv_pre(ext, rows, taps)
    sig_pre = jax.nn.sigmoid(pre)
    act = (pre * sig_pre).astype(BF16)
    slope = sig_pre * (1.0 + pre * (1.0 - sig_pre))
    bmat = act[:, chans : chans + half]
    cmat = act[:, chans + half :]
    xmat = act[:, :chans]
    xval = xmat.astype(F32)
    dt_pre, steps, logs = steps_of(bd[:, wide:], heads)
    row, col = iota((rows, rows), 0), iota((rows, rows), 1)
    cumul = dot((row >= col).astype(F32), logs, precision=HIGH)
    cumul_t = cumul.T
    last = cumul[rows - 1 :, :]
    later = row <= col
    scores = dot(bmat, cmat, ((1,), (1,)))
    grown = jnp.exp(cumul)
    shrunk = jnp.exp(last - cumul)
    final = jnp.exp(last)
    entering = enter[...]
    dleave = dstate[...]
    dleave_half = dleave.astype(BF16)
    from_state = dot(bmat, dleave_half)
    across = dot(cmat, entering)
    grown_all = spread_all(grown, pairs, low_half)
    ending_all = spread_all(steps * shrunk, pairs, low_half)
    dy_grown = (dy * grown_all).astype(BF16)
    x_end = (xval * ending_all).astype(BF16)
    dstate[...] = dleave * spread_all(final, pairs, low_half[0:1, :]) + dot(
        cmat, dy_grown, ((0,), (0,))
    )
    owner = (iota((chans, LANES), 0) // P_SIZE == iota((chans, LANES), 1)).astype(F32)
    near = dot(xval * from_state, owner, precision=HIGH) * shrunk
    reach = dot(dy * across, owner, precision=HIGH) * grown
    kept = jnp.sum(entering.astype(F32) * dleave, axis=0, keepdims=True)
    kept = dot(jnp.broadcast_to(kept, (8, chans)), owner, precision=HIGH)[0:1, :] * final
    pairs_sum = jnp.zeros((rows, rows), F32)
    head_lane = iota((rows, LANES), 1)
    col_sum = jnp.zeros((rows, LANES), F32)
    row_sums = []
    for pair in range(pairs):
        lanes = slice(pair * LANES, (pair + 1) * LANES)
        products = dot(stack_heads(xmat[:, lanes], low_half), dy_half[:, lanes], ((1,), (1,)))
        weights = []
        for place, head in enumerate((2 * pair, 2 * pair + 1)):
            product = products[place * rows : (place + 1) * rows, :]
            differ = cumul_t[head : head + 1, :] - cumul[:, head : head + 1]
            decay = jnp.where(later, jnp.exp(jnp.minimum(differ, 0.0)), 0.0)
            weight = decay * scores
            step_col = steps[:, head : head + 1]
            weights.append(weight.astype(BF16))
            pairs_sum = pairs_sum + decay * product * step_col
            terms = weight * product
            col_sum = jnp.where(head_lane == head, jnp.sum(terms, axis=1, keepdims=True), col_sum)
            row_sums.append(jnp.sum(terms * step_col, axis=0, keepdims=True))
        inside = dot(
            jnp.concatenate(weights, axis=1), stack_heads(dy_half[:, lanes], low_half)
        )
        dx = spread(steps, pair, low_half) * (
            inside + spread(shrunk, pair, low_half) * from_state[:, lanes]
        )
        dx = dx + skip[0:1, lanes] * dy[:, lanes]
        gext[0:rows, lanes] = dx * slope[:, lanes]
    pairs_half = pairs_sum.astype(BF16)
    d_b = dot(pairs_half, cmat) + dot(x_end, dleave_half, ((1,), (1,)))
    d_c = dot(pairs_half, bmat, ((0,), (0,))) + dot(dy_grown, entering, ((1,), (1,)))
    gext[0:rows, chans : chans + half] = d_b * slope[:, chans : chans + half]
    gext[0:rows, chans + half :] = d_c * slope[:, chans + half :]

    row_sum = jnp.concatenate(
        row_sums + [jnp.zeros((LANES - 2 * pairs, rows), F32)], axis=0
    ).T
    d_logs = dot((row <= col).astype(F32), row_sum - steps * col_sum + reach, precision=HIGH)
    d_logs = d_logs + dot((row > col).astype(F32), steps * near, precision=HIGH) + kept
    d_steps = col_sum + near - heads[1:2, :] * d_logs
    d_pre = d_steps * jax.nn.sigmoid(dt_pre)
    dbd[:, wide:] = d_pre.astype(BF16)
    dheads[0:1, :] += jnp.sum(d_pre, axis=0, keepdims=True)
    dheads[1:2, :] += jnp.sum(d_logs * logs, axis=0, keepdims=True)
    dskip[0:1, :] += jnp.sum(dy * xval, axis=0, keepdims=True)

    gext[rows : rows + 8, :] = halo[...]
    g = gext[0:rows, :]
    halo[...] = g[0:8, :]
    d_in = jnp.zeros((rows, chans + wide), F32)
    for tap in range(4):
        d_in = d_in + taps[tap : tap + 1, :] * gext[pl.ds(3 - tap, rows), :]
        dtaps[tap : tap + 1, :] += jnp.sum(g * ext[pl.ds(5 + tap, rows), :], axis=0, keepdims=True)
    dtaps[4:5, :] += jnp.sum(g, axis=0, keepdims=True)
    dx_out[...] = d_in[:, :chans].astype(BF16)
    dbd[:, :wide] = d_in[:, chans:].astype(BF16)


MESH = pl.DeviceIdType.MESH
ANY = pl.BlockSpec(memory_space=pl.ANY)


class Place:
    def __init__(self, dp, sp, seqs):
        self.dp, self.sp, self.seqs = dp, sp, seqs
        self.groups = sp // seqs
        self.chips = sp // 2
        self.per = self.groups // 2
        self.p = lax.axis_index("dp")
        self.s = lax.axis_index("sp")
        self.chip = self.s // 2
        self.core = lax.rem(self.s, 2)
        self.seq = self.s // self.groups
        self.group = lax.rem(self.s, self.groups)
        self.low = self.seq * self.per
        self.high = self.low + self.per - 1
        self.bits = [1 << i for i in range(dp.bit_length() - 1)]

    def along_sp(self, other):
        return (self.p, other)

    def along_dp(self, other):
        return (other, self.s)

    def flip(self, bit):
        return self.p + bit - 2 * bit * lax.rem(self.p // bit, 2)

    def masked(self, mask):
        other = self.p
        for bit in self.bits:
            if mask & bit:
                other = other + bit - 2 * bit * lax.rem(self.p // bit, 2)
        return other

    def sp_peer(self, step):
        return lax.rem(self.s + step, self.sp)

    def meet(self, sp_peers=True, dp_peers=True, group_peers=False, more=0):
        barrier = pltpu.get_barrier_semaphore()
        peers = []
        if sp_peers:
            peers += [self.along_sp(self.sp_peer(i)) for i in range(1, self.sp)]
        if group_peers:
            peers += [self.along_sp(self.group_peer(i)) for i in range(1, self.groups)]
        if dp_peers:
            peers += [self.along_dp(self.masked(m)) for m in range(1, self.dp)]
        for peer in peers:
            pl.semaphore_signal(barrier, inc=1, device_id=peer, device_id_type=MESH)
        pl.semaphore_wait(barrier, len(peers) + more)

    def group_peer(self, step):
        return self.seq * self.groups + lax.rem(self.group + step, self.groups)


def remote(src, dst, send, recv, device):
    return pltpu.make_async_remote_copy(
        src_ref=src, dst_ref=dst, send_sem=send, recv_sem=recv, device_id=device,
        device_id_type=MESH,
    )


def dma(*shape):
    return pltpu.SemaphoreType.DMA(shape)


class DpTree:
    @staticmethod
    def scratch(dp):
        return [dma(2, dp), dma(2, dp, dp.bit_length() - 1)]

    def __init__(self, place, part, recv, send):
        self.at, self.part, self.recv, self.send = place, part, recv, send

    def children(self, odd, mask):
        at = self.at
        order = at.bits if odd == 0 else at.bits[::-1]
        last = max([order.index(b) for b in order if mask & b], default=-1)
        src = self.part(at.masked(mask), odd)
        return [
            remote(
                src, src, self.send.at[odd, mask, at.bits.index(bit)],
                self.recv.at[odd, mask ^ bit], at.along_dp(at.flip(bit)),
            )
            for bit in order[last + 1 :]
        ]

    def start(self, odd):
        for copy in self.children(odd, 0):
            copy.start()

    def arrived(self, odd, mask):
        at = self.at
        dst = self.part(at.masked(mask), odd)
        remote(dst, dst, self.send.at[odd, 0, 0], self.recv.at[odd, mask], at.along_dp(at.p)).wait_recv()

    def passed(self, odd, mask):
        order = self.at.bits if odd == 0 else self.at.bits[::-1]
        return not mask & order[-1]

    def forward(self):
        for mask in sorted(range(1, self.at.dp), key=lambda m: (bin(m).count("1"), m)):
            for odd in range(2):
                if self.passed(odd, mask):
                    self.arrived(odd, mask)
                    for copy in self.children(odd, mask):
                        copy.start()

    def complete(self):
        for mask in range(1, self.at.dp):
            for odd in range(2):
                if not self.passed(odd, mask):
                    self.arrived(odd, mask)

    def finish(self):
        for odd in range(2):
            for mask in range(self.at.dp):
                for copy in self.children(odd, mask):
                    copy.wait_send()


class Owners:
    def __init__(self, place):
        self.at, self.each = place, place.sp // place.dp

    def holder(self, seq):
        at = self.at
        p, s = lax.rem(at.s // self.each + at.p, at.dp), seq * at.groups + at.p
        return (p, s), (p == at.p) & (s == at.s)

    def first(self, p):
        at = self.at
        return lax.rem(p + at.dp - at.group, at.dp) * self.each

    def owner(self, i):
        at = self.at
        p, s = at.group, self.first(at.p) + i
        return (p, s), (p == at.p) & (s == at.s)

    def meet(self, spread):
        barrier = pltpu.get_barrier_semaphore()
        holders = [self.holder(seq) for seq in range(self.at.seqs)]
        owners = [self.owner(i) for i in range(self.each)]
        greet, wait = (owners, holders) if spread else (holders, owners)
        for device, mine in greet:

            @pl.when(jnp.logical_not(mine))
            def _():
                pl.semaphore_signal(barrier, inc=1, device_id=device, device_id_type=MESH)

        count = jnp.int32(0)
        for _, mine in wait:
            count = count + jnp.where(mine, 0, 1)
        return count


class OutGather:
    @staticmethod
    def scratch(dp, sp, seqs):
        return [dma(seqs), dma(sp), dma(1)] + DpTree.scratch(dp)

    def __init__(self, place, x, out, sent, got, local, *tree):
        self.at, self.x, self.out = place, x, out
        self.sent, self.got, self.local = sent, got, local.at[0]
        self.ways = Owners(place)
        each = self.ways.each
        size = each // 2
        part = lambda p, odd: out.at[pl.ds(self.ways.first(p) + odd * size, size)]
        self.tree = DpTree(place, part, *tree)

    def shard_copy(self, seq):
        at = self.at
        device, mine = self.ways.holder(seq)
        return jnp.logical_not(mine), remote(
            self.x, self.out.at[at.s], self.sent.at[seq], self.got.at[at.s], device
        )

    def keep(self):
        return pltpu.make_async_copy(self.x, self.out.at[self.at.s], self.local)

    def start(self):
        for seq in range(self.at.seqs):
            needed, copy = self.shard_copy(seq)
            pl.when(needed)(copy.start)
        for i in range(self.ways.each):
            pl.when(self.ways.owner(i)[1])(lambda: self.keep().start())

    def along_dp(self, odd):
        at, each = self.at, self.ways.each
        for i in range(odd * each // 2, (odd + 1) * each // 2):
            _, mine = self.ways.owner(i)
            slot = self.ways.first(at.p) + i
            pl.when(mine)(lambda: self.keep().wait())

            @pl.when(jnp.logical_not(mine))
            def _():
                dst = self.out.at[slot]
                remote(dst, dst, self.sent.at[0], self.got.at[slot], at.along_sp(at.s)).wait_recv()

        self.tree.start(odd)

    def forward(self):
        self.tree.forward()

    def complete(self):
        self.tree.complete()

    def finish(self):
        for seq in range(self.at.seqs):
            needed, copy = self.shard_copy(seq)
            pl.when(needed)(copy.wait_send)
        self.tree.finish()


class BlockReduce:
    @staticmethod
    def scratch(dp, sp, seqs, rows, cols, own):
        chips, sides = sp // 2, (2 if sp // seqs > 4 else 1)
        block = lambda *n: pltpu.VMEM(n + (rows, cols), BF16)
        return ([block(chips)] if own else []) + [
            block(chips), block(sides, chips), block(seqs), dma(7, chips), dma(2, seqs),
        ]

    def __init__(self, place, part, acc, cross, chain, total, sems, ends):
        self.at, self.part, self.acc = place, part, acc
        self.cross, self.chain, self.total = cross, chain, total
        (self.local, self.cross_send, self.cross_recv, self.chain_send, self.low_recv,
         self.high_recv, self.far_send) = (sems.at[i] for i in range(7))
        self.end_send, self.end_recv = ends.at[0], ends.at[1]

    def mine(self, k):
        return self.part.at[k * 2 + self.at.core] if self.acc is None else self.acc.at[k]

    def keep(self, k):
        return pltpu.make_async_copy(
            self.part.at[k * 2 + self.at.core], self.acc.at[k], self.local.at[k]
        )

    def crossing(self, k):
        at = self.at
        return remote(
            self.part.at[k * 2 + 1 - at.core], self.cross.at[k], self.cross_send.at[k],
            self.cross_recv.at[k], at.along_sp(at.chip * 2 + 1 - at.core),
        )

    def onward(self, k, up):
        at = self.at
        side = 0 if up else self.chain.shape[0] - 1
        return remote(
            self.mine(k), self.chain.at[side, k], self.chain_send.at[k],
            (self.low_recv if up else self.high_recv).at[k],
            at.along_sp((at.chip + (1 if up else -1)) * 2 + at.core),
        )

    def ending(self, k):
        at = self.at
        return remote(
            self.mine(k), self.total.at[at.seq], self.far_send.at[k], self.end_recv.at[at.seq],
            at.along_sp(k * 2 + at.core),
        )

    def exit_of(self, k):
        return jnp.clip(k, self.at.low, self.at.high)

    def add(self, k, other):
        mine = self.mine(k)
        mine[...] = (mine[...].astype(F32) + other[...].astype(F32)).astype(BF16)

    def start(self, k):
        self.crossing(k).start()
        if self.acc is not None:
            self.keep(k).start()

    def upstream(self, k, out):
        at = self.at

        @pl.when((at.chip <= out) & (at.chip > at.low))
        def _():
            self.onward(k, True).wait_recv()
            self.add(k, self.chain.at[0, k])

        @pl.when((at.chip >= out) & (at.chip < at.high))
        def _():
            self.onward(k, False).wait_recv()
            self.add(k, self.chain.at[self.chain.shape[0] - 1, k])

    def collect(self, k):
        at, out = self.at, self.exit_of(k)
        self.crossing(k).wait_recv()
        if self.acc is not None:
            self.keep(k).wait()
        self.add(k, self.cross.at[k])

        @pl.when(at.chip != out)
        def _():
            self.upstream(k, out)
            pl.when(at.chip < out)(lambda: self.onward(k, True).start())
            pl.when(at.chip > out)(lambda: self.onward(k, False).start())

    def settle(self, k):
        at, out = self.at, self.exit_of(k)

        @pl.when(at.chip == out)
        def _():
            self.upstream(k, out)

            @pl.when(k == at.chip)
            def _():
                self.total[at.seq] = self.mine(k)[...]

            @pl.when(k != at.chip)
            def _():
                self.ending(k).start()

    def finish(self):
        at = self.at
        for target in range(at.seqs):

            @pl.when(target != at.seq)
            def _():
                dst = self.total.at[target]
                remote(dst, dst, self.end_send.at[0], self.end_recv.at[target], at.along_sp(at.s)).wait_recv()

        for k in range(at.chips):
            out = self.exit_of(k)
            self.crossing(k).wait_send()
            pl.when(at.chip < out)(lambda: self.onward(k, True).wait_send())
            pl.when(at.chip > out)(lambda: self.onward(k, False).wait_send())
            pl.when((at.chip == out) & (at.chip != k))(lambda: self.ending(k).wait_send())


class TreeReduce:
    @staticmethod
    def scratch(dp, half, kept):
        own = [pltpu.VMEM((2, dp // 2) + half, BF16)] if kept else []
        return own + [pltpu.VMEM((2, dp - 1) + half, BF16), dma(3, 2, dp)]

    def __init__(self, place, source, kept, *scratch):
        self.at, self.source = place, source
        self.own = scratch[0] if kept else None
        self.recv, sems = scratch[-2:]
        self.send_sem, self.recv_sem, self.local = (sems.at[i] for i in range(3))
        self.steps = len(place.bits)

    def order(self, odd):
        return self.at.bits if odd == 0 else self.at.bits[::-1]

    def kept(self, odd):
        return [m for m in range(self.at.dp) if not m & self.order(odd)[0]]

    def block(self, odd, mask):
        if self.own is None:
            return self.source(self.at.masked(mask), odd)
        return self.own.at[odd, self.kept(odd).index(mask)]

    def sent(self, odd, i):
        order = self.order(odd)
        before = sum(order[:i])
        masks = [m for m in range(self.at.dp) if m & order[i] and not m & before]
        first = sum(self.at.dp >> (k + 1) for k in range(i))
        return [(first + n, m) for n, m in enumerate(masks)]

    def copy(self, odd, i, n, mask):
        at = self.at
        src = self.block(odd, mask) if i else self.source(at.masked(mask), odd)
        return remote(
            src, self.recv.at[odd, n], self.send_sem.at[odd, n], self.recv_sem.at[odd, n],
            at.along_dp(at.flip(self.order(odd)[i])),
        )

    def load(self, odd, mask):
        n = self.kept(odd).index(mask)
        return pltpu.make_async_copy(
            self.source(self.at.masked(mask), odd), self.own.at[odd, n], self.local.at[odd, n]
        )

    def start(self):
        for odd in range(2):
            for n, mask in self.sent(odd, 0):
                self.copy(odd, 0, n, mask).start()
            if self.own is not None:
                for mask in self.kept(odd):
                    self.load(odd, mask).start()

    def step(self, i):
        for odd in range(2):
            if i == 0 and self.own is not None:
                for mask in self.kept(odd):
                    self.load(odd, mask).wait()
            bit = self.order(odd)[i]
            for n, mask in self.sent(odd, i):
                self.copy(odd, i, n, mask).wait_recv()
                block = self.block(odd, mask ^ bit)
                block[...] = (block[...].astype(F32) + self.recv[odd, n].astype(F32)).astype(BF16)
            if i + 1 < self.steps:
                for n, mask in self.sent(odd, i + 1):
                    self.copy(odd, i + 1, n, mask).start()

    def total(self, odd):
        return self.block(odd, 0)

    def finish(self):
        for odd in range(2):
            for i in range(self.steps):
                for n, mask in self.sent(odd, i):
                    self.copy(odd, i, n, mask).wait_send()


class ShardReduce:
    @staticmethod
    def scratch(dp, sp, shape, kept):
        return [dma(2, sp), dma(1)] + TreeReduce.scratch(dp, (sp // 2,) + shape, kept)

    def __init__(self, place, terms, out, kept, sems, local, *tree):
        self.at, self.out, self.sems, self.local = place, out, sems, local.at[0]
        self.size = place.sp // 2
        source = lambda p, odd: terms.at[p, pl.ds(odd * self.size, self.size)]
        self.tree = TreeReduce(place, source, kept, *tree)

    def sp_copy(self, slot):
        at = self.at
        src = self.tree.total(slot // self.size).at[slot % self.size]
        return remote(
            src, self.out.at[at.s], self.sems.at[0, slot], self.sems.at[1, at.s], at.along_sp(slot)
        )

    def back(self, slot):
        src = self.tree.total(slot // self.size).at[slot % self.size]
        return pltpu.make_async_copy(src, self.out.at[slot], self.local)

    def spread(self):
        for slot in range(self.at.sp):
            pl.when(self.at.s == slot)(lambda: self.back(slot).start())
            pl.when(self.at.s != slot)(lambda: self.sp_copy(slot).start())

    def finish(self):
        at = self.at
        self.tree.finish()
        for slot in range(at.sp):

            @pl.when(at.s == slot)
            def _():
                self.back(slot).wait()

            @pl.when(at.s != slot)
            def _():
                dst = self.out.at[slot]
                remote(dst, dst, self.sems.at[0, 0], self.sems.at[1, slot], at.along_sp(at.s)).wait_recv()
                self.sp_copy(slot).wait_send()


class OutReduce:
    @staticmethod
    def scratch(dp, sp, seqs, shape):
        each = sp // dp
        return [dma(each), dma(seqs), dma(1)] + TreeReduce.scratch(dp, (each // 2,) + shape, True)

    def __init__(self, place, terms, out, sent, got, local, *tree):
        self.at, self.out = place, out
        self.sent, self.got, self.local = sent, got, local.at[0]
        self.ways = Owners(place)
        self.size = self.ways.each // 2
        source = lambda p, odd: terms.at[pl.ds(self.ways.first(p) + odd * self.size, self.size)]
        self.tree = TreeReduce(place, source, True, *tree)

    def shard_copy(self, i):
        at = self.at
        device, mine = self.ways.owner(i)
        src = self.tree.total(i // self.size).at[i % self.size]
        return mine, remote(src, self.out.at[at.seq], self.sent.at[i], self.got.at[at.seq], device)

    def back(self, i):
        src = self.tree.total(i // self.size).at[i % self.size]
        return pltpu.make_async_copy(src, self.out.at[self.at.seq], self.local)

    def spread(self):
        for i in range(self.ways.each):
            mine, copy = self.shard_copy(i)
            pl.when(jnp.logical_not(mine))(copy.start)
            pl.when(mine)(lambda: self.back(i).start())

    def finish(self):
        at = self.at
        self.tree.finish()
        for i in range(self.ways.each):
            mine, copy = self.shard_copy(i)
            pl.when(jnp.logical_not(mine))(copy.wait_send)
            pl.when(mine)(lambda: self.back(i).wait())
        for seq in range(at.seqs):
            _, mine = self.ways.holder(seq)

            @pl.when(jnp.logical_not(mine))
            def _():
                dst = self.out.at[seq]
                remote(dst, dst, self.sent.at[0], self.got.at[seq], at.along_sp(at.s)).wait_recv()


class SmallReduce:
    @staticmethod
    def scratch(dp, sp, seqs, own, common):
        return [
            pltpu.VMEM((dp,) + own, F32), pltpu.VMEM((dp,) + common, F32),
            pltpu.VMEM((seqs,) + own, F32), pltpu.VMEM((sp,) + common, F32),
            dma(4, dp), dma(2, sp), dma(2, seqs),
        ]

    def __init__(self, place, own, common, own_buf, common_buf, out_own, out_common, dp_sems, sp_sems, own_sems):
        self.at = place
        self.parts = ((own, own_buf), (common, common_buf))
        self.out_own, self.out_common = out_own, out_common
        self.dp_sems, self.sp_sems, self.own_sems = dp_sems, sp_sems, own_sems

    def dp_copy(self, which, mask):
        at = self.at
        x, buf = self.parts[which]
        return remote(
            x, buf.at[mask], self.dp_sems.at[2 * which, mask], self.dp_sems.at[2 * which + 1, mask],
            at.along_dp(at.masked(mask)),
        )

    def own_copy(self, i):
        at = self.at
        target = at.group * at.seqs + i
        return target == at.s, remote(
            self.parts[0][1].at[0], self.out_own.at[at.seq], self.own_sems.at[0, i],
            self.own_sems.at[1, at.seq], at.along_sp(target),
        )

    def common_copy(self, i):
        at = self.at
        return remote(
            self.parts[1][1].at[0], self.out_common.at[at.s], self.sp_sems.at[0, i],
            self.sp_sems.at[1, at.s], at.along_sp(at.sp_peer(i)),
        )

    def start(self):
        for which in range(2):
            for mask in range(1, self.at.dp):
                self.dp_copy(which, mask).start()

    def add(self):
        at = self.at
        for which in range(2):
            x, buf = self.parts[which]
            total = x[...]
            for mask in range(1, at.dp):
                self.dp_copy(which, mask).wait_recv()
                total = total + buf[mask]
            buf[0] = total
        for i in range(at.seqs):
            mine, copy = self.own_copy(i)
            pl.when(jnp.logical_not(mine))(copy.start)

            @pl.when(mine)
            def _():
                self.out_own[at.seq] = self.parts[0][1][0]

        self.out_common[at.s] = self.parts[1][1][0]
        for i in range(1, at.sp):
            self.common_copy(i).start()

    def finish(self):
        at = self.at
        for which in range(2):
            for mask in range(1, at.dp):
                self.dp_copy(which, mask).wait_send()
        for i in range(at.seqs):
            mine, copy = self.own_copy(i)
            pl.when(jnp.logical_not(mine))(copy.wait_send)
            sender = i * at.groups + at.s // at.seqs

            @pl.when(sender != at.s)
            def _():
                dst = self.out_own.at[i]
                remote(dst, dst, self.own_sems.at[0, 0], self.own_sems.at[1, i], at.along_sp(at.s)).wait_recv()

        for i in range(1, at.sp):
            slot = at.sp_peer(i)
            dst = self.out_common.at[slot]
            remote(dst, dst, self.sp_sems.at[0, 0], self.sp_sems.at[1, slot], at.along_sp(at.s)).wait_recv()
            self.common_copy(i).wait_send()


def comm_params(number):
    return pltpu.CompilerParams(
        collective_id=number, has_side_effects=True, vmem_limit_bytes=VMEM_LIMIT
    )


class BlockGather:
    @staticmethod
    def scratch(dp, sp, seqs):
        return [dma(5, sp // 2)]

    def __init__(self, place, x, out, sems):
        self.at, self.x, self.out = place, x, out
        self.send, self.recv, self.cross_send, self.cross_recv, self.local = (
            sems.at[i] for i in range(5)
        )

    def chip_at(self, i):
        return lax.rem(self.at.chip + i, self.at.chips)

    def chip_copy(self, i):
        at = self.at
        chip = self.chip_at(i)
        return remote(
            self.x.at[chip // at.per], self.out.at[at.s], self.send.at[i], self.recv.at[at.chip],
            at.along_sp(chip * 2 + at.core),
        )

    def keep(self):
        return pltpu.make_async_copy(self.x.at[self.at.seq], self.out.at[self.at.s], self.local.at[0])

    def crossing(self, k, src):
        at = self.at
        return remote(
            src, self.out.at[k * 2 + at.core], self.cross_send.at[k], self.cross_recv.at[k],
            at.along_sp(at.chip * 2 + 1 - at.core),
        )

    def start(self):
        for i in range(1, self.at.chips):
            self.chip_copy(i).start()
        self.crossing(self.at.chip, self.x.at[self.at.seq]).start()
        self.keep().start()

    def arrive(self, i):
        at = self.at
        k = self.chip_at(i)
        dst = self.out.at[k * 2 + at.core]

        @pl.when(i == 0)
        def _():
            self.keep().wait()

        @pl.when(i != 0)
        def _():
            remote(dst, dst, self.send.at[0], self.recv.at[k], at.along_sp(at.s)).wait_recv()
            self.crossing(k, dst).start()

        return k * 2 + at.core

    def arrive_other(self, i):
        at = self.at
        k = self.chip_at(i)
        dst = self.out.at[k * 2 + 1 - at.core]
        remote(dst, dst, self.cross_send.at[0], self.cross_recv.at[k], at.along_sp(at.s)).wait_recv()
        return k * 2 + 1 - at.core

    def finish(self):
        for i in range(1, self.at.chips):
            self.chip_copy(i).wait_send()
        for k in range(self.at.chips):
            self.crossing(k, self.out.at[k * 2 + self.at.core]).wait_send()


class ColumnGather:
    @staticmethod
    def scratch(dp, sp, seqs):
        return [dma(2, sp), dma(1)] + DpTree.scratch(dp)

    def __init__(self, place, piece, out, along, local, *tree):
        self.at, self.piece, self.out = place, piece, out
        self.along, self.local = along, local.at[0]
        size = place.sp // 2
        self.tree = DpTree(place, lambda p, odd: out.at[p, pl.ds(odd * size, size)], *tree)

    def sp_copy(self, i):
        at = self.at
        target = at.sp_peer(i)
        return remote(
            self.piece(lax.rem(target, at.groups)), self.out.at[at.p, at.s],
            self.along.at[0, i], self.along.at[1, at.s], at.along_sp(target),
        )

    def keep(self):
        at = self.at
        return pltpu.make_async_copy(self.piece(at.group), self.out.at[at.p, at.s], self.local)

    def start(self):
        for i in range(1, self.at.sp):
            self.sp_copy(i).start()
        self.keep().start()

    def along_dp(self, odd):
        at = self.at
        size = at.sp // 2
        for slot in range(odd * size, (odd + 1) * size):

            @pl.when(at.s == slot)
            def _():
                self.keep().wait()

            @pl.when(at.s != slot)
            def _():
                dst = self.out.at[at.p, slot]
                remote(dst, dst, self.along.at[0, 0], self.along.at[1, slot], at.along_sp(at.s)).wait_recv()

        self.tree.start(odd)

    def forward(self):
        self.tree.forward()

    def complete(self):
        self.tree.complete()

    def finish(self):
        for i in range(1, self.at.sp):
            self.sp_copy(i).wait_send()
        self.tree.finish()


class CommonGather:
    @staticmethod
    def scratch(dp, sp, seqs):
        return [dma(2, sp // 2), dma(2, dp), dma(3)]

    def __init__(self, place, x, out, along, across, ends):
        self.at, self.x, self.out = place, x, out
        self.along, self.across, self.ends = along, across, ends

    def chip_copy(self, i):
        at = self.at
        chip = lax.rem(at.chip + i, at.chips)
        return remote(
            self.x, self.out.at[at.core, at.p, at.chip], self.along.at[0, i],
            self.along.at[1, at.chip], at.along_sp(chip * 2 + at.core),
        )

    def keep(self):
        at = self.at
        return pltpu.make_async_copy(self.x, self.out.at[at.core, at.p, at.chip], self.ends.at[0])

    def dp_copy(self, mask):
        at = self.at
        src = self.out.at[at.core, at.p]
        return remote(
            src, src, self.across.at[0, mask], self.across.at[1, mask], at.along_dp(at.masked(mask))
        )

    def crossing(self):
        at = self.at
        src = self.out.at[at.core]
        return remote(
            src, src, self.ends.at[1], self.ends.at[2], at.along_sp(at.chip * 2 + 1 - at.core)
        )

    def start(self):
        for i in range(1, self.at.chips):
            self.chip_copy(i).start()
        self.keep().start()

    def along_dp(self):
        at = self.at
        self.keep().wait()
        for i in range(1, at.chips):
            k = lax.rem(at.chip + i, at.chips)
            dst = self.out.at[at.core, at.p, k]
            remote(dst, dst, self.along.at[0, 0], self.along.at[1, k], at.along_sp(at.s)).wait_recv()
        for mask in range(1, at.dp):
            self.dp_copy(mask).start()

    def cross(self):
        at = self.at
        for mask in range(1, at.dp):
            dst = self.out.at[at.core, at.masked(mask)]
            remote(dst, dst, self.across.at[0, 0], self.across.at[1, mask], at.along_dp(at.p)).wait_recv()
        self.crossing().start()

    def finish(self):
        at = self.at
        dst = self.out.at[1 - at.core]
        remote(dst, dst, self.ends.at[1], self.ends.at[2], at.along_sp(at.s)).wait_recv()
        self.crossing().wait_send()
        for mask in range(1, at.dp):
            self.dp_copy(mask).wait_send()
        for i in range(1, at.chips):
            self.chip_copy(i).wait_send()


def first_kernel(
    dp, sp, seqs, chans, w_ref, misc_ref, hid_ref, o_ref, wx_out, misc_out, hid_out, o_out, *sems
):
    place = Place(dp, sp, seqs)
    inner = w_ref.shape[1] // 2
    columns = lambda g: w_ref.at[:, pl.ds(pl.multiple_of(inner + g * chans, LANES), chans)]
    rest = list(sems)

    def take(scratch):
        taken = rest[: len(scratch)]
        del rest[: len(scratch)]
        return taken

    wx = ColumnGather(place, columns, wx_out, *take(ColumnGather.scratch(dp, sp, seqs)))
    misc = CommonGather(place, misc_ref, misc_out, *take(CommonGather.scratch(dp, sp, seqs)))
    hid = BlockGather(place, hid_ref, hid_out, *take(BlockGather.scratch(dp, sp, seqs)))
    out = OutGather(place, o_ref, o_out, *take(OutGather.scratch(dp, sp, seqs)))
    place.meet(more=out.ways.meet(True))
    misc.start()
    wx.start()
    out.start()
    hid.start()
    misc.along_dp()
    for odd in range(2):
        wx.along_dp(odd)
    for odd in range(2):
        out.along_dp(odd)
    misc.cross()
    hid.arrive(0)
    wx.forward()
    out.forward()
    for i in range(1, place.chips):
        hid.arrive(i)
    for i in range(place.chips):
        hid.arrive_other(i)
    wx.complete()
    out.complete()
    misc.finish()
    wx.finish()
    hid.finish()
    out.finish()


def run_first(dp, sp, seqs, chans, w_zx, misc, hidden, w_out):
    share = w_zx.shape[0]
    _, rows, cols = hidden.shape
    return pl.pallas_call(
        functools.partial(first_kernel, dp, sp, seqs, chans),
        in_specs=[ANY] * 4,
        out_specs=[ANY] * 4,
        out_shape=[
            jax.ShapeDtypeStruct((dp, sp, share, chans), BF16),
            jax.ShapeDtypeStruct((2, dp, sp // 2) + misc.shape, BF16),
            jax.ShapeDtypeStruct((sp, rows, cols), BF16),
            jax.ShapeDtypeStruct((sp,) + w_out.shape, BF16),
        ],
        scratch_shapes=ColumnGather.scratch(dp, sp, seqs)
        + CommonGather.scratch(dp, sp, seqs)
        + BlockGather.scratch(dp, sp, seqs)
        + OutGather.scratch(dp, sp, seqs),
        compiler_params=comm_params(1),
        name="first_gather",
    )(w_zx, misc, hidden, w_out)


def scan_block(wide, chans, x, bd, taps, heads, skip, mixed, enter, ext, halo, state):
    rows = x.shape[0]
    pairs = chans // LANES
    low_half = iota((rows, LANES), 1) < P_SIZE
    ext[0:8, :] = halo[...]
    ext[8 : 8 + rows, :chans] = x.astype(F32)
    ext[8 : 8 + rows, chans:] = bd[:, :wide].astype(F32)
    halo[...] = ext[rows : rows + 8, :]
    pre = conv_pre(ext, rows, taps)
    act = (pre * jax.nn.sigmoid(pre)).astype(BF16)
    half = wide // 2
    bmat = act[:, chans : chans + half]
    cmat = act[:, chans + half :]
    _, steps, logs = steps_of(bd[:, wide:], heads)
    earlier = iota((rows, rows), 0) >= iota((rows, rows), 1)
    cumul = dot(earlier.astype(F32), logs, precision=HIGH)
    cumul_t = cumul.T
    last = cumul[rows - 1 :, :]
    scores = dot(cmat, bmat, ((1,), (1,)))
    grown = jnp.exp(cumul)
    to_end = steps * jnp.exp(last - cumul)
    final = jnp.exp(last)
    entering = state[...]
    entering_half = entering.astype(BF16)
    enter[...] = entering_half
    across = dot(cmat, entering_half)
    for pair in range(pairs):
        lanes = slice(pair * LANES, (pair + 1) * LANES)
        weights = []
        for head in (2 * pair, 2 * pair + 1):
            differ = cumul[:, head : head + 1] - cumul_t[head : head + 1, :]
            decay = jnp.where(earlier, jnp.exp(jnp.minimum(differ, 0.0)), 0.0)
            weights.append((decay * scores).astype(BF16))
        values = act[:, lanes].astype(F32)
        scaled = (values * spread(steps, pair, low_half)).astype(BF16)
        total = dot(jnp.concatenate(weights, axis=1), stack_heads(scaled, low_half))
        total = total + spread(grown, pair, low_half) * across[:, lanes]
        total = total + skip[0:1, lanes] * values
        mixed[:, lanes] = total.astype(BF16)
        ending = (values * spread(to_end, pair, low_half)).astype(BF16)
        state[:, lanes] = entering[:, lanes] * spread(final, pair, low_half[0:1, :]) + dot(
            bmat, ending, ((0,), (0,))
        )


def forward_kernel(
    dp, sp, seqs, wide, inner,
    w_ref, cot_ref, hid_ref, wx_ref, wb_ref, o_ref, norm, taps, heads, skip, gain,
    wg_out, normed_out, x_out, bd_out, enter_out, dgate_out, dy_out, part_out, tg_out, to_out,
    hid, wx, wb, rows_out, wg, cot, normed, x, bd, mixed, enter, gate, d_gated, gated, dgate, dy,
    part, tg, to, ext, halo, state, sums, got, saves, sum_sems, *sems,
):
    place = Place(dp, sp, seqs)
    chans = wx.shape[1]
    blocks, rows, width = hid.shape
    columns = lambda g: w_ref.at[:, pl.ds(pl.multiple_of(g * chans, LANES), chans)]
    wg_comm = ColumnGather(place, columns, wg, *sems[:-1])
    cot_comm = BlockGather(place, cot_ref, cot, sems[-1])
    loads = [
        pltpu.make_async_copy(src, dst, saves.at[7, i])
        for i, (src, dst) in enumerate(
            ((hid_ref, hid), (wx_ref, wx), (wb_ref, wb), (o_ref, rows_out))
        )
    ]
    for load in loads:
        load.start()
    place.meet()
    wg_comm.start()
    cot_comm.start()
    halo[...] = jnp.zeros(halo.shape, F32)
    state[...] = jnp.zeros(state.shape, F32)
    sums[...] = jnp.zeros(sums.shape, F32)
    for load in loads[:3]:
        load.wait()

    def save(src, dst, index, b):
        return pltpu.make_async_copy(src.at[b], dst.at[b], saves.at[index, b])

    early = ((normed, normed_out), (x, x_out), (bd, bd_out), (enter, enter_out))
    late = ((dgate, dgate_out), (dy, dy_out), (part, part_out))

    def first(b, carry):
        @pl.when(b == blocks - 3)
        def _():
            for odd in range(2):
                wg_comm.along_dp(odd)

        hidden = hid[b].astype(F32)
        scale = lax.rsqrt(jnp.mean(hidden * hidden, axis=-1, keepdims=True) + EPS)
        normed[b] = (hidden * scale * norm[0:1, :]).astype(BF16)
        x[b] = dot(normed[b], wx[...]).astype(BF16)
        bd[b] = dot(normed[b], wb[...]).astype(BF16)
        scan_block(
            wide, chans, x[b], bd[b], taps, heads, skip, mixed.at[b], enter.at[b], ext, halo, state
        )
        for index, (src, dst) in enumerate(early):
            save(src, dst, index, b).start()
        return carry

    lax.fori_loop(0, blocks, first, 0)
    wg_comm.forward()
    wg_comm.complete()
    loads[3].wait()
    lane = iota((rows, LANES), 1)

    def gates(b):
        gate[b] = dot(normed[b], wg[...].reshape(width, chans)).astype(BF16)

    def second(b):
        d_gated[b] = dot(cot[b], rows_out[...].reshape(chans, width), ((1,), (1,)))
        gate_f = gate[b].astype(F32)
        value = mixed[b].astype(F32) * gate_f * jax.nn.sigmoid(gate_f)
        square = jnp.sum(value * value, axis=1, keepdims=True)
        cross = jnp.sum(value * d_gated[b] * gain[0:1, :], axis=1, keepdims=True)
        sums[...] = sums[...] + jnp.where(lane == 2 * b, square, 0.0) + jnp.where(
            lane == 2 * b + 1, cross, 0.0
        )

    def gates_loop(b, carry):
        gates(b)
        return carry

    lax.fori_loop(0, blocks, gates_loop, 0)

    def own_core(i, carry):
        second(cot_comm.arrive(i))
        return carry

    def other_core(i, carry):
        second(cot_comm.arrive_other(i))
        return carry

    lax.fori_loop(0, place.chips, own_core, 0)
    lax.fori_loop(0, place.chips, other_core, 0)

    copies = [
        remote(sums, got.at[i], sum_sems.at[0, i], sum_sems.at[1, i], place.along_sp(place.group_peer(i)))
        for i in range(1, place.groups)
    ]
    for copy in copies:
        copy.start()
    keep_wg = pltpu.make_async_copy(wg, wg_out, saves.at[7, 0])
    keep_wg.start()
    total = sums[...]
    for i, copy in enumerate(copies):
        copy.wait_recv()
        total = total + got[i + 1]
    got[0] = total

    def third(b, carry):
        total = got[0]
        square = jnp.sum(jnp.where(lane == 2 * b, total, 0.0), axis=1, keepdims=True)
        cross = jnp.sum(jnp.where(lane == 2 * b + 1, total, 0.0), axis=1, keepdims=True)
        scale = lax.rsqrt(square * (1.0 / inner) + EPS)
        mean = cross * scale * (1.0 / inner)
        gate_f = gate[b].astype(F32)
        sig = jax.nn.sigmoid(gate_f)
        silu = gate_f * sig
        mix = mixed[b].astype(F32)
        unit = mix * silu * scale
        gated[b] = (unit * gain[0:1, :]).astype(BF16)
        back = scale * (d_gated[b] * gain[0:1, :] - unit * mean)
        dy[b] = (back * silu).astype(BF16)
        dgate[b] = (back * mix * sig * (1.0 + gate_f * (1.0 - sig))).astype(BF16)
        part[b] = dot(gated[b], rows_out[...].reshape(chans, width)).astype(BF16)
        for index, (src, dst) in enumerate(late):
            save(src, dst, 4 + index, b).start()
        return carry

    lax.fori_loop(0, blocks, third, 0)
    everything = blocks * rows
    tile = width // dp
    keep_tg, keep_to = [], []
    for p in range(dp):
        columns = normed[:, :, p * tile : (p + 1) * tile].reshape(everything, tile)
        value = dot(columns, dgate[...].reshape(everything, chans), ((0,), (0,)))
        tg[p] = value.astype(BF16).reshape(tg.shape[1:])
        keep_tg.append(pltpu.make_async_copy(tg.at[p], tg_out.at[p], saves.at[7, 1 + p]))
        keep_tg[-1].start()
    slots = sp // 2
    for half in range(2):
        size = chans // 2
        columns = gated[:, :, half * size : (half + 1) * size].reshape(everything, size)
        value = dot(columns, cot[...].reshape(everything, width), ((0,), (0,)))
        span = pl.ds(half * slots, slots)
        to[span] = value.astype(BF16).reshape((slots,) + to.shape[1:])
        keep_to.append(
            pltpu.make_async_copy(to.at[span], to_out.at[span], saves.at[8, half])
        )
        keep_to[-1].start()
    for copy in copies:
        copy.wait_send()
    cot_comm.finish()
    wg_comm.finish()
    for keep in [keep_wg] + keep_tg + keep_to:
        keep.wait()
    for index, (src, dst) in enumerate(early + late):
        for b in range(blocks):
            save(src, dst, index, b).wait()


def run_middle(dp, sp, seqs, wide, inner, w_zx, cotangent, hidden, wx, wb, w_rows, norm, taps, heads, skip, gain):
    share = w_zx.shape[0]
    blocks, rows, width = hidden.shape
    chans, cols = wx.shape[1], wb.shape[1]
    states = wide // 2
    shapes = [
        (dp, sp, share, chans), hidden.shape, (blocks, rows, chans), (blocks, rows, cols),
        (blocks, states, chans), (blocks, rows, chans), (blocks, rows, chans), hidden.shape,
        (dp, sp, share, chans), w_rows.shape,
    ]
    block = lambda n, kind: pltpu.VMEM((blocks, rows, n), kind)
    vmem = pl.BlockSpec(memory_space=pltpu.VMEM)
    return pl.pallas_call(
        functools.partial(forward_kernel, dp, sp, seqs, wide, inner),
        in_specs=[ANY] * 6 + [vmem] * 5,
        out_specs=[ANY] * len(shapes),
        out_shape=[jax.ShapeDtypeStruct(shape, BF16) for shape in shapes],
        scratch_shapes=[
            pltpu.VMEM(hidden.shape, BF16),
            pltpu.VMEM(wx.shape, BF16),
            pltpu.VMEM(wb.shape, BF16),
            pltpu.VMEM(w_rows.shape, BF16),
            pltpu.VMEM(shapes[0], BF16),
            pltpu.VMEM(hidden.shape, BF16),
            block(width, BF16), block(chans, BF16), block(cols, BF16), block(chans, BF16),
            pltpu.VMEM(shapes[4], BF16),
            block(chans, BF16), block(chans, F32), block(chans, BF16), block(chans, BF16),
            block(chans, BF16), block(width, BF16),
            pltpu.VMEM(shapes[0], BF16),
            pltpu.VMEM(w_rows.shape, BF16),
            pltpu.VMEM((rows + 8, chans + wide), F32),
            pltpu.VMEM((8, chans + wide), F32),
            pltpu.VMEM((states, chans), F32),
            pltpu.VMEM((rows, LANES), F32),
            pltpu.VMEM((sp // seqs, rows, LANES), F32),
            dma(9, max(blocks, dp + 1, 4)),
            dma(2, sp // seqs),
        ]
        + ColumnGather.scratch(dp, sp, seqs)
        + BlockGather.scratch(dp, sp, seqs),
        compiler_params=comm_params(2),
        name="forward",
    )(w_zx, cotangent, hidden, wx, wb, w_rows, norm, taps, heads, skip, gain)


def backward_kernel(
    dp, sp, seqs, wide, chans,
    dy, x, x_before, bd, bd_before, dgate, enter, taps, heads, skip, norm, wg, wx, wb,
    normed_ref, out_part, terms_out, terms_gate, hid_ref, cot_ref, w_zx_ref, w_bc_ref, w_out_ref,
    hidden_out, grad_hidden, grad_zx, grad_bc, grad_dt, norm_sum, grad_out, gate_sum, own_small, common_small,
    ext, gext, halo, dstate, dtaps, dheads, dskip, dx, dbd, normed, part,
    hid, cot, w_zx, w_bc, w_out, loads, tb, og, ob, oo, own, *scratch,
):
    step, steps = pl.program_id(0), pl.num_programs(0)
    chunk = steps - 1 - step
    place = Place(dp, sp, seqs)
    chips = place.chips
    blocks, rows, width = part.shape
    rest = list(scratch)

    def take(n):
        taken = rest[:n]
        del rest[:n]
        return taken

    out_red = BlockReduce(place, out_part, *take(6))
    dn_red = BlockReduce(place, part, None, *take(5))
    gate_red = ShardReduce(place, terms_gate, og, True, *take(5))
    b_red = ShardReduce(place, tb, ob, False, *take(4))
    out_grads = OutReduce(place, terms_out, oo, *take(6))
    few = SmallReduce(place, own, dtaps.at[:, pl.ds(chans, wide)], *take(7))
    x_reds, x_parts = [], []
    while rest:
        tx, landed = take(2)
        x_reds.append((tx, ShardReduce(place, tx, landed, False, *take(4))))
        x_parts.append(landed)
    last_loads = [
        pltpu.make_async_copy(src, dst, loads.at[i])
        for i, (src, dst) in enumerate(
            (
                (normed_ref, normed), (hid_ref, hid), (cot_ref, cot), (w_zx_ref, w_zx),
                (w_bc_ref, w_bc), (w_out_ref, w_out),
            )
        )
    ]

    @pl.when(step == 0)
    def _():
        place.meet(more=out_grads.ways.meet(False))
        for k in range(chips):
            out_red.start(k)
        gate_red.tree.start()
        for load in last_loads:
            load.start()

    scan_backward(
        wide, chans, dy, x, x_before, bd, bd_before, taps, heads, skip, enter,
        dx.at[chunk], dbd.at[chunk], dtaps, dheads, dskip, ext, gext, halo, dstate,
    )
    across = ((1,), (1,))
    total = dot(dgate[...], wg[...], across) + dot(dx[chunk], wx[...], across)
    part[chunk] = (total + dot(dbd[chunk], wb[...], across)).astype(BF16)

    def both_ways(i, fn):
        for k in (place.chip + i, place.chip - i):
            pl.when((k >= 0) & (k < chips))(functools.partial(fn, k))

    @pl.when(step == 0)
    def _():
        for i in range(chips - 1, 0, -1):
            both_ways(i, out_red.collect)
        out_red.collect(place.chip)

    for i in range(chips - 1, -1, -1):

        @pl.when(step == steps - 1 - i * (steps - 3) // chips)
        def _():
            if i:
                both_ways(i, out_red.settle)
            else:
                out_red.settle(place.chip)

    levels = len(place.bits)

    def at_step(when, fn):
        pl.when(step == min(when, steps - 1))(fn)

    at_step(1, out_grads.tree.start)
    for i in range(levels):
        at_step(3 + 2 * i, functools.partial(gate_red.tree.step, i))
        at_step(5 + i, functools.partial(out_grads.tree.step, i))
    at_step(1 + 2 * levels, gate_red.spread)
    at_step(4 + levels, out_grads.spread)

    @pl.when(lax.rem(step, 2) == 1)
    def _():
        dn_red.start(chunk // 2)

    @pl.when((lax.rem(step, 2) == 0) & (step >= 2))
    def _():
        dn_red.collect(chunk // 2 + 1)

    wait = 6

    @pl.when((lax.rem(step, 2) == 0) & (step >= wait))
    def _():
        dn_red.settle(chunk // 2 + wait // 2)

    @pl.when(step == steps - 1)
    def _():
        for load in last_loads:
            load.wait()
        rows_all = blocks * rows
        share_rows = tb.shape[1] * tb.shape[2]
        size = chans // len(x_reds)
        own[:, :chans] = dtaps[:, :chans]
        own[5:6, :chans] = dskip[0:1, :]
        own[:, chans:] = dheads[...]
        few.start()

        def terms(red, out, values):
            for p in range(dp):
                columns = normed[:, :, p * share_rows : (p + 1) * share_rows]
                value = dot(columns.reshape(rows_all, share_rows), values, ((0,), (0,)))
                out[p] = value.astype(BF16).reshape(out.shape[1:])
            red.tree.start()

        for n, (tx, red) in enumerate(x_reds):
            terms(red, tx, dx[:, :, n * size : (n + 1) * size].reshape(rows_all, size))
        dn_red.collect(jnp.int32(0))
        terms(b_red, tb, dbd[...].reshape(rows_all, -1))
        for k in range(chips - 1 - (steps - 1 - wait) // 2 - 1, 0, -1):
            dn_red.settle(jnp.int32(k))
        few.add()
        late = [red for _, red in x_reds] + [b_red]
        for i in range(levels):
            for red in late:
                red.tree.step(i)
                if i == levels - 1:
                    red.spread()
            if i == 0:
                dn_red.settle(jnp.int32(0))
        out_red.finish()
        hidden_out[...] = (hid[...].astype(F32) + out_red.total[...].astype(F32)).astype(BF16)
        out_grads.finish()
        value = oo[0].astype(F32)
        for seq in range(1, seqs):
            value = value + oo[seq].astype(F32)
        grad_out[...] = value
        gate_sum[...] = jnp.broadcast_to(
            jnp.sum(value * w_out[...].astype(F32), axis=1, keepdims=True), gate_sum.shape
        )
        gate_red.finish()
        by_seq = lambda ref, g: functools.reduce(
            jnp.add, [ref[seq * place.groups + g].astype(F32) for seq in range(seqs)]
        )
        inner = grad_zx.shape[1] // 2
        norm_total = jnp.zeros((grad_zx.shape[0], 1), F32)

        def write(first, value):
            lanes = slice(first, first + value.shape[1])
            grad_zx[:, lanes] = value
            return jnp.sum(value * w_zx[:, lanes].astype(F32), axis=1, keepdims=True)

        for g in range(place.groups):
            norm_total = norm_total + write(g * chans, by_seq(og, g))
        dn_red.finish()
        for seq in range(seqs):
            value = hid[seq].astype(F32)
            scale = lax.rsqrt(jnp.mean(value * value, axis=-1, keepdims=True) + EPS)
            unit = value * scale
            weighted = dn_red.total[seq].astype(F32) * norm[0:1, :]
            weighted = weighted - unit * jnp.mean(weighted * unit, axis=-1, keepdims=True)
            grad_hidden[seq] = (cot[seq].astype(F32) + scale * weighted).astype(BF16)
        few.finish()
        own_small[...] = functools.reduce(jnp.add, [few.out_own[seq] for seq in range(seqs)])
        common_small[...] = functools.reduce(jnp.add, [few.out_common[slot] for slot in range(sp)])
        for n, landed in enumerate(x_parts):
            x_reds[n][1].finish()
            for g in range(place.groups):
                norm_total = norm_total + write(inner + g * chans + n * size, by_seq(landed, g))
        b_red.finish()
        value = functools.reduce(jnp.add, [ob[slot, :, :wide].astype(F32) for slot in range(sp)])
        grad_bc[...] = value
        norm_total = norm_total + jnp.sum(value * w_bc[...].astype(F32), axis=1, keepdims=True)
        norm_sum[...] = jnp.broadcast_to(norm_total, norm_sum.shape)
        for g in range(place.groups):
            grad_dt[g] = functools.reduce(
                jnp.add,
                [ob[seq * place.groups + g, :, wide:].astype(F32) for seq in range(seqs)],
            )


def run_backward(
    dp, sp, seqs, dy, x, bd, dgate, enter, taps, heads, skip, norm, wg, wx, wb,
    normed, out_part, terms_out, terms_gate, hidden, cotangent, w_zx, w_bc, w_out, wide,
):
    blocks, rows, chans = x.shape
    states = wide // 2
    cols, width = bd.shape[2], normed.shape[2]
    share = terms_gate.shape[2]
    groups = sp // seqs
    pieces = 2 if chans % (2 * LANES) == 0 else 1
    back = lambda i: blocks - 1 - i
    block = lambda n: pl.BlockSpec((None, rows, n), lambda i: (back(i), 0, 0))
    whole = lambda a: pl.BlockSpec(a.shape, lambda i: (0,) * a.ndim)
    before = lambda n: pl.BlockSpec(
        (None, 16, n), lambda i: (jnp.maximum(back(i) - 1, 0), rows // 16 - 1, 0)
    )
    outs = [
        jax.ShapeDtypeStruct(hidden.shape, BF16),
        jax.ShapeDtypeStruct(hidden.shape, BF16),
        jax.ShapeDtypeStruct(w_zx.shape, F32),
        jax.ShapeDtypeStruct(w_bc.shape, F32),
        jax.ShapeDtypeStruct((groups, share, LANES), F32),
        jax.ShapeDtypeStruct((share, LANES), F32),
        jax.ShapeDtypeStruct(w_out.shape, F32),
        jax.ShapeDtypeStruct((w_out.shape[0], LANES), F32),
        jax.ShapeDtypeStruct((8, chans + LANES), F32),
        jax.ShapeDtypeStruct((8, wide), F32),
    ]
    vmem = lambda a: pltpu.VMEM(a.shape, a.dtype)
    scratch = [
        pltpu.VMEM((rows + 8, chans + wide), F32),
        pltpu.VMEM((rows + 8, chans + wide), F32),
        pltpu.VMEM((8, chans + wide), F32),
        pltpu.VMEM((states, chans), F32),
        pltpu.VMEM((8, chans + wide), F32),
        pltpu.VMEM((8, LANES), F32),
        pltpu.VMEM((8, chans), F32),
        pltpu.VMEM((blocks, rows, chans), BF16),
        pltpu.VMEM((blocks, rows, cols), BF16),
        vmem(normed),
        pltpu.VMEM((blocks, rows, width), BF16),
        vmem(hidden), vmem(cotangent), vmem(w_zx), vmem(w_bc), vmem(w_out),
        dma(6),
        pltpu.VMEM((dp, sp, share, cols), BF16),
        pltpu.VMEM((sp, share, chans), BF16),
        pltpu.VMEM((sp, share, cols), BF16),
        pltpu.VMEM((seqs,) + w_out.shape, BF16),
        pltpu.VMEM((8, chans + LANES), F32),
    ]
    scratch += BlockReduce.scratch(dp, sp, seqs, rows, width, True)
    scratch += BlockReduce.scratch(dp, sp, seqs, rows, width, False)
    scratch += ShardReduce.scratch(dp, sp, (share, chans), True)
    scratch += ShardReduce.scratch(dp, sp, (share, cols), False)
    scratch += OutReduce.scratch(dp, sp, seqs, w_out.shape)
    scratch += SmallReduce.scratch(dp, sp, seqs, (8, chans + LANES), (8, wide))
    for _ in range(pieces):
        shape = (share, chans // pieces)
        scratch += [pltpu.VMEM((dp, sp) + shape, BF16), pltpu.VMEM((sp,) + shape, BF16)]
        scratch += ShardReduce.scratch(dp, sp, shape, False)
    return pl.pallas_call(
        functools.partial(backward_kernel, dp, sp, seqs, wide, chans),
        grid=(blocks,),
        in_specs=[
            block(chans), block(chans), before(chans), block(cols), before(cols), block(chans),
            pl.BlockSpec((None, states, chans), lambda i: (back(i), 0, 0)),
            whole(taps), whole(heads), whole(skip), whole(norm), whole(wg), whole(wx), whole(wb),
        ]
        + [ANY] * 9,
        out_specs=[whole(out) for out in outs],
        out_shape=outs,
        scratch_shapes=scratch,
        compiler_params=comm_params(4),
        name="backward",
    )(
        dy, x, x, bd, bd, dgate, enter, taps, heads, skip, norm, wg, wx, wb,
        normed, out_part, terms_out, terms_gate, hidden, cotangent, w_zx, w_bc, w_out,
    )


def pad_last(value, size):
    return jnp.pad(value, [(0, 0)] * (value.ndim - 1) + [(0, size - value.shape[-1])])


def eight_rows(*rows):
    stacked = jnp.stack(rows, axis=0)
    return jnp.pad(stacked, ((0, 8 - stacked.shape[0]), (0, 0)))


def on_device(
    dp, sp,
    hidden_in, w_zx, w_bc, w_dt, norm_gain, conv_bc_weight, conv_bc_bias,
    conv_x_weight, conv_x_bias, dt_bias, a_log, d_skip, gate_gain, w_out, cotangent,
):
    me_dp, me_sp = lax.axis_index("dp"), lax.axis_index("sp")
    seqs, block, width = hidden_in.shape
    groups = sp // seqs
    group = lax.rem(me_sp, groups)
    wide, heads = w_bc.shape[1], w_dt.shape[1]
    share, taps_n = w_zx.shape[0], conv_x_weight.shape[1]
    inner = heads * P_SIZE
    chans = inner // groups
    own_heads = heads // groups
    gate_share, bc_share = gate_gain.shape[0], conv_bc_bias.shape[0]
    x_share, head_share = conv_x_bias.shape[0], dt_bias.shape[0]
    cols = wide + LANES

    small = jnp.concatenate(
        [
            norm_gain,
            gate_gain,
            jnp.concatenate([conv_bc_weight, conv_bc_bias[:, None]], axis=1).reshape(-1),
            jnp.concatenate([conv_x_weight, conv_x_bias[:, None]], axis=1).reshape(-1),
            dt_bias,
            a_log,
            d_skip,
        ]
    )
    spare = cols - wide - heads
    high = -(-max(share, -(-small.shape[0] // spare)) // 16) * 16
    tall = lambda v: jnp.pad(v, ((0, high - share), (0, 0)))
    misc = jnp.concatenate(
        [tall(w_bc), tall(w_dt), pad_last(small, high * spare).reshape(high, spare)], axis=1
    )
    wx, misc_all, hidden_all, w_rows = run_first(dp, sp, seqs, chans, w_zx, misc, hidden_in, w_out)
    misc_all = jnp.transpose(misc_all, (1, 2, 0, 3, 4)).reshape((dp, sp) + misc.shape)

    wx = wx.reshape(width, chans)
    bd_all = misc_all[:, :, :share, :].reshape(width, cols)
    dt_cols = lax.dynamic_slice_in_dim(bd_all[:, wide : wide + heads], group * own_heads, own_heads, axis=1)
    wb = jnp.concatenate([bd_all[:, :wide], pad_last(dt_cols, LANES)], axis=1)
    few = misc_all[:, :, :, wide + heads :].reshape(dp, sp, high * spare)
    ends = []
    for size in (share, gate_share, bc_share * (taps_n + 1), x_share * (taps_n + 1)) + (head_share,) * 3:
        ends.append(size + (ends[-1] if ends else 0))
    piece = lambda i: few[:, :, (ends[i - 1] if i else 0) : ends[i]]
    mine = lambda i: lax.dynamic_slice_in_dim(piece(i)[0], group * seqs, seqs, axis=0).astype(F32)
    norm_all = piece(0).reshape(width).astype(F32)
    gate_mine = lax.dynamic_slice_in_dim(
        piece(1).reshape(inner), group * chans, chans
    ).astype(F32)
    bc_all = piece(2).reshape(wide, taps_n + 1).astype(F32)
    x_all = mine(3).reshape(chans, taps_n + 1)
    taps = jnp.concatenate([x_all, bc_all], axis=0).T
    taps = jnp.pad(taps, ((0, 8 - taps.shape[0]), (0, 0)))
    head_rows = eight_rows(
        pad_last(mine(4).reshape(own_heads), LANES),
        pad_last(jnp.exp(mine(5).reshape(own_heads)), LANES),
    )
    skip = eight_rows(jnp.repeat(mine(6).reshape(own_heads), P_SIZE))
    gain = eight_rows(gate_mine)

    norm = eight_rows(norm_all)
    wg, normed, x_blocks, bd_blocks, entering, dgate, dy, out_part, terms_gate, terms_out = run_middle(
        dp, sp, seqs, wide, inner, w_zx, cotangent, hidden_all, wx, wb, w_rows,
        norm, taps, head_rows, skip, gain,
    )
    (hidden_out, grad_hidden, grad_w_zx, grad_w_bc, dt_parts, norm_sum, grad_w_out, gate_sum,
     own_small, common_small) = run_backward(
        dp, sp, seqs, dy, x_blocks, bd_blocks, dgate, entering, taps, head_rows, skip, norm,
        wg.reshape(width, chans), wx, wb, normed, out_part, terms_out, terms_gate,
        hidden_in, cotangent, w_zx, w_bc, w_out, wide,
    )
    grad_w_dt = jnp.transpose(dt_parts[:, :, :own_heads], (1, 0, 2)).reshape(share, heads)
    grad_norm_gain = (
        norm_sum[:, 0] + jnp.sum(grad_w_dt * w_dt.astype(F32), axis=1)
    ) / norm_gain.astype(F32)
    grad_gate_gain = gate_sum[:, 0] / gate_gain.astype(F32)

    part = lax.rem(me_sp, seqs)
    g_x = lax.dynamic_slice_in_dim(own_small[:, :chans], part * x_share, x_share, axis=1)
    g_heads = lax.dynamic_slice_in_dim(own_small[:, chans:], part * head_share, head_share, axis=1)
    g_skip = jnp.sum(g_x[5].reshape(head_share, P_SIZE), axis=1)
    first = (me_dp * sp + me_sp) * bc_share
    g_bc = lax.dynamic_slice_in_dim(common_small, first, bc_share, axis=1)
    return (
        hidden_out,
        grad_hidden,
        grad_w_zx,
        grad_w_bc,
        grad_w_dt,
        grad_norm_gain,
        g_bc[:taps_n].T,
        g_bc[taps_n],
        g_x[:taps_n].T,
        g_x[taps_n],
        g_heads[0],
        g_heads[1],
        g_skip,
        grad_gate_gain,
        grad_w_out,
    )


def solution(mesh):
    both = P(("dp", "sp"))
    rows = P(("dp", "sp"), None)
    tokens = P("dp", "sp", None)
    return jax.shard_map(
        functools.partial(on_device, mesh.shape["dp"], mesh.shape["sp"]),
        mesh=mesh,
        in_specs=(
            tokens, rows, rows, rows, both, rows, both, P("sp", None), P("sp"), P("sp"),
            P("sp"), P("sp"), both, rows, tokens,
        ),
        out_specs=(
            tokens, tokens, rows, rows, rows, both, rows, both, P("sp", None), P("sp"),
            P("sp"), P("sp"), P("sp"), both, rows,
        ),
        check_vma=False,
    )
```

```python
import functools

import jax
import jax.numpy as jnp
from jax import lax
from jax.experimental import pallas as pl
from jax.experimental.pallas import tpu as pltpu
from jax.sharding import PartitionSpec as P

P_SIZE = 64
EPS = 1e-05
F32 = jnp.float32
BF16 = jnp.bfloat16
HIGH = lax.Precision.HIGHEST
LANES = 128
VMEM_LIMIT = 58 * 1024 * 1024


def dot(left, right, dims=((1,), (0,)), precision=None):
    return lax.dot_general(
        left, right, (dims, ((), ())), precision=precision, preferred_element_type=F32
    )


def iota(shape, axis):
    return lax.broadcasted_iota(jnp.int32, shape, axis)


def spread(cols, pair, low_half):
    return jnp.where(low_half, cols[:, 2 * pair : 2 * pair + 1], cols[:, 2 * pair + 1 : 2 * pair + 2])


def spread_all(cols, pairs, low_half):
    return jnp.concatenate([spread(cols, pair, low_half) for pair in range(pairs)], axis=1)


def stack_heads(values, low_half):
    zero = jnp.zeros_like(values)
    return jnp.concatenate(
        [jnp.where(low_half, values, zero), jnp.where(low_half, zero, values)], axis=0
    )


def softplus(value):
    return jnp.maximum(value, 0.0) + jnp.log1p(jnp.exp(-jnp.abs(value)))


def conv_pre(ext, rows, taps):
    total = taps[4:5, :]
    for tap in range(4):
        total = total + taps[tap : tap + 1, :] * ext[pl.ds(5 + tap, rows), :]
    return total


def steps_of(dt_raw, head_ref):
    pre = dt_raw.astype(F32) + head_ref[0:1, :]
    steps = softplus(pre)
    return pre, steps, -steps * head_ref[1:2, :]


def scan_backward(
    wide, chans,
    dy_in, x, x_before, bd, bd_before, taps, heads, skip, enter,
    dx_out, dbd, dtaps, dheads, dskip,
    ext, gext, halo, dstate,
):
    step = pl.program_id(0)
    chunk = pl.num_programs(0) - 1 - step
    rows = x.shape[0]
    pairs = chans // LANES
    half = wide // 2
    low_half = iota((rows, LANES), 1) < P_SIZE

    @pl.when(step == 0)
    def _():
        halo[...] = jnp.zeros(halo.shape, F32)
        dstate[...] = jnp.zeros(dstate.shape, F32)
        dtaps[...] = jnp.zeros_like(dtaps)
        dheads[...] = jnp.zeros_like(dheads)
        dskip[...] = jnp.zeros_like(dskip)

    dy_half = dy_in[...]
    dy = dy_half.astype(F32)

    last_rows = x_before.shape[0] - 8
    past = jnp.concatenate(
        [x_before[last_rows:, :], bd_before[last_rows:, :wide]], axis=1
    ).astype(F32)
    ext[0:8, :] = jnp.where(chunk == 0, 0.0, past)
    ext[8 : 8 + rows, :chans] = x[...].astype(F32)
    ext[8 : 8 + rows, chans:] = bd[:, :wide].astype(F32)
    pre = conv_pre(ext, rows, taps)
    sig_pre = jax.nn.sigmoid(pre)
    act = (pre * sig_pre).astype(BF16)
    slope = sig_pre * (1.0 + pre * (1.0 - sig_pre))
    bmat = act[:, chans : chans + half]
    cmat = act[:, chans + half :]
    xmat = act[:, :chans]
    xval = xmat.astype(F32)
    dt_pre, steps, logs = steps_of(bd[:, wide:], heads)
    row, col = iota((rows, rows), 0), iota((rows, rows), 1)
    cumul = dot((row >= col).astype(F32), logs, precision=HIGH)
    cumul_t = cumul.T
    last = cumul[rows - 1 :, :]
    later = row <= col
    scores = dot(bmat, cmat, ((1,), (1,)))
    grown = jnp.exp(cumul)
    shrunk = jnp.exp(last - cumul)
    final = jnp.exp(last)
    entering = enter[...]
    dleave = dstate[...]
    dleave_half = dleave.astype(BF16)
    from_state = dot(bmat, dleave_half)
    across = dot(cmat, entering)
    grown_all = spread_all(grown, pairs, low_half)
    ending_all = spread_all(steps * shrunk, pairs, low_half)
    dy_grown = (dy * grown_all).astype(BF16)
    x_end = (xval * ending_all).astype(BF16)
    dstate[...] = dleave * spread_all(final, pairs, low_half[0:1, :]) + dot(
        cmat, dy_grown, ((0,), (0,))
    )
    owner = (iota((chans, LANES), 0) // P_SIZE == iota((chans, LANES), 1)).astype(F32)
    near = dot(xval * from_state, owner, precision=HIGH) * shrunk
    reach = dot(dy * across, owner, precision=HIGH) * grown
    kept = jnp.sum(entering.astype(F32) * dleave, axis=0, keepdims=True)
    kept = dot(jnp.broadcast_to(kept, (8, chans)), owner, precision=HIGH)[0:1, :] * final
    pairs_sum = jnp.zeros((rows, rows), F32)
    head_lane = iota((rows, LANES), 1)
    col_sum = jnp.zeros((rows, LANES), F32)
    row_sums = []
    for pair in range(pairs):
        lanes = slice(pair * LANES, (pair + 1) * LANES)
        products = dot(stack_heads(xmat[:, lanes], low_half), dy_half[:, lanes], ((1,), (1,)))
        weights = []
        for place, head in enumerate((2 * pair, 2 * pair + 1)):
            product = products[place * rows : (place + 1) * rows, :]
            differ = cumul_t[head : head + 1, :] - cumul[:, head : head + 1]
            decay = jnp.where(later, jnp.exp(jnp.minimum(differ, 0.0)), 0.0)
            weight = decay * scores
            step_col = steps[:, head : head + 1]
            weights.append(weight.astype(BF16))
            pairs_sum = pairs_sum + decay * product * step_col
            terms = weight * product
            col_sum = jnp.where(head_lane == head, jnp.sum(terms, axis=1, keepdims=True), col_sum)
            row_sums.append(jnp.sum(terms * step_col, axis=0, keepdims=True))
        inside = dot(
            jnp.concatenate(weights, axis=1), stack_heads(dy_half[:, lanes], low_half)
        )
        dx = spread(steps, pair, low_half) * (
            inside + spread(shrunk, pair, low_half) * from_state[:, lanes]
        )
        dx = dx + skip[0:1, lanes] * dy[:, lanes]
        gext[0:rows, lanes] = dx * slope[:, lanes]
    pairs_half = pairs_sum.astype(BF16)
    d_b = dot(pairs_half, cmat) + dot(x_end, dleave_half, ((1,), (1,)))
    d_c = dot(pairs_half, bmat, ((0,), (0,))) + dot(dy_grown, entering, ((1,), (1,)))
    gext[0:rows, chans : chans + half] = d_b * slope[:, chans : chans + half]
    gext[0:rows, chans + half :] = d_c * slope[:, chans + half :]

    row_sum = jnp.concatenate(
        row_sums + [jnp.zeros((LANES - 2 * pairs, rows), F32)], axis=0
    ).T
    d_logs = dot((row <= col).astype(F32), row_sum - steps * col_sum + reach, precision=HIGH)
    d_logs = d_logs + dot((row > col).astype(F32), steps * near, precision=HIGH) + kept
    d_steps = col_sum + near - heads[1:2, :] * d_logs
    d_pre = d_steps * jax.nn.sigmoid(dt_pre)
    dbd[:, wide:] = d_pre.astype(BF16)
    dheads[0:1, :] += jnp.sum(d_pre, axis=0, keepdims=True)
    dheads[1:2, :] += jnp.sum(d_logs * logs, axis=0, keepdims=True)
    dskip[0:1, :] += jnp.sum(dy * xval, axis=0, keepdims=True)

    gext[rows : rows + 8, :] = halo[...]
    g = gext[0:rows, :]
    halo[...] = g[0:8, :]
    d_in = jnp.zeros((rows, chans + wide), F32)
    for tap in range(4):
        d_in = d_in + taps[tap : tap + 1, :] * gext[pl.ds(3 - tap, rows), :]
        dtaps[tap : tap + 1, :] += jnp.sum(g * ext[pl.ds(5 + tap, rows), :], axis=0, keepdims=True)
    dtaps[4:5, :] += jnp.sum(g, axis=0, keepdims=True)
    dx_out[...] = d_in[:, :chans].astype(BF16)
    dbd[:, :wide] = d_in[:, chans:].astype(BF16)


MESH = pl.DeviceIdType.MESH
ANY = pl.BlockSpec(memory_space=pl.ANY)


class Place:
    def __init__(self, dp, sp, seqs):
        self.dp, self.sp, self.seqs = dp, sp, seqs
        self.groups = sp // seqs
        self.chips = sp // 2
        self.per = self.groups // 2
        self.p = lax.axis_index("dp")
        self.s = lax.axis_index("sp")
        self.chip = self.s // 2
        self.core = lax.rem(self.s, 2)
        self.seq = self.s // self.groups
        self.group = lax.rem(self.s, self.groups)
        self.low = self.seq * self.per
        self.high = self.low + self.per - 1
        self.bits = [1 << i for i in range(dp.bit_length() - 1)]

    def along_sp(self, other):
        return (self.p, other)

    def along_dp(self, other):
        return (other, self.s)

    def flip(self, bit):
        return self.p + bit - 2 * bit * lax.rem(self.p // bit, 2)

    def masked(self, mask):
        other = self.p
        for bit in self.bits:
            if mask & bit:
                other = other + bit - 2 * bit * lax.rem(self.p // bit, 2)
        return other

    def sp_peer(self, step):
        return lax.rem(self.s + step, self.sp)

    def meet(self, sp_peers=True, dp_peers=True, group_peers=False, more=0):
        barrier = pltpu.get_barrier_semaphore()
        peers = []
        if sp_peers:
            peers += [self.along_sp(self.sp_peer(i)) for i in range(1, self.sp)]
        if group_peers:
            peers += [self.along_sp(self.group_peer(i)) for i in range(1, self.groups)]
        if dp_peers:
            peers += [self.along_dp(self.masked(m)) for m in range(1, self.dp)]
        for peer in peers:
            pl.semaphore_signal(barrier, inc=1, device_id=peer, device_id_type=MESH)
        pl.semaphore_wait(barrier, len(peers) + more)

    def group_peer(self, step):
        return self.seq * self.groups + lax.rem(self.group + step, self.groups)


def remote(src, dst, send, recv, device):
    return pltpu.make_async_remote_copy(
        src_ref=src, dst_ref=dst, send_sem=send, recv_sem=recv, device_id=device,
        device_id_type=MESH,
    )


def dma(*shape):
    return pltpu.SemaphoreType.DMA(shape)


class DpTree:
    @staticmethod
    def scratch(dp):
        return [dma(2, dp), dma(2, dp, dp.bit_length() - 1)]

    def __init__(self, place, part, recv, send):
        self.at, self.part, self.recv, self.send = place, part, recv, send

    def children(self, odd, mask):
        at = self.at
        order = at.bits if odd == 0 else at.bits[::-1]
        last = max([order.index(b) for b in order if mask & b], default=-1)
        src = self.part(at.masked(mask), odd)
        return [
            remote(
                src, src, self.send.at[odd, mask, at.bits.index(bit)],
                self.recv.at[odd, mask ^ bit], at.along_dp(at.flip(bit)),
            )
            for bit in order[last + 1 :]
        ]

    def start(self, odd):
        for copy in self.children(odd, 0):
            copy.start()

    def arrived(self, odd, mask):
        at = self.at
        dst = self.part(at.masked(mask), odd)
        remote(dst, dst, self.send.at[odd, 0, 0], self.recv.at[odd, mask], at.along_dp(at.p)).wait_recv()

    def passed(self, odd, mask):
        order = self.at.bits if odd == 0 else self.at.bits[::-1]
        return not mask & order[-1]

    def forward(self):
        for mask in sorted(range(1, self.at.dp), key=lambda m: (bin(m).count("1"), m)):
            for odd in range(2):
                if self.passed(odd, mask):
                    self.arrived(odd, mask)
                    for copy in self.children(odd, mask):
                        copy.start()

    def complete(self):
        for mask in range(1, self.at.dp):
            for odd in range(2):
                if not self.passed(odd, mask):
                    self.arrived(odd, mask)

    def finish(self):
        for odd in range(2):
            for mask in range(self.at.dp):
                for copy in self.children(odd, mask):
                    copy.wait_send()


class Owners:
    def __init__(self, place):
        self.at, self.each = place, place.sp // place.dp

    def holder(self, seq):
        at = self.at
        p, s = lax.rem(at.s // self.each + at.p, at.dp), seq * at.groups + at.p
        return (p, s), (p == at.p) & (s == at.s)

    def first(self, p):
        at = self.at
        return lax.rem(p + at.dp - at.group, at.dp) * self.each

    def owner(self, i):
        at = self.at
        p, s = at.group, self.first(at.p) + i
        return (p, s), (p == at.p) & (s == at.s)

    def meet(self, spread):
        barrier = pltpu.get_barrier_semaphore()
        holders = [self.holder(seq) for seq in range(self.at.seqs)]
        owners = [self.owner(i) for i in range(self.each)]
        greet, wait = (owners, holders) if spread else (holders, owners)
        for device, mine in greet:

            @pl.when(jnp.logical_not(mine))
            def _():
                pl.semaphore_signal(barrier, inc=1, device_id=device, device_id_type=MESH)

        count = jnp.int32(0)
        for _, mine in wait:
            count = count + jnp.where(mine, 0, 1)
        return count


class OutGather:
    @staticmethod
    def scratch(dp, sp, seqs):
        return [dma(seqs), dma(sp), dma(1)] + DpTree.scratch(dp)

    def __init__(self, place, x, out, sent, got, local, *tree):
        self.at, self.x, self.out = place, x, out
        self.sent, self.got, self.local = sent, got, local.at[0]
        self.ways = Owners(place)
        each = self.ways.each
        size = each // 2
        part = lambda p, odd: out.at[pl.ds(self.ways.first(p) + odd * size, size)]
        self.tree = DpTree(place, part, *tree)

    def shard_copy(self, seq):
        at = self.at
        device, mine = self.ways.holder(seq)
        return jnp.logical_not(mine), remote(
            self.x, self.out.at[at.s], self.sent.at[seq], self.got.at[at.s], device
        )

    def keep(self):
        return pltpu.make_async_copy(self.x, self.out.at[self.at.s], self.local)

    def start(self):
        for seq in range(self.at.seqs):
            needed, copy = self.shard_copy(seq)
            pl.when(needed)(copy.start)
        for i in range(self.ways.each):
            pl.when(self.ways.owner(i)[1])(lambda: self.keep().start())

    def along_dp(self, odd):
        at, each = self.at, self.ways.each
        for i in range(odd * each // 2, (odd + 1) * each // 2):
            _, mine = self.ways.owner(i)
            slot = self.ways.first(at.p) + i
            pl.when(mine)(lambda: self.keep().wait())

            @pl.when(jnp.logical_not(mine))
            def _():
                dst = self.out.at[slot]
                remote(dst, dst, self.sent.at[0], self.got.at[slot], at.along_sp(at.s)).wait_recv()

        self.tree.start(odd)

    def forward(self):
        self.tree.forward()

    def complete(self):
        self.tree.complete()

    def finish(self):
        for seq in range(self.at.seqs):
            needed, copy = self.shard_copy(seq)
            pl.when(needed)(copy.wait_send)
        self.tree.finish()


class BlockReduce:
    @staticmethod
    def scratch(dp, sp, seqs, rows, cols, own):
        chips, sides = sp // 2, (2 if sp // seqs > 4 else 1)
        block = lambda *n: pltpu.VMEM(n + (rows, cols), BF16)
        return ([block(chips)] if own else []) + [
            block(chips), block(sides, chips), block(seqs), dma(7, chips), dma(2, seqs),
        ]

    def __init__(self, place, part, acc, cross, chain, total, sems, ends):
        self.at, self.part, self.acc = place, part, acc
        self.cross, self.chain, self.total = cross, chain, total
        (self.local, self.cross_send, self.cross_recv, self.chain_send, self.low_recv,
         self.high_recv, self.far_send) = (sems.at[i] for i in range(7))
        self.end_send, self.end_recv = ends.at[0], ends.at[1]

    def mine(self, k):
        return self.part.at[k * 2 + self.at.core] if self.acc is None else self.acc.at[k]

    def keep(self, k):
        return pltpu.make_async_copy(
            self.part.at[k * 2 + self.at.core], self.acc.at[k], self.local.at[k]
        )

    def crossing(self, k):
        at = self.at
        return remote(
            self.part.at[k * 2 + 1 - at.core], self.cross.at[k], self.cross_send.at[k],
            self.cross_recv.at[k], at.along_sp(at.chip * 2 + 1 - at.core),
        )

    def onward(self, k, up):
        at = self.at
        side = 0 if up else self.chain.shape[0] - 1
        return remote(
            self.mine(k), self.chain.at[side, k], self.chain_send.at[k],
            (self.low_recv if up else self.high_recv).at[k],
            at.along_sp((at.chip + (1 if up else -1)) * 2 + at.core),
        )

    def ending(self, k):
        at = self.at
        return remote(
            self.mine(k), self.total.at[at.seq], self.far_send.at[k], self.end_recv.at[at.seq],
            at.along_sp(k * 2 + at.core),
        )

    def exit_of(self, k):
        return jnp.clip(k, self.at.low, self.at.high)

    def add(self, k, other):
        mine = self.mine(k)
        mine[...] = (mine[...].astype(F32) + other[...].astype(F32)).astype(BF16)

    def start(self, k):
        self.crossing(k).start()
        if self.acc is not None:
            self.keep(k).start()

    def upstream(self, k, out):
        at = self.at

        @pl.when((at.chip <= out) & (at.chip > at.low))
        def _():
            self.onward(k, True).wait_recv()
            self.add(k, self.chain.at[0, k])

        @pl.when((at.chip >= out) & (at.chip < at.high))
        def _():
            self.onward(k, False).wait_recv()
            self.add(k, self.chain.at[self.chain.shape[0] - 1, k])

    def collect(self, k):
        at, out = self.at, self.exit_of(k)
        self.crossing(k).wait_recv()
        if self.acc is not None:
            self.keep(k).wait()
        self.add(k, self.cross.at[k])

        @pl.when(at.chip != out)
        def _():
            self.upstream(k, out)
            pl.when(at.chip < out)(lambda: self.onward(k, True).start())
            pl.when(at.chip > out)(lambda: self.onward(k, False).start())

    def settle(self, k):
        at, out = self.at, self.exit_of(k)

        @pl.when(at.chip == out)
        def _():
            self.upstream(k, out)

            @pl.when(k == at.chip)
            def _():
                self.total[at.seq] = self.mine(k)[...]

            @pl.when(k != at.chip)
            def _():
                self.ending(k).start()

    def finish(self):
        at = self.at
        for target in range(at.seqs):

            @pl.when(target != at.seq)
            def _():
                dst = self.total.at[target]
                remote(dst, dst, self.end_send.at[0], self.end_recv.at[target], at.along_sp(at.s)).wait_recv()

        for k in range(at.chips):
            out = self.exit_of(k)
            self.crossing(k).wait_send()
            pl.when(at.chip < out)(lambda: self.onward(k, True).wait_send())
            pl.when(at.chip > out)(lambda: self.onward(k, False).wait_send())
            pl.when((at.chip == out) & (at.chip != k))(lambda: self.ending(k).wait_send())


class TreeReduce:
    @staticmethod
    def scratch(dp, half, kept):
        own = [pltpu.VMEM((2, dp // 2) + half, BF16)] if kept else []
        return own + [pltpu.VMEM((2, dp - 1) + half, BF16), dma(3, 2, dp)]

    def __init__(self, place, source, kept, *scratch):
        self.at, self.source = place, source
        self.own = scratch[0] if kept else None
        self.recv, sems = scratch[-2:]
        self.send_sem, self.recv_sem, self.local = (sems.at[i] for i in range(3))
        self.steps = len(place.bits)

    def order(self, odd):
        return self.at.bits if odd == 0 else self.at.bits[::-1]

    def kept(self, odd):
        return [m for m in range(self.at.dp) if not m & self.order(odd)[0]]

    def block(self, odd, mask):
        if self.own is None:
            return self.source(self.at.masked(mask), odd)
        return self.own.at[odd, self.kept(odd).index(mask)]

    def sent(self, odd, i):
        order = self.order(odd)
        before = sum(order[:i])
        masks = [m for m in range(self.at.dp) if m & order[i] and not m & before]
        first = sum(self.at.dp >> (k + 1) for k in range(i))
        return [(first + n, m) for n, m in enumerate(masks)]

    def copy(self, odd, i, n, mask):
        at = self.at
        src = self.block(odd, mask) if i else self.source(at.masked(mask), odd)
        return remote(
            src, self.recv.at[odd, n], self.send_sem.at[odd, n], self.recv_sem.at[odd, n],
            at.along_dp(at.flip(self.order(odd)[i])),
        )

    def load(self, odd, mask):
        n = self.kept(odd).index(mask)
        return pltpu.make_async_copy(
            self.source(self.at.masked(mask), odd), self.own.at[odd, n], self.local.at[odd, n]
        )

    def start(self):
        for odd in range(2):
            for n, mask in self.sent(odd, 0):
                self.copy(odd, 0, n, mask).start()
            if self.own is not None:
                for mask in self.kept(odd):
                    self.load(odd, mask).start()

    def step(self, i):
        for odd in range(2):
            if i == 0 and self.own is not None:
                for mask in self.kept(odd):
                    self.load(odd, mask).wait()
            bit = self.order(odd)[i]
            for n, mask in self.sent(odd, i):
                self.copy(odd, i, n, mask).wait_recv()
                block = self.block(odd, mask ^ bit)
                block[...] = (block[...].astype(F32) + self.recv[odd, n].astype(F32)).astype(BF16)
            if i + 1 < self.steps:
                for n, mask in self.sent(odd, i + 1):
                    self.copy(odd, i + 1, n, mask).start()

    def total(self, odd):
        return self.block(odd, 0)

    def finish(self):
        for odd in range(2):
            for i in range(self.steps):
                for n, mask in self.sent(odd, i):
                    self.copy(odd, i, n, mask).wait_send()


class ShardReduce:
    @staticmethod
    def scratch(dp, sp, shape, kept):
        return [dma(2, sp), dma(1)] + TreeReduce.scratch(dp, (sp // 2,) + shape, kept)

    def __init__(self, place, terms, out, kept, sems, local, *tree):
        self.at, self.out, self.sems, self.local = place, out, sems, local.at[0]
        self.size = place.sp // 2
        source = lambda p, odd: terms.at[p, pl.ds(odd * self.size, self.size)]
        self.tree = TreeReduce(place, source, kept, *tree)

    def sp_copy(self, slot):
        at = self.at
        src = self.tree.total(slot // self.size).at[slot % self.size]
        return remote(
            src, self.out.at[at.s], self.sems.at[0, slot], self.sems.at[1, at.s], at.along_sp(slot)
        )

    def back(self, slot):
        src = self.tree.total(slot // self.size).at[slot % self.size]
        return pltpu.make_async_copy(src, self.out.at[slot], self.local)

    def spread(self):
        for slot in range(self.at.sp):
            pl.when(self.at.s == slot)(lambda: self.back(slot).start())
            pl.when(self.at.s != slot)(lambda: self.sp_copy(slot).start())

    def finish(self):
        at = self.at
        self.tree.finish()
        for slot in range(at.sp):

            @pl.when(at.s == slot)
            def _():
                self.back(slot).wait()

            @pl.when(at.s != slot)
            def _():
                dst = self.out.at[slot]
                remote(dst, dst, self.sems.at[0, 0], self.sems.at[1, slot], at.along_sp(at.s)).wait_recv()
                self.sp_copy(slot).wait_send()


class OutReduce:
    @staticmethod
    def scratch(dp, sp, seqs, shape):
        each = sp // dp
        return [dma(each), dma(seqs), dma(1)] + TreeReduce.scratch(dp, (each // 2,) + shape, True)

    def __init__(self, place, terms, out, sent, got, local, *tree):
        self.at, self.out = place, out
        self.sent, self.got, self.local = sent, got, local.at[0]
        self.ways = Owners(place)
        self.size = self.ways.each // 2
        source = lambda p, odd: terms.at[pl.ds(self.ways.first(p) + odd * self.size, self.size)]
        self.tree = TreeReduce(place, source, True, *tree)

    def shard_copy(self, i):
        at = self.at
        device, mine = self.ways.owner(i)
        src = self.tree.total(i // self.size).at[i % self.size]
        return mine, remote(src, self.out.at[at.seq], self.sent.at[i], self.got.at[at.seq], device)

    def back(self, i):
        src = self.tree.total(i // self.size).at[i % self.size]
        return pltpu.make_async_copy(src, self.out.at[self.at.seq], self.local)

    def spread(self):
        for i in range(self.ways.each):
            mine, copy = self.shard_copy(i)
            pl.when(jnp.logical_not(mine))(copy.start)
            pl.when(mine)(lambda: self.back(i).start())

    def finish(self):
        at = self.at
        self.tree.finish()
        for i in range(self.ways.each):
            mine, copy = self.shard_copy(i)
            pl.when(jnp.logical_not(mine))(copy.wait_send)
            pl.when(mine)(lambda: self.back(i).wait())
        for seq in range(at.seqs):
            _, mine = self.ways.holder(seq)

            @pl.when(jnp.logical_not(mine))
            def _():
                dst = self.out.at[seq]
                remote(dst, dst, self.sent.at[0], self.got.at[seq], at.along_sp(at.s)).wait_recv()


class SmallReduce:
    @staticmethod
    def scratch(dp, sp, seqs, own, common):
        return [
            pltpu.VMEM((dp,) + own, F32), pltpu.VMEM((dp,) + common, F32),
            pltpu.VMEM((seqs,) + own, F32), pltpu.VMEM((sp,) + common, F32),
            dma(4, dp), dma(2, sp), dma(2, seqs),
        ]

    def __init__(self, place, own, common, own_buf, common_buf, out_own, out_common, dp_sems, sp_sems, own_sems):
        self.at = place
        self.parts = ((own, own_buf), (common, common_buf))
        self.out_own, self.out_common = out_own, out_common
        self.dp_sems, self.sp_sems, self.own_sems = dp_sems, sp_sems, own_sems

    def dp_copy(self, which, mask):
        at = self.at
        x, buf = self.parts[which]
        return remote(
            x, buf.at[mask], self.dp_sems.at[2 * which, mask], self.dp_sems.at[2 * which + 1, mask],
            at.along_dp(at.masked(mask)),
        )

    def own_copy(self, i):
        at = self.at
        target = at.group * at.seqs + i
        return target == at.s, remote(
            self.parts[0][1].at[0], self.out_own.at[at.seq], self.own_sems.at[0, i],
            self.own_sems.at[1, at.seq], at.along_sp(target),
        )

    def common_copy(self, i):
        at = self.at
        return remote(
            self.parts[1][1].at[0], self.out_common.at[at.s], self.sp_sems.at[0, i],
            self.sp_sems.at[1, at.s], at.along_sp(at.sp_peer(i)),
        )

    def start(self):
        for which in range(2):
            for mask in range(1, self.at.dp):
                self.dp_copy(which, mask).start()

    def add(self):
        at = self.at
        for which in range(2):
            x, buf = self.parts[which]
            total = x[...]
            for mask in range(1, at.dp):
                self.dp_copy(which, mask).wait_recv()
                total = total + buf[mask]
            buf[0] = total
        for i in range(at.seqs):
            mine, copy = self.own_copy(i)
            pl.when(jnp.logical_not(mine))(copy.start)

            @pl.when(mine)
            def _():
                self.out_own[at.seq] = self.parts[0][1][0]

        self.out_common[at.s] = self.parts[1][1][0]
        for i in range(1, at.sp):
            self.common_copy(i).start()

    def finish(self):
        at = self.at
        for which in range(2):
            for mask in range(1, at.dp):
                self.dp_copy(which, mask).wait_send()
        for i in range(at.seqs):
            mine, copy = self.own_copy(i)
            pl.when(jnp.logical_not(mine))(copy.wait_send)
            sender = i * at.groups + at.s // at.seqs

            @pl.when(sender != at.s)
            def _():
                dst = self.out_own.at[i]
                remote(dst, dst, self.own_sems.at[0, 0], self.own_sems.at[1, i], at.along_sp(at.s)).wait_recv()

        for i in range(1, at.sp):
            slot = at.sp_peer(i)
            dst = self.out_common.at[slot]
            remote(dst, dst, self.sp_sems.at[0, 0], self.sp_sems.at[1, slot], at.along_sp(at.s)).wait_recv()
            self.common_copy(i).wait_send()


def comm_params(number):
    return pltpu.CompilerParams(
        collective_id=number, has_side_effects=True, vmem_limit_bytes=VMEM_LIMIT
    )


class BlockGather:
    @staticmethod
    def scratch(dp, sp, seqs):
        return [dma(5, sp // 2)]

    def __init__(self, place, x, out, sems):
        self.at, self.x, self.out = place, x, out
        self.send, self.recv, self.cross_send, self.cross_recv, self.local = (
            sems.at[i] for i in range(5)
        )

    def chip_at(self, i):
        return lax.rem(self.at.chip + i, self.at.chips)

    def chip_copy(self, i):
        at = self.at
        chip = self.chip_at(i)
        return remote(
            self.x.at[chip // at.per], self.out.at[at.s], self.send.at[i], self.recv.at[at.chip],
            at.along_sp(chip * 2 + at.core),
        )

    def keep(self):
        return pltpu.make_async_copy(self.x.at[self.at.seq], self.out.at[self.at.s], self.local.at[0])

    def crossing(self, k, src):
        at = self.at
        return remote(
            src, self.out.at[k * 2 + at.core], self.cross_send.at[k], self.cross_recv.at[k],
            at.along_sp(at.chip * 2 + 1 - at.core),
        )

    def start(self):
        for i in range(1, self.at.chips):
            self.chip_copy(i).start()
        self.crossing(self.at.chip, self.x.at[self.at.seq]).start()
        self.keep().start()

    def arrive(self, i):
        at = self.at
        k = self.chip_at(i)
        dst = self.out.at[k * 2 + at.core]

        @pl.when(i == 0)
        def _():
            self.keep().wait()

        @pl.when(i != 0)
        def _():
            remote(dst, dst, self.send.at[0], self.recv.at[k], at.along_sp(at.s)).wait_recv()
            self.crossing(k, dst).start()

        return k * 2 + at.core

    def arrive_other(self, i):
        at = self.at
        k = self.chip_at(i)
        dst = self.out.at[k * 2 + 1 - at.core]
        remote(dst, dst, self.cross_send.at[0], self.cross_recv.at[k], at.along_sp(at.s)).wait_recv()
        return k * 2 + 1 - at.core

    def finish(self):
        for i in range(1, self.at.chips):
            self.chip_copy(i).wait_send()
        for k in range(self.at.chips):
            self.crossing(k, self.out.at[k * 2 + self.at.core]).wait_send()


class ColumnGather:
    @staticmethod
    def scratch(dp, sp, seqs):
        return [dma(2, sp), dma(1)] + DpTree.scratch(dp)

    def __init__(self, place, piece, out, along, local, *tree):
        self.at, self.piece, self.out = place, piece, out
        self.along, self.local = along, local.at[0]
        size = place.sp // 2
        self.tree = DpTree(place, lambda p, odd: out.at[p, pl.ds(odd * size, size)], *tree)

    def sp_copy(self, i):
        at = self.at
        target = at.sp_peer(i)
        return remote(
            self.piece(lax.rem(target, at.groups)), self.out.at[at.p, at.s],
            self.along.at[0, i], self.along.at[1, at.s], at.along_sp(target),
        )

    def keep(self):
        at = self.at
        return pltpu.make_async_copy(self.piece(at.group), self.out.at[at.p, at.s], self.local)

    def start(self):
        for i in range(1, self.at.sp):
            self.sp_copy(i).start()
        self.keep().start()

    def along_dp(self, odd):
        at = self.at
        size = at.sp // 2
        for slot in range(odd * size, (odd + 1) * size):

            @pl.when(at.s == slot)
            def _():
                self.keep().wait()

            @pl.when(at.s != slot)
            def _():
                dst = self.out.at[at.p, slot]
                remote(dst, dst, self.along.at[0, 0], self.along.at[1, slot], at.along_sp(at.s)).wait_recv()

        self.tree.start(odd)

    def forward(self):
        self.tree.forward()

    def complete(self):
        self.tree.complete()

    def finish(self):
        for i in range(1, self.at.sp):
            self.sp_copy(i).wait_send()
        self.tree.finish()


class CommonGather:
    @staticmethod
    def scratch(dp, sp, seqs):
        return [dma(2, sp // 2), dma(2, dp), dma(3)]

    def __init__(self, place, x, out, along, across, ends):
        self.at, self.x, self.out = place, x, out
        self.along, self.across, self.ends = along, across, ends

    def chip_copy(self, i):
        at = self.at
        chip = lax.rem(at.chip + i, at.chips)
        return remote(
            self.x, self.out.at[at.core, at.p, at.chip], self.along.at[0, i],
            self.along.at[1, at.chip], at.along_sp(chip * 2 + at.core),
        )

    def keep(self):
        at = self.at
        return pltpu.make_async_copy(self.x, self.out.at[at.core, at.p, at.chip], self.ends.at[0])

    def dp_copy(self, mask):
        at = self.at
        src = self.out.at[at.core, at.p]
        return remote(
            src, src, self.across.at[0, mask], self.across.at[1, mask], at.along_dp(at.masked(mask))
        )

    def crossing(self):
        at = self.at
        src = self.out.at[at.core]
        return remote(
            src, src, self.ends.at[1], self.ends.at[2], at.along_sp(at.chip * 2 + 1 - at.core)
        )

    def start(self):
        for i in range(1, self.at.chips):
            self.chip_copy(i).start()
        self.keep().start()

    def along_dp(self):
        at = self.at
        self.keep().wait()
        for i in range(1, at.chips):
            k = lax.rem(at.chip + i, at.chips)
            dst = self.out.at[at.core, at.p, k]
            remote(dst, dst, self.along.at[0, 0], self.along.at[1, k], at.along_sp(at.s)).wait_recv()
        for mask in range(1, at.dp):
            self.dp_copy(mask).start()

    def cross(self):
        at = self.at
        for mask in range(1, at.dp):
            dst = self.out.at[at.core, at.masked(mask)]
            remote(dst, dst, self.across.at[0, 0], self.across.at[1, mask], at.along_dp(at.p)).wait_recv()
        self.crossing().start()

    def complete(self):
        at = self.at
        dst = self.out.at[1 - at.core]
        remote(dst, dst, self.ends.at[1], self.ends.at[2], at.along_sp(at.s)).wait_recv()

    def finish(self):
        at = self.at
        self.crossing().wait_send()
        for mask in range(1, at.dp):
            self.dp_copy(mask).wait_send()
        for i in range(1, at.chips):
            self.chip_copy(i).wait_send()


def pack_kernel(
    w_bc, w_dt, norm, gate, bc_taps, bc_bias, x_taps, x_bias, dt_bias, a_log, d_skip, out, rows
):
    share, wide = w_bc.shape
    high = out.shape[0] - 16
    out[...] = jnp.zeros(out.shape, BF16)
    out[:share, :wide] = w_bc[...]
    out[:share, wide : wide + w_dt.shape[1]] = w_dt[...]
    rows[...] = jnp.zeros(rows.shape, F32)
    lines = ((0, norm), (1, gate), (6, bc_bias), (7, dt_bias), (8, a_log), (9, d_skip), (14, x_bias))
    for line, ref in lines:
        size = ref.shape[0]
        rows[line : line + 1, :size] = ref[...].astype(F32).reshape(1, size)
    for line, ref in ((2, bc_taps), (10, x_taps)):
        rows[line : line + 4, : ref.shape[1]] = ref[...].astype(F32)
    out[high:, :] = rows[...].astype(BF16)


def run_pack(w_bc, *args):
    share, wide = w_bc.shape
    shape = (-(-share // 16) * 16 + 16, wide + LANES)
    vmem = pl.BlockSpec(memory_space=pltpu.VMEM)
    return pl.pallas_call(
        pack_kernel,
        in_specs=[vmem] * (1 + len(args)),
        out_specs=vmem,
        out_shape=jax.ShapeDtypeStruct(shape, BF16),
        scratch_shapes=[pltpu.VMEM((16, shape[1]), F32)],
        name="pack",
    )(w_bc, *args)


def flatten(values, each, total):
    count, size = values.shape
    lane = iota((size, total), 1)
    place = (iota((size, total), 0) == lane - lane // each * each).astype(BF16)
    wide = dot(values.astype(BF16), place)
    keep = iota((count, total), 0) == iota((count, total), 1) // each
    return jnp.sum(jnp.where(keep, wide, 0.0), axis=0, keepdims=True)


def unpack(place, shards, misc, wb, dt_all, lines, norm, taps, heads, skip, gain):
    share, gate_share, bc_share, x_share, head_share = shards
    high = misc.shape[3] - 16
    wide = misc.shape[4] - LANES
    chans = gain.shape[1]
    count = place.dp * place.sp
    for index in range(count):
        p, s = index // place.sp, index % place.sp
        tile = misc[s % 2, p, s // 2]
        span = slice(index * share, (index + 1) * share)
        wb[span, :wide] = tile[:share, :wide]
        dt_all[span, :] = tile[:share, wide:].astype(F32)
        below = tile[high:, :].astype(F32)
        for line in range(7):
            lines[line, index : index + 1, :] = below[line : line + 1, :]
    own_heads = head_share * place.seqs
    turned = pltpu.roll(dt_all[...], lax.rem(LANES - place.group * own_heads, LANES), 1)
    wb[:, wide:] = jnp.where(iota(turned.shape, 1) < own_heads, turned, 0.0).astype(BF16)
    norm[0:1, :] = flatten(lines[0], share, norm.shape[1])
    mine = lines[1, pl.ds(place.group * place.sp, place.sp), :]
    gain[0:1, :] = flatten(mine, gate_share, chans)
    taps[...] = jnp.zeros(taps.shape, F32)
    for tap in range(5):
        taps[tap : tap + 1, chans:] = flatten(lines[2 + tap], bc_share, wide)
    found = []
    for i in range(place.seqs):
        holder = place.group * place.seqs + i
        tile = misc[lax.rem(holder, 2), place.p, holder // 2]
        below = tile[high:, :].astype(F32)
        taps[0:5, i * x_share : (i + 1) * x_share] = below[10:15, :x_share]
        found.append(below)
    rows = [
        flatten(jnp.concatenate([f[line : line + 1, :LANES] for f in found], axis=0), head_share, LANES)
        for line in (7, 8, 9)
    ]
    rows = [jnp.where(iota((1, LANES), 1) < own_heads, row, 0.0) for row in rows]
    heads[...] = jnp.zeros(heads.shape, F32)
    heads[0:1, :] = rows[0]
    heads[1:2, :] = jnp.exp(rows[1])
    owner = iota((LANES, chans), 0) == iota((LANES, chans), 1) // P_SIZE
    skip[...] = jnp.broadcast_to(dot(rows[2].astype(BF16), owner.astype(BF16)), skip.shape)


def scan_block(wide, chans, x, bd, taps, heads, skip, mixed, enter, ext, halo, state):
    rows = x.shape[0]
    pairs = chans // LANES
    low_half = iota((rows, LANES), 1) < P_SIZE
    ext[0:8, :] = halo[...]
    ext[8 : 8 + rows, :chans] = x.astype(F32)
    ext[8 : 8 + rows, chans:] = bd[:, :wide].astype(F32)
    halo[...] = ext[rows : rows + 8, :]
    pre = conv_pre(ext, rows, taps)
    act = (pre * jax.nn.sigmoid(pre)).astype(BF16)
    half = wide // 2
    bmat = act[:, chans : chans + half]
    cmat = act[:, chans + half :]
    _, steps, logs = steps_of(bd[:, wide:], heads)
    earlier = iota((rows, rows), 0) >= iota((rows, rows), 1)
    cumul = dot(earlier.astype(F32), logs, precision=HIGH)
    cumul_t = cumul.T
    last = cumul[rows - 1 :, :]
    scores = dot(cmat, bmat, ((1,), (1,)))
    grown = jnp.exp(cumul)
    to_end = steps * jnp.exp(last - cumul)
    final = jnp.exp(last)
    entering = state[...]
    entering_half = entering.astype(BF16)
    enter[...] = entering_half
    across = dot(cmat, entering_half)
    for pair in range(pairs):
        lanes = slice(pair * LANES, (pair + 1) * LANES)
        weights = []
        for head in (2 * pair, 2 * pair + 1):
            differ = cumul[:, head : head + 1] - cumul_t[head : head + 1, :]
            decay = jnp.where(earlier, jnp.exp(jnp.minimum(differ, 0.0)), 0.0)
            weights.append((decay * scores).astype(BF16))
        values = act[:, lanes].astype(F32)
        scaled = (values * spread(steps, pair, low_half)).astype(BF16)
        total = dot(jnp.concatenate(weights, axis=1), stack_heads(scaled, low_half))
        total = total + spread(grown, pair, low_half) * across[:, lanes]
        total = total + skip[0:1, lanes] * values
        mixed[:, lanes] = total.astype(BF16)
        ending = (values * spread(to_end, pair, low_half)).astype(BF16)
        state[:, lanes] = entering[:, lanes] * spread(final, pair, low_half[0:1, :]) + dot(
            bmat, ending, ((0,), (0,))
        )


def forward_kernel(
    dp, sp, seqs, wide, inner,
    shards, w_ref, misc_ref, hid_ref, o_ref, cot_ref,
    normed_out, x_out, bd_out, enter_out, dgate_out, dy_out, part_out, tg_out, to_out,
    wx_out, wg_out, wb_out, norm, taps, heads, skip,
    misc, dt_all, lines, gain, hid, wx_all, wb, rows_out, wg, cot, normed, x, bd, mixed, enter, gate, d_gated, gated, dgate, dy,
    part, tg, to, ext, halo, state, sums, mine, got, saves, sum_sems, *sems,
):
    place = Place(dp, sp, seqs)
    chans = gain.shape[1]
    chips = place.chips
    blocks, rows, width = hid.shape
    rest = list(sems)

    def take(scratch):
        taken = rest[: len(scratch)]
        del rest[: len(scratch)]
        return taken

    def columns(first):
        return lambda g: w_ref.at[:, pl.ds(pl.multiple_of(first + g * chans, LANES), chans)]

    half = ColumnGather.scratch(dp, sp, seqs)
    wx_comm = ColumnGather(place, columns(inner), wx_all, *take(half))
    wg_comm = ColumnGather(place, columns(0), wg, *take(half))
    misc_comm = CommonGather(place, misc_ref, misc, *take(CommonGather.scratch(dp, sp, seqs)))
    out_comm = OutGather(place, o_ref, rows_out, *take(OutGather.scratch(dp, sp, seqs)))
    hid_comm = BlockGather(place, hid_ref, hid, *take(BlockGather.scratch(dp, sp, seqs)))
    cot_comm = BlockGather(place, cot_ref, cot, *take(BlockGather.scratch(dp, sp, seqs)))
    place.meet(more=out_comm.ways.meet(True))
    misc_comm.start()
    wx_comm.start()
    halo[...] = jnp.zeros(halo.shape, F32)
    state[...] = jnp.zeros(state.shape, F32)
    sums[...] = jnp.zeros(sums.shape, F32)
    for odd in range(2):
        wx_comm.along_dp(odd)
    wg_comm.start()
    out_comm.start()
    misc_comm.along_dp()
    wx_comm.forward()
    misc_comm.cross()
    for odd in range(2):
        wg_comm.along_dp(odd)
    hid_comm.start()
    for odd in range(2):
        out_comm.along_dp(odd)
    hid_comm.arrive(0)
    misc_comm.complete()
    unpack(place, shards, misc, wb, dt_all, lines, norm, taps, heads, skip, gain)
    wg_comm.forward()
    hid_comm.arrive(1)
    cot_comm.start()
    for i in range(2, chips):
        hid_comm.arrive(i)
    out_comm.forward()
    for i in range(chips):
        hid_comm.arrive_other(i)
    wx_comm.complete()
    keeps = [
        pltpu.make_async_copy(src, dst, saves.at[7, i])
        for i, (src, dst) in enumerate(((wx_all, wx_out), (wb, wb_out)))
    ]
    for keep in keeps:
        keep.start()

    def save(src, dst, index, b):
        return pltpu.make_async_copy(src.at[b], dst.at[b], saves.at[index, b])

    early = ((normed, normed_out), (x, x_out), (bd, bd_out), (enter, enter_out))
    late = ((dgate, dgate_out), (dy, dy_out), (part, part_out))

    def first(b, carry):
        hidden = hid[b].astype(F32)
        scale = lax.rsqrt(jnp.mean(hidden * hidden, axis=-1, keepdims=True) + EPS)
        normed[b] = (hidden * scale * norm[0:1, :]).astype(BF16)
        x[b] = dot(normed[b], wx_all[...].reshape(width, chans)).astype(BF16)
        bd[b] = dot(normed[b], wb[...]).astype(BF16)
        scan_block(
            wide, chans, x[b], bd[b], taps, heads, skip, mixed.at[b], enter.at[b], ext, halo, state
        )
        for index, (src, dst) in enumerate(early):
            save(src, dst, index, b).start()
        return carry

    lax.fori_loop(0, blocks, first, 0)
    wg_comm.complete()
    keeps.append(pltpu.make_async_copy(wg, wg_out, saves.at[7, 2]))
    keeps[-1].start()
    lane = iota((rows, LANES), 1)

    def sum_copies(n):
        return [
            remote(
                mine.at[n], got.at[n, i], sum_sems.at[2 * n, i], sum_sems.at[2 * n + 1, i],
                place.along_sp(place.group_peer(i)),
            )
            for i in range(1, place.groups)
        ]

    def send_sums(n):
        mine[n] = sums[...].T[:blocks]
        for copy in sum_copies(n):
            copy.start()

    def take_sums(n):
        total = mine[n]
        for i, copy in enumerate(sum_copies(n)):
            copy.wait_recv()
            total = total + got[n, i + 1]
        sums[...] = jnp.concatenate([total, jnp.zeros((LANES - blocks, rows), F32)], axis=0).T

    def column(b):
        return jnp.sum(jnp.where(lane == b, sums[...], 0.0), axis=1, keepdims=True)

    def activated(b):
        gate_f = gate[b].astype(F32)
        sig = jax.nn.sigmoid(gate_f)
        return gate_f, sig, mixed[b].astype(F32) * gate_f * sig

    def second(b, carry):
        gate[b] = dot(normed[b], wg[...].reshape(width, chans)).astype(BF16)
        _, _, value = activated(b)
        square = jnp.sum(value * value, axis=1, keepdims=True)
        sums[...] = jnp.where(lane == b, square, sums[...])
        return carry

    lax.fori_loop(0, blocks, second, 0)
    send_sums(0)
    out_comm.complete()
    take_sums(0)
    scales = lax.rsqrt(sums[...] * (1.0 / inner) + EPS)
    sums[...] = scales

    def third(b, carry):
        _, _, value = activated(b)
        gated[b] = (value * column(b) * gain[0:1, :]).astype(BF16)
        part[b] = dot(gated[b], rows_out[...].reshape(chans, width)).astype(BF16)
        save(part, part_out, 6, b).start()
        return carry

    lax.fori_loop(0, blocks, third, 0)
    got[0, 0] = sums[...].T[:blocks]

    def fourth(b):
        d_gated[b] = dot(cot[b], rows_out[...].reshape(chans, width), ((1,), (1,)))
        _, _, value = activated(b)
        cross = jnp.sum(value * d_gated[b] * gain[0:1, :], axis=1, keepdims=True)
        sums[...] = jnp.where(lane == b, cross, sums[...])

    def own_core(i, carry):
        fourth(cot_comm.arrive(i))
        return carry

    def other_core(i, carry):
        fourth(cot_comm.arrive_other(i))
        return carry

    lax.fori_loop(0, chips, own_core, 0)
    lax.fori_loop(0, chips, other_core, 0)
    send_sums(1)
    everything = blocks * rows
    slots = sp // 2
    keep_to = []
    for half in range(2):
        size = chans // 2
        lanes = gated[:, :, half * size : (half + 1) * size].reshape(everything, size)
        value = dot(lanes, cot[...].reshape(everything, width), ((0,), (0,)))
        span = pl.ds(half * slots, slots)
        to[span] = value.astype(BF16).reshape((slots,) + to.shape[1:])
        keep_to.append(pltpu.make_async_copy(to.at[span], to_out.at[span], saves.at[8, half]))
        keep_to[-1].start()
    take_sums(1)
    crosses = sums[...]
    scales = jnp.concatenate([got[0, 0], jnp.zeros((LANES - blocks, rows), F32)], axis=0).T

    def fifth(b, carry):
        scale = jnp.sum(jnp.where(lane == b, scales, 0.0), axis=1, keepdims=True)
        mean = column(b) * scale * (1.0 / inner)
        gate_f, sig, value = activated(b)
        unit = value * scale
        back = scale * (d_gated[b] * gain[0:1, :] - unit * mean)
        dy[b] = (back * gate_f * sig).astype(BF16)
        dgate[b] = (
            back * mixed[b].astype(F32) * sig * (1.0 + gate_f * (1.0 - sig))
        ).astype(BF16)
        for index, (src, dst) in enumerate(late[:2]):
            save(src, dst, 4 + index, b).start()
        return carry

    lax.fori_loop(0, blocks, fifth, 0)
    tile = width // dp
    keep_tg = []
    for p in range(dp):
        lanes = normed[:, :, p * tile : (p + 1) * tile].reshape(everything, tile)
        value = dot(lanes, dgate[...].reshape(everything, chans), ((0,), (0,)))
        tg[p] = value.astype(BF16).reshape(tg.shape[1:])
        keep_tg.append(pltpu.make_async_copy(tg.at[p], tg_out.at[p], saves.at[7, 3 + p]))
        keep_tg[-1].start()
    for n in range(2):
        for copy in sum_copies(n):
            copy.wait_send()
    for comm in (misc_comm, wx_comm, wg_comm, out_comm, hid_comm, cot_comm):
        comm.finish()
    for keep in keeps + keep_tg + keep_to:
        keep.wait()
    for index, (src, dst) in enumerate(early + late):
        for b in range(blocks):
            save(src, dst, index, b).wait()


def run_forward(dp, sp, seqs, wide, inner, shards, w_zx, misc, hidden, w_out, cotangent):
    share = w_zx.shape[0]
    _, rows, width = hidden.shape
    blocks, chans, cols = sp, inner * seqs // sp, misc.shape[1]
    states = wide // 2
    columns = (dp, sp, share, chans)
    w_rows = (sp,) + w_out.shape
    tokens = lambda n: (blocks, rows, n)
    shapes = [
        tokens(width), tokens(chans), tokens(cols), (blocks, states, chans), tokens(chans),
        tokens(chans), tokens(width), columns, w_rows, columns, columns, (width, cols),
    ]
    params = [(8, width), (8, chans + wide), (8, LANES), (8, chans)]
    half = lambda shape: pltpu.VMEM(shape, BF16)
    full = lambda *shape: pltpu.VMEM(shape, F32)
    vmem = pl.BlockSpec(memory_space=pltpu.VMEM)
    return pl.pallas_call(
        functools.partial(forward_kernel, dp, sp, seqs, wide, inner, shards),
        in_specs=[ANY] * 5,
        out_specs=[ANY] * len(shapes) + [vmem] * len(params),
        out_shape=[jax.ShapeDtypeStruct(shape, BF16) for shape in shapes]
        + [jax.ShapeDtypeStruct(shape, F32) for shape in params],
        scratch_shapes=[
            half((2, dp, sp // 2) + misc.shape),
            full(width, LANES),
            full(7, dp * sp, cols),
            full(8, chans),
            half(tokens(width)),
            half(columns),
            half((width, cols)),
            half(w_rows),
            half(columns),
            half(tokens(width)),
            half(tokens(width)), half(tokens(chans)), half(tokens(cols)), half(tokens(chans)),
            half((blocks, states, chans)),
            half(tokens(chans)), full(*tokens(chans)), half(tokens(chans)), half(tokens(chans)),
            half(tokens(chans)), half(tokens(width)),
            half(columns),
            half(w_rows),
            full(rows + 8, chans + wide),
            full(8, chans + wide),
            full(states, chans),
            full(rows, LANES),
            full(2, blocks, rows),
            full(2, sp // seqs, blocks, rows),
            dma(9, max(blocks, dp + 3)),
            dma(4, sp // seqs),
        ]
        + ColumnGather.scratch(dp, sp, seqs) * 2
        + CommonGather.scratch(dp, sp, seqs)
        + OutGather.scratch(dp, sp, seqs)
        + BlockGather.scratch(dp, sp, seqs) * 2,
        compiler_params=comm_params(2),
        name="forward",
    )(w_zx, misc, hidden, w_out, cotangent)


def backward_kernel(
    dp, sp, seqs, wide, chans,
    dy, x, x_before, bd, bd_before, dgate, enter, taps, heads, skip, norm, wg, wx, wb,
    normed_ref, out_part, terms_out, terms_gate, hid_ref, cot_ref, w_zx_ref, w_bc_ref, w_out_ref,
    hidden_out, grad_hidden, grad_zx, grad_bc, grad_dt, norm_sum, grad_out, gate_sum, own_small, common_small,
    ext, gext, halo, dstate, dtaps, dheads, dskip, dx, dbd, normed, part,
    hid, cot, w_zx, w_bc, w_out, loads, tb, og, ob, oo, own, *scratch,
):
    step, steps = pl.program_id(0), pl.num_programs(0)
    chunk = steps - 1 - step
    place = Place(dp, sp, seqs)
    chips = place.chips
    blocks, rows, width = part.shape
    rest = list(scratch)

    def take(n):
        taken = rest[:n]
        del rest[:n]
        return taken

    out_red = BlockReduce(place, out_part, *take(6))
    dn_red = BlockReduce(place, part, None, *take(5))
    gate_red = ShardReduce(place, terms_gate, og, True, *take(5))
    b_red = ShardReduce(place, tb, ob, False, *take(4))
    out_grads = OutReduce(place, terms_out, oo, *take(6))
    few = SmallReduce(place, own, dtaps.at[:, pl.ds(chans, wide)], *take(7))
    x_reds, x_parts = [], []
    while rest:
        tx, landed = take(2)
        x_reds.append((tx, ShardReduce(place, tx, landed, False, *take(4))))
        x_parts.append(landed)
    last_loads = [
        pltpu.make_async_copy(src, dst, loads.at[i])
        for i, (src, dst) in enumerate(
            (
                (normed_ref, normed), (hid_ref, hid), (cot_ref, cot), (w_zx_ref, w_zx),
                (w_bc_ref, w_bc), (w_out_ref, w_out),
            )
        )
    ]

    @pl.when(step == 0)
    def _():
        place.meet(more=out_grads.ways.meet(False))
        for k in range(chips):
            out_red.start(k)
        gate_red.tree.start()
        for load in last_loads:
            load.start()

    scan_backward(
        wide, chans, dy, x, x_before, bd, bd_before, taps, heads, skip, enter,
        dx.at[chunk], dbd.at[chunk], dtaps, dheads, dskip, ext, gext, halo, dstate,
    )
    across = ((1,), (1,))
    total = dot(dgate[...], wg[...], across) + dot(dx[chunk], wx[...], across)
    part[chunk] = (total + dot(dbd[chunk], wb[...], across)).astype(BF16)

    def both_ways(i, fn):
        for k in (place.chip + i, place.chip - i):
            pl.when((k >= 0) & (k < chips))(functools.partial(fn, k))

    @pl.when(step == 0)
    def _():
        for i in range(chips - 1, 0, -1):
            both_ways(i, out_red.collect)
        out_red.collect(place.chip)

    for i in range(chips - 1, -1, -1):

        @pl.when(step == steps - 1 - i * (steps - 3) // chips)
        def _():
            if i:
                both_ways(i, out_red.settle)
            else:
                out_red.settle(place.chip)

    levels = len(place.bits)

    def at_step(when, fn):
        pl.when(step == min(when, steps - 1))(fn)

    at_step(1, out_grads.tree.start)
    for i in range(levels):
        at_step(3 + 2 * i, functools.partial(gate_red.tree.step, i))
        at_step(5 + i, functools.partial(out_grads.tree.step, i))
    at_step(1 + 2 * levels, gate_red.spread)
    at_step(4 + levels, out_grads.spread)

    @pl.when(lax.rem(step, 2) == 1)
    def _():
        dn_red.start(chunk // 2)

    @pl.when((lax.rem(step, 2) == 0) & (step >= 2))
    def _():
        dn_red.collect(chunk // 2 + 1)

    wait = 6

    @pl.when((lax.rem(step, 2) == 0) & (step >= wait))
    def _():
        dn_red.settle(chunk // 2 + wait // 2)

    @pl.when(step == steps - 1)
    def _():
        for load in last_loads:
            load.wait()
        rows_all = blocks * rows
        share_rows = tb.shape[1] * tb.shape[2]
        size = chans // len(x_reds)
        own[:, :chans] = dtaps[:, :chans]
        own[5:6, :chans] = dskip[0:1, :]
        own[:, chans:] = dheads[...]
        few.start()

        def terms(red, out, values):
            for p in range(dp):
                columns = normed[:, :, p * share_rows : (p + 1) * share_rows]
                value = dot(columns.reshape(rows_all, share_rows), values, ((0,), (0,)))
                out[p] = value.astype(BF16).reshape(out.shape[1:])
            red.tree.start()

        for n, (tx, red) in enumerate(x_reds):
            terms(red, tx, dx[:, :, n * size : (n + 1) * size].reshape(rows_all, size))
        dn_red.collect(jnp.int32(0))
        terms(b_red, tb, dbd[...].reshape(rows_all, -1))
        for k in range(chips - 1 - (steps - 1 - wait) // 2 - 1, 0, -1):
            dn_red.settle(jnp.int32(k))
        few.add()
        late = [red for _, red in x_reds] + [b_red]
        for i in range(levels):
            for red in late:
                red.tree.step(i)
                if i == levels - 1:
                    red.spread()
            if i == 0:
                dn_red.settle(jnp.int32(0))
        out_red.finish()
        hidden_out[...] = (hid[...].astype(F32) + out_red.total[...].astype(F32)).astype(BF16)
        out_grads.finish()
        value = oo[0].astype(F32)
        for seq in range(1, seqs):
            value = value + oo[seq].astype(F32)
        grad_out[...] = value
        gate_sum[...] = jnp.broadcast_to(
            jnp.sum(value * w_out[...].astype(F32), axis=1, keepdims=True), gate_sum.shape
        )
        gate_red.finish()
        by_seq = lambda ref, g: functools.reduce(
            jnp.add, [ref[seq * place.groups + g].astype(F32) for seq in range(seqs)]
        )
        inner = grad_zx.shape[1] // 2
        norm_total = jnp.zeros((grad_zx.shape[0], 1), F32)

        def write(first, value):
            lanes = slice(first, first + value.shape[1])
            grad_zx[:, lanes] = value
            return jnp.sum(value * w_zx[:, lanes].astype(F32), axis=1, keepdims=True)

        for g in range(place.groups):
            norm_total = norm_total + write(g * chans, by_seq(og, g))
        dn_red.finish()
        for seq in range(seqs):
            value = hid[seq].astype(F32)
            scale = lax.rsqrt(jnp.mean(value * value, axis=-1, keepdims=True) + EPS)
            unit = value * scale
            weighted = dn_red.total[seq].astype(F32) * norm[0:1, :]
            weighted = weighted - unit * jnp.mean(weighted * unit, axis=-1, keepdims=True)
            grad_hidden[seq] = (cot[seq].astype(F32) + scale * weighted).astype(BF16)
        few.finish()
        own_small[...] = functools.reduce(jnp.add, [few.out_own[seq] for seq in range(seqs)])
        common_small[...] = functools.reduce(jnp.add, [few.out_common[slot] for slot in range(sp)])
        for n, landed in enumerate(x_parts):
            x_reds[n][1].finish()
            for g in range(place.groups):
                norm_total = norm_total + write(inner + g * chans + n * size, by_seq(landed, g))
        b_red.finish()
        value = functools.reduce(jnp.add, [ob[slot, :, :wide].astype(F32) for slot in range(sp)])
        grad_bc[...] = value
        norm_total = norm_total + jnp.sum(value * w_bc[...].astype(F32), axis=1, keepdims=True)
        norm_sum[...] = jnp.broadcast_to(norm_total, norm_sum.shape)
        for g in range(place.groups):
            grad_dt[g] = functools.reduce(
                jnp.add,
                [ob[seq * place.groups + g, :, wide:].astype(F32) for seq in range(seqs)],
            )


def run_backward(
    dp, sp, seqs, dy, x, bd, dgate, enter, taps, heads, skip, norm, wg, wx, wb,
    normed, out_part, terms_out, terms_gate, hidden, cotangent, w_zx, w_bc, w_out, wide,
):
    blocks, rows, chans = x.shape
    states = wide // 2
    cols, width = bd.shape[2], normed.shape[2]
    share = terms_gate.shape[2]
    groups = sp // seqs
    pieces = 2 if chans % (2 * LANES) == 0 else 1
    back = lambda i: blocks - 1 - i
    block = lambda n: pl.BlockSpec((None, rows, n), lambda i: (back(i), 0, 0))
    whole = lambda a: pl.BlockSpec(a.shape, lambda i: (0,) * a.ndim)
    before = lambda n: pl.BlockSpec(
        (None, 16, n), lambda i: (jnp.maximum(back(i) - 1, 0), rows // 16 - 1, 0)
    )
    outs = [
        jax.ShapeDtypeStruct(hidden.shape, BF16),
        jax.ShapeDtypeStruct(hidden.shape, BF16),
        jax.ShapeDtypeStruct(w_zx.shape, F32),
        jax.ShapeDtypeStruct(w_bc.shape, F32),
        jax.ShapeDtypeStruct((groups, share, LANES), F32),
        jax.ShapeDtypeStruct((share, LANES), F32),
        jax.ShapeDtypeStruct(w_out.shape, F32),
        jax.ShapeDtypeStruct((w_out.shape[0], LANES), F32),
        jax.ShapeDtypeStruct((8, chans + LANES), F32),
        jax.ShapeDtypeStruct((8, wide), F32),
    ]
    vmem = lambda a: pltpu.VMEM(a.shape, a.dtype)
    scratch = [
        pltpu.VMEM((rows + 8, chans + wide), F32),
        pltpu.VMEM((rows + 8, chans + wide), F32),
        pltpu.VMEM((8, chans + wide), F32),
        pltpu.VMEM((states, chans), F32),
        pltpu.VMEM((8, chans + wide), F32),
        pltpu.VMEM((8, LANES), F32),
        pltpu.VMEM((8, chans), F32),
        pltpu.VMEM((blocks, rows, chans), BF16),
        pltpu.VMEM((blocks, rows, cols), BF16),
        vmem(normed),
        pltpu.VMEM((blocks, rows, width), BF16),
        vmem(hidden), vmem(cotangent), vmem(w_zx), vmem(w_bc), vmem(w_out),
        dma(6),
        pltpu.VMEM((dp, sp, share, cols), BF16),
        pltpu.VMEM((sp, share, chans), BF16),
        pltpu.VMEM((sp, share, cols), BF16),
        pltpu.VMEM((seqs,) + w_out.shape, BF16),
        pltpu.VMEM((8, chans + LANES), F32),
    ]
    scratch += BlockReduce.scratch(dp, sp, seqs, rows, width, True)
    scratch += BlockReduce.scratch(dp, sp, seqs, rows, width, False)
    scratch += ShardReduce.scratch(dp, sp, (share, chans), True)
    scratch += ShardReduce.scratch(dp, sp, (share, cols), False)
    scratch += OutReduce.scratch(dp, sp, seqs, w_out.shape)
    scratch += SmallReduce.scratch(dp, sp, seqs, (8, chans + LANES), (8, wide))
    for _ in range(pieces):
        shape = (share, chans // pieces)
        scratch += [pltpu.VMEM((dp, sp) + shape, BF16), pltpu.VMEM((sp,) + shape, BF16)]
        scratch += ShardReduce.scratch(dp, sp, shape, False)
    return pl.pallas_call(
        functools.partial(backward_kernel, dp, sp, seqs, wide, chans),
        grid=(blocks,),
        in_specs=[
            block(chans), block(chans), before(chans), block(cols), before(cols), block(chans),
            pl.BlockSpec((None, states, chans), lambda i: (back(i), 0, 0)),
            whole(taps), whole(heads), whole(skip), whole(norm), whole(wg), whole(wx), whole(wb),
        ]
        + [ANY] * 9,
        out_specs=[whole(out) for out in outs],
        out_shape=outs,
        scratch_shapes=scratch,
        compiler_params=comm_params(4),
        name="backward",
    )(
        dy, x, x, bd, bd, dgate, enter, taps, heads, skip, norm, wg, wx, wb,
        normed, out_part, terms_out, terms_gate, hidden, cotangent, w_zx, w_bc, w_out,
    )


def finish_kernel(
    dp, sp, seqs,
    hidden, grad, zx, bc, dt_parts, norm_sum, out, gate_sum, own, common, w_dt, norm_gain, gate_gain,
    hidden_to, grad_to, zx_to, bc_to, dt_to, norm_to, bc_taps, bc_bias, x_taps, x_bias, g_dt, g_log,
    g_skip, gate_to, out_to, tall,
):
    place = Place(dp, sp, seqs)
    for src, dst in ((hidden, hidden_to), (grad, grad_to), (zx, zx_to), (bc, bc_to), (out, out_to)):
        dst[...] = src[...]
    share, heads = w_dt.shape
    each = heads // place.groups
    lane = iota((share, LANES), 1)
    value = jnp.zeros((share, LANES), F32)
    for g in range(place.groups):
        part = jnp.where(lane < each, dt_parts[g], 0.0)
        value = value + (pltpu.roll(part, g * each, 1) if g else part)
    value = value[:, :heads]
    dt_to[...] = value
    dt_sum = jnp.sum(value * w_dt[...].astype(F32), axis=1, keepdims=True)

    def row(column):
        size = column.shape[0]
        wide = -(-size // LANES) * LANES
        tall[:size, :] = jnp.broadcast_to(column, (size, LANES))
        return tall[:wide, :].T[0:1, :size]

    share_sum = row(norm_sum[:, 0:1] + dt_sum)
    norm_to[...] = (share_sum / norm_gain[...].astype(F32).reshape(1, share)).reshape(share)
    size = gate_gain.shape[0]
    gate_to[...] = (row(gate_sum[:, 0:1]) / gate_gain[...].astype(F32).reshape(1, size)).reshape(size)
    x_share, bc_share = x_bias.shape[0], bc_bias.shape[0]
    chans = own.shape[1] - LANES
    place_in = lax.rem(place.s, place.seqs)
    mine = jnp.zeros((8, x_share), F32)
    for i in range(place.seqs):
        mine = mine + jnp.where(place_in == i, own[:, i * x_share : (i + 1) * x_share], 0.0)
    x_taps[...] = mine[0:4]
    x_bias[...] = mine[4:5].reshape(x_share)
    head_share = g_dt.shape[0]
    owner = (iota((x_share, LANES), 0) // P_SIZE == iota((x_share, LANES), 1)).astype(F32)
    skips = dot(mine, owner, precision=HIGH)[5:6, :head_share]
    g_skip[...] = skips.reshape(head_share)
    per_head = own[:, chans:]
    turned = per_head
    for i in range(1, place.seqs):
        turned = jnp.where(place_in == i, pltpu.roll(per_head, LANES - i * head_share, 1), turned)
    g_dt[...] = turned[0:1, :head_share].reshape(head_share)
    g_log[...] = turned[1:2, :head_share].reshape(head_share)
    wide = common.shape[1]
    index = place.p * sp + place.s
    pick = (iota((wide, LANES), 0) == iota((wide, LANES), 1) + index * bc_share).astype(F32)
    mine = dot(common[...], pick, precision=HIGH)[:, :bc_share]
    bc_taps[...] = mine[0:4]
    bc_bias[...] = mine[4:5].reshape(bc_share)


def run_finish(dp, sp, seqs, x_share, head_share, bc_share, *args):
    hidden, grad, zx, bc, _, _, out, _, _, _, w_dt, norm_gain, gate_gain = args
    vmem = pl.BlockSpec(memory_space=pltpu.VMEM)
    shapes = [
        hidden.shape, grad.shape, zx.shape, bc.shape, w_dt.shape, norm_gain.shape, (4, bc_share),
        (bc_share,), (4, x_share), (x_share,), (head_share,), (head_share,), (head_share,),
        gate_gain.shape, out.shape,
    ]
    kinds = [BF16, BF16] + [F32] * 13
    tall = max(-(-n // LANES) * LANES for n in (norm_gain.shape[0], gate_gain.shape[0]))
    return pl.pallas_call(
        functools.partial(finish_kernel, dp, sp, seqs),
        in_specs=[vmem] * len(args),
        out_specs=[vmem] * len(shapes),
        out_shape=[jax.ShapeDtypeStruct(s, k) for s, k in zip(shapes, kinds)],
        scratch_shapes=[pltpu.VMEM((tall, LANES), F32)],
        compiler_params=pltpu.CompilerParams(vmem_limit_bytes=VMEM_LIMIT),
        name="finish",
    )(*args)


def on_device(
    dp, sp,
    hidden_in, w_zx, w_bc, w_dt, norm_gain, conv_bc_weight, conv_bc_bias,
    conv_x_weight, conv_x_bias, dt_bias, a_log, d_skip, gate_gain, w_out, cotangent,
):
    seqs, width = hidden_in.shape[0], hidden_in.shape[2]
    wide, heads = w_bc.shape[1], w_dt.shape[1]
    inner = heads * P_SIZE
    chans = inner * seqs // sp
    x_share, head_share, bc_share = conv_x_bias.shape[0], dt_bias.shape[0], conv_bc_bias.shape[0]
    misc = run_pack(
        w_bc, w_dt, norm_gain, gate_gain, conv_bc_weight.T, conv_bc_bias, conv_x_weight.T,
        conv_x_bias, dt_bias, a_log, d_skip,
    )
    shards = (w_zx.shape[0], gate_gain.shape[0], bc_share, x_share, head_share)
    (normed, x, bd, entering, dgate, dy, out_part, terms_gate, terms_out, wx, wg, wb,
     norm, taps, head_rows, skip) = run_forward(
        dp, sp, seqs, wide, inner, shards, w_zx, misc, hidden_in, w_out, cotangent
    )
    grads = run_backward(
        dp, sp, seqs, dy, x, bd, dgate, entering, taps, head_rows, skip, norm,
        wg.reshape(width, chans), wx.reshape(width, chans), wb, normed, out_part, terms_out,
        terms_gate, hidden_in, cotangent, w_zx, w_bc, w_out, wide,
    )
    results = list(
        run_finish(dp, sp, seqs, x_share, head_share, bc_share, *grads, w_dt, norm_gain, gate_gain)
    )
    for taps_at in (6, 8):
        results[taps_at] = results[taps_at].T
    return tuple(results)


def solution(mesh):
    both = P(("dp", "sp"))
    rows = P(("dp", "sp"), None)
    tokens = P("dp", "sp", None)
    return jax.shard_map(
        functools.partial(on_device, mesh.shape["dp"], mesh.shape["sp"]),
        mesh=mesh,
        in_specs=(
            tokens, rows, rows, rows, both, rows, both, P("sp", None), P("sp"), P("sp"),
            P("sp"), P("sp"), both, rows, tokens,
        ),
        out_specs=(
            tokens, tokens, rows, rows, rows, both, rows, both, P("sp", None), P("sp"),
            P("sp"), P("sp"), P("sp"), both, rows,
        ),
        check_vma=False,
    )
```

```python
import functools

import jax
import jax.numpy as jnp
from jax import lax
from jax.experimental import pallas as pl
from jax.experimental.pallas import tpu as pltpu
from jax.sharding import PartitionSpec as P

P_SIZE = 64
EPS = 1e-05
F32 = jnp.float32
BF16 = jnp.bfloat16
HIGH = lax.Precision.HIGHEST
LANES = 128
PIECES = 3
VMEM_LIMIT = 58 * 1024 * 1024


def dot(left, right, dims=((1,), (0,)), precision=None):
    return lax.dot_general(
        left, right, (dims, ((), ())), precision=precision, preferred_element_type=F32
    )


def parts_of(value, count):
    found = []
    for _ in range(count):
        found.append(value.astype(BF16))
        value = value - found[-1].astype(F32)
    return found


def select_rows(chosen, value):
    size = value.shape[1]
    wide = dot(chosen.astype(BF16), jnp.concatenate(parts_of(value, 3), axis=1))
    return wide[:, :size] + wide[:, size : 2 * size] + wide[:, 2 * size :]


def head_sums(value, owner):
    return dot(jnp.concatenate(parts_of(value, 2), axis=1), jnp.concatenate([owner, owner], axis=0))


def iota(shape, axis):
    return lax.broadcasted_iota(jnp.int32, shape, axis)


def spread(cols, pair, low_half):
    return jnp.where(low_half, cols[:, 2 * pair : 2 * pair + 1], cols[:, 2 * pair + 1 : 2 * pair + 2])


def spread_all(cols, pairs, low_half):
    return jnp.concatenate([spread(cols, pair, low_half) for pair in range(pairs)], axis=1)


def stack_heads(values, low_half):
    zero = jnp.zeros_like(values)
    return jnp.concatenate(
        [jnp.where(low_half, values, zero), jnp.where(low_half, zero, values)], axis=0
    )


def softplus(value):
    return jnp.maximum(value, 0.0) + jnp.log1p(jnp.exp(-jnp.abs(value)))


def conv_pre(ext, rows, taps):
    total = taps[4:5, :]
    for tap in range(4):
        total = total + taps[tap : tap + 1, :] * ext[pl.ds(5 + tap, rows), :]
    return total


def steps_of(dt_raw, head_ref):
    pre = dt_raw.astype(F32) + head_ref[0:1, :]
    steps = softplus(pre)
    return pre, steps, -steps * head_ref[1:2, :]


def scan_backward(
    wide, chans,
    dy_in, x, x_before, bd, bd_before, taps, heads, skip, enter,
    dx_out, dbd, dtaps, dheads, dskip,
    ext, gext, halo, dstate,
):
    step = pl.program_id(0)
    chunk = pl.num_programs(0) - 1 - step
    rows = x.shape[0]
    pairs = chans // LANES
    half = wide // 2
    low_half = iota((rows, LANES), 1) < P_SIZE

    @pl.when(step == 0)
    def _():
        halo[...] = jnp.zeros(halo.shape, F32)
        dstate[...] = jnp.zeros(dstate.shape, F32)
        dtaps[...] = jnp.zeros_like(dtaps)
        dheads[...] = jnp.zeros_like(dheads)
        dskip[...] = jnp.zeros_like(dskip)

    dy_half = dy_in[...]
    dy = dy_half.astype(F32)

    last_rows = x_before.shape[0] - 8
    past = jnp.concatenate(
        [x_before[last_rows:, :], bd_before[last_rows:, :wide]], axis=1
    ).astype(F32)
    ext[0:8, :] = jnp.where(chunk == 0, 0.0, past)
    ext[8 : 8 + rows, :chans] = x[...].astype(F32)
    ext[8 : 8 + rows, chans:] = bd[:, :wide].astype(F32)
    pre = conv_pre(ext, rows, taps)
    sig_pre = jax.nn.sigmoid(pre)
    act = (pre * sig_pre).astype(BF16)
    slope = sig_pre * (1.0 + pre * (1.0 - sig_pre))
    bmat = act[:, chans : chans + half]
    cmat = act[:, chans + half :]
    xmat = act[:, :chans]
    xval = xmat.astype(F32)
    dt_pre, steps, logs = steps_of(bd[:, wide:], heads)
    row, col = iota((rows, rows), 0), iota((rows, rows), 1)
    cumul = select_rows(row >= col, logs)
    cumul_t = cumul.T
    last = cumul[rows - 1 :, :]
    later = row <= col
    scores = dot(bmat, cmat, ((1,), (1,)))
    grown = jnp.exp(cumul)
    shrunk = jnp.exp(last - cumul)
    final = jnp.exp(last)
    entering = enter[...]
    dleave = dstate[...]
    dleave_half = dleave.astype(BF16)
    from_state = dot(bmat, dleave_half)
    across = dot(cmat, entering)
    grown_all = spread_all(grown, pairs, low_half)
    ending_all = spread_all(steps * shrunk, pairs, low_half)
    dy_grown = (dy * grown_all).astype(BF16)
    x_end = (xval * ending_all).astype(BF16)
    dstate[...] = dleave * spread_all(final, pairs, low_half[0:1, :]) + dot(
        cmat, dy_grown, ((0,), (0,))
    )
    owner = (iota((chans, LANES), 0) // P_SIZE == iota((chans, LANES), 1)).astype(BF16)
    kept = jnp.sum(entering.astype(F32) * dleave, axis=0, keepdims=True)
    found = head_sums(
        jnp.concatenate(
            [xval * from_state, dy * across, jnp.broadcast_to(kept, (8, chans))], axis=0
        ),
        owner,
    )
    near = found[:rows] * shrunk
    reach = found[rows : 2 * rows] * grown
    kept = found[2 * rows : 2 * rows + 1] * final
    pairs_sum = jnp.zeros((rows, rows), F32)
    head_lane = iota((rows, LANES), 1)
    col_sum = jnp.zeros((rows, LANES), F32)
    row_sums = []
    for pair in range(pairs):
        lanes = slice(pair * LANES, (pair + 1) * LANES)
        products = dot(stack_heads(xmat[:, lanes], low_half), dy_half[:, lanes], ((1,), (1,)))
        weights = []
        for place, head in enumerate((2 * pair, 2 * pair + 1)):
            product = products[place * rows : (place + 1) * rows, :]
            differ = cumul_t[head : head + 1, :] - cumul[:, head : head + 1]
            decay = jnp.where(later, jnp.exp(jnp.minimum(differ, 0.0)), 0.0)
            weight = decay * scores
            step_col = steps[:, head : head + 1]
            weights.append(weight.astype(BF16))
            pairs_sum = pairs_sum + decay * product * step_col
            terms = weight * product
            col_sum = jnp.where(head_lane == head, jnp.sum(terms, axis=1, keepdims=True), col_sum)
            row_sums.append(jnp.sum(terms * step_col, axis=0, keepdims=True))
        inside = dot(
            jnp.concatenate(weights, axis=1), stack_heads(dy_half[:, lanes], low_half)
        )
        dx = spread(steps, pair, low_half) * (
            inside + spread(shrunk, pair, low_half) * from_state[:, lanes]
        )
        dx = dx + skip[0:1, lanes] * dy[:, lanes]
        gext[0:rows, lanes] = dx * slope[:, lanes]
    pairs_half = pairs_sum.astype(BF16)
    d_b = dot(pairs_half, cmat) + dot(x_end, dleave_half, ((1,), (1,)))
    d_c = dot(pairs_half, bmat, ((0,), (0,))) + dot(dy_grown, entering, ((1,), (1,)))
    gext[0:rows, chans : chans + half] = d_b * slope[:, chans : chans + half]
    gext[0:rows, chans + half :] = d_c * slope[:, chans + half :]

    row_sum = jnp.concatenate(
        row_sums + [jnp.zeros((LANES - 2 * pairs, rows), F32)], axis=0
    ).T
    d_logs = select_rows(row <= col, row_sum - steps * col_sum + reach)
    d_logs = d_logs + select_rows(row > col, steps * near) + kept
    d_steps = col_sum + near - heads[1:2, :] * d_logs
    d_pre = d_steps * jax.nn.sigmoid(dt_pre)
    dbd[:, wide:] = d_pre.astype(BF16)
    dheads[0:1, :] += jnp.sum(d_pre, axis=0, keepdims=True)
    dheads[1:2, :] += jnp.sum(d_logs * logs, axis=0, keepdims=True)
    dskip[0:1, :] += jnp.sum(dy * xval, axis=0, keepdims=True)

    gext[rows : rows + 8, :] = halo[...]
    g = gext[0:rows, :]
    halo[...] = g[0:8, :]
    d_in = jnp.zeros((rows, chans + wide), F32)
    for tap in range(4):
        d_in = d_in + taps[tap : tap + 1, :] * gext[pl.ds(3 - tap, rows), :]
        dtaps[tap : tap + 1, :] += jnp.sum(g * ext[pl.ds(5 + tap, rows), :], axis=0, keepdims=True)
    dtaps[4:5, :] += jnp.sum(g, axis=0, keepdims=True)
    dx_out[...] = d_in[:, :chans].astype(BF16)
    dbd[:, :wide] = d_in[:, chans:].astype(BF16)


MESH = pl.DeviceIdType.MESH
ANY = pl.BlockSpec(memory_space=pl.ANY)


class Place:
    def __init__(self, dp, sp, seqs):
        self.dp, self.sp, self.seqs = dp, sp, seqs
        self.groups = sp // seqs
        self.chips = sp // 2
        self.per = self.groups // 2
        self.p = lax.axis_index("dp")
        self.s = lax.axis_index("sp")
        self.chip = self.s // 2
        self.core = lax.rem(self.s, 2)
        self.seq = self.s // self.groups
        self.group = lax.rem(self.s, self.groups)
        self.low = self.seq * self.per
        self.high = self.low + self.per - 1
        self.bits = [1 << i for i in range(dp.bit_length() - 1)]

    def along_sp(self, other):
        return (self.p, other)

    def along_dp(self, other):
        return (other, self.s)

    def flip(self, bit):
        return self.p + bit - 2 * bit * lax.rem(self.p // bit, 2)

    def masked(self, mask):
        other = self.p
        for bit in self.bits:
            if mask & bit:
                other = other + bit - 2 * bit * lax.rem(self.p // bit, 2)
        return other

    def sp_peer(self, step):
        return lax.rem(self.s + step, self.sp)

    def meet(self, sp_peers=True, dp_peers=True, group_peers=False, more=0):
        barrier = pltpu.get_barrier_semaphore()
        peers = []
        if sp_peers:
            peers += [self.along_sp(self.sp_peer(i)) for i in range(1, self.sp)]
        if group_peers:
            peers += [self.along_sp(self.group_peer(i)) for i in range(1, self.groups)]
        if dp_peers:
            peers += [self.along_dp(self.masked(m)) for m in range(1, self.dp)]
        for peer in peers:
            pl.semaphore_signal(barrier, inc=1, device_id=peer, device_id_type=MESH)
        pl.semaphore_wait(barrier, len(peers) + more)

    def group_peer(self, step):
        return self.seq * self.groups + lax.rem(self.group + step, self.groups)


def remote(src, dst, send, recv, device):
    return pltpu.make_async_remote_copy(
        src_ref=src, dst_ref=dst, send_sem=send, recv_sem=recv, device_id=device,
        device_id_type=MESH,
    )


def dma(*shape):
    return pltpu.SemaphoreType.DMA(shape)


class DpTree:
    @staticmethod
    def scratch(dp):
        return [dma(2, dp), dma(2, dp, dp.bit_length() - 1)]

    def __init__(self, place, part, recv, send):
        self.at, self.part, self.recv, self.send = place, part, recv, send

    def children(self, odd, mask):
        at = self.at
        order = at.bits if odd == 0 else at.bits[::-1]
        last = max([order.index(b) for b in order if mask & b], default=-1)
        src = self.part(at.masked(mask), odd)
        return [
            remote(
                src, src, self.send.at[odd, mask, at.bits.index(bit)],
                self.recv.at[odd, mask ^ bit], at.along_dp(at.flip(bit)),
            )
            for bit in order[last + 1 :]
        ]

    def start(self, odd):
        for copy in self.children(odd, 0):
            copy.start()

    def arrived(self, odd, mask):
        at = self.at
        dst = self.part(at.masked(mask), odd)
        remote(dst, dst, self.send.at[odd, 0, 0], self.recv.at[odd, mask], at.along_dp(at.p)).wait_recv()

    def passed(self, odd, mask):
        order = self.at.bits if odd == 0 else self.at.bits[::-1]
        return not mask & order[-1]

    def forward(self):
        for mask in sorted(range(1, self.at.dp), key=lambda m: (bin(m).count("1"), m)):
            for odd in range(2):
                if self.passed(odd, mask):
                    self.arrived(odd, mask)
                    for copy in self.children(odd, mask):
                        copy.start()

    def complete(self):
        for mask in range(1, self.at.dp):
            for odd in range(2):
                if not self.passed(odd, mask):
                    self.arrived(odd, mask)

    def finish(self):
        for odd in range(2):
            for mask in range(self.at.dp):
                for copy in self.children(odd, mask):
                    copy.wait_send()


class Owners:
    def __init__(self, place):
        self.at, self.each = place, place.sp // place.dp

    def holder(self, seq):
        at = self.at
        p, s = lax.rem(at.s // self.each + at.p, at.dp), seq * at.groups + at.p
        return (p, s), (p == at.p) & (s == at.s)

    def first(self, p):
        at = self.at
        return lax.rem(p + at.dp - at.group, at.dp) * self.each

    def owner(self, i):
        at = self.at
        p, s = at.group, self.first(at.p) + i
        return (p, s), (p == at.p) & (s == at.s)

    def meet(self, spread):
        barrier = pltpu.get_barrier_semaphore()
        holders = [self.holder(seq) for seq in range(self.at.seqs)]
        owners = [self.owner(i) for i in range(self.each)]
        greet, wait = (owners, holders) if spread else (holders, owners)
        for device, mine in greet:

            @pl.when(jnp.logical_not(mine))
            def _():
                pl.semaphore_signal(barrier, inc=1, device_id=device, device_id_type=MESH)

        count = jnp.int32(0)
        for _, mine in wait:
            count = count + jnp.where(mine, 0, 1)
        return count


class OutGather:
    @staticmethod
    def scratch(dp, sp, seqs):
        return [dma(seqs), dma(sp), dma(1)] + DpTree.scratch(dp)

    def __init__(self, place, x, out, sent, got, local, *tree):
        self.at, self.x, self.out = place, x, out
        self.sent, self.got, self.local = sent, got, local.at[0]
        self.ways = Owners(place)
        each = self.ways.each
        size = each // 2
        part = lambda p, odd: out.at[pl.ds(self.ways.first(p) + odd * size, size)]
        self.tree = DpTree(place, part, *tree)

    def shard_copy(self, seq):
        at = self.at
        device, mine = self.ways.holder(seq)
        return jnp.logical_not(mine), remote(
            self.x, self.out.at[at.s], self.sent.at[seq], self.got.at[at.s], device
        )

    def keep(self):
        return pltpu.make_async_copy(self.x, self.out.at[self.at.s], self.local)

    def start(self):
        for seq in range(self.at.seqs):
            needed, copy = self.shard_copy(seq)
            pl.when(needed)(copy.start)
        for i in range(self.ways.each):
            pl.when(self.ways.owner(i)[1])(lambda: self.keep().start())

    def along_dp(self, odd):
        at, each = self.at, self.ways.each
        for i in range(odd * each // 2, (odd + 1) * each // 2):
            _, mine = self.ways.owner(i)
            slot = self.ways.first(at.p) + i
            pl.when(mine)(lambda: self.keep().wait())

            @pl.when(jnp.logical_not(mine))
            def _():
                dst = self.out.at[slot]
                remote(dst, dst, self.sent.at[0], self.got.at[slot], at.along_sp(at.s)).wait_recv()

        self.tree.start(odd)

    def forward(self):
        self.tree.forward()

    def complete(self):
        self.tree.complete()

    def finish(self):
        for seq in range(self.at.seqs):
            needed, copy = self.shard_copy(seq)
            pl.when(needed)(copy.wait_send)
        self.tree.finish()


class BlockReduce:
    @staticmethod
    def scratch(dp, sp, seqs, rows, cols, own):
        chips, sides = sp // 2, (2 if sp // seqs > 4 else 1)
        block = lambda *n: pltpu.VMEM(n + (rows, cols), BF16)
        return ([block(chips)] if own else []) + [
            block(chips), block(sides, chips), block(seqs), dma(7, chips), dma(2, seqs),
        ]

    def __init__(self, place, part, acc, cross, chain, total, sems, ends):
        self.at, self.part, self.acc = place, part, acc
        self.cross, self.chain, self.total = cross, chain, total
        (self.local, self.cross_send, self.cross_recv, self.chain_send, self.low_recv,
         self.high_recv, self.far_send) = (sems.at[i] for i in range(7))
        self.end_send, self.end_recv = ends.at[0], ends.at[1]

    def mine(self, k):
        return self.part.at[k * 2 + self.at.core] if self.acc is None else self.acc.at[k]

    def keep(self, k):
        return pltpu.make_async_copy(
            self.part.at[k * 2 + self.at.core], self.acc.at[k], self.local.at[k]
        )

    def crossing(self, k):
        at = self.at
        return remote(
            self.part.at[k * 2 + 1 - at.core], self.cross.at[k], self.cross_send.at[k],
            self.cross_recv.at[k], at.along_sp(at.chip * 2 + 1 - at.core),
        )

    def onward(self, k, up):
        at = self.at
        side = 0 if up else self.chain.shape[0] - 1
        return remote(
            self.mine(k), self.chain.at[side, k], self.chain_send.at[k],
            (self.low_recv if up else self.high_recv).at[k],
            at.along_sp((at.chip + (1 if up else -1)) * 2 + at.core),
        )

    def ending(self, k):
        at = self.at
        return remote(
            self.mine(k), self.total.at[at.seq], self.far_send.at[k], self.end_recv.at[at.seq],
            at.along_sp(k * 2 + at.core),
        )

    def exit_of(self, k):
        return jnp.clip(k, self.at.low, self.at.high)

    def add(self, k, other):
        mine = self.mine(k)
        mine[...] = (mine[...].astype(F32) + other[...].astype(F32)).astype(BF16)

    def start(self, k):
        self.crossing(k).start()
        if self.acc is not None:
            self.keep(k).start()

    def upstream(self, k, out):
        at = self.at

        @pl.when((at.chip <= out) & (at.chip > at.low))
        def _():
            self.onward(k, True).wait_recv()
            self.add(k, self.chain.at[0, k])

        @pl.when((at.chip >= out) & (at.chip < at.high))
        def _():
            self.onward(k, False).wait_recv()
            self.add(k, self.chain.at[self.chain.shape[0] - 1, k])

    def collect(self, k):
        at, out = self.at, self.exit_of(k)
        self.crossing(k).wait_recv()
        if self.acc is not None:
            self.keep(k).wait()
        self.add(k, self.cross.at[k])

        @pl.when(at.chip != out)
        def _():
            self.upstream(k, out)
            pl.when(at.chip < out)(lambda: self.onward(k, True).start())
            pl.when(at.chip > out)(lambda: self.onward(k, False).start())

    def settle(self, k):
        at, out = self.at, self.exit_of(k)

        @pl.when(at.chip == out)
        def _():
            self.upstream(k, out)

            @pl.when(k == at.chip)
            def _():
                self.total[at.seq] = self.mine(k)[...]

            @pl.when(k != at.chip)
            def _():
                self.ending(k).start()

    def finish(self):
        at = self.at
        for target in range(at.seqs):

            @pl.when(target != at.seq)
            def _():
                dst = self.total.at[target]
                remote(dst, dst, self.end_send.at[0], self.end_recv.at[target], at.along_sp(at.s)).wait_recv()

        for k in range(at.chips):
            out = self.exit_of(k)
            self.crossing(k).wait_send()
            pl.when(at.chip < out)(lambda: self.onward(k, True).wait_send())
            pl.when(at.chip > out)(lambda: self.onward(k, False).wait_send())
            pl.when((at.chip == out) & (at.chip != k))(lambda: self.ending(k).wait_send())


class TreeReduce:
    @staticmethod
    def scratch(dp, half, kept):
        own = [pltpu.VMEM((2, dp // 2) + half, BF16)] if kept else []
        return own + [pltpu.VMEM((2, dp - 1) + half, BF16), dma(3, 2, dp)]

    def __init__(self, place, source, kept, *scratch):
        self.at, self.source = place, source
        self.own = scratch[0] if kept else None
        self.recv, sems = scratch[-2:]
        self.send_sem, self.recv_sem, self.local = (sems.at[i] for i in range(3))
        self.steps = len(place.bits)

    def order(self, odd):
        return self.at.bits if odd == 0 else self.at.bits[::-1]

    def kept(self, odd):
        return [m for m in range(self.at.dp) if not m & self.order(odd)[0]]

    def block(self, odd, mask):
        if self.own is None:
            return self.source(self.at.masked(mask), odd)
        return self.own.at[odd, self.kept(odd).index(mask)]

    def sent(self, odd, i):
        order = self.order(odd)
        before = sum(order[:i])
        masks = [m for m in range(self.at.dp) if m & order[i] and not m & before]
        first = sum(self.at.dp >> (k + 1) for k in range(i))
        return [(first + n, m) for n, m in enumerate(masks)]

    def copy(self, odd, i, n, mask):
        at = self.at
        src = self.block(odd, mask) if i else self.source(at.masked(mask), odd)
        return remote(
            src, self.recv.at[odd, n], self.send_sem.at[odd, n], self.recv_sem.at[odd, n],
            at.along_dp(at.flip(self.order(odd)[i])),
        )

    def load(self, odd, mask):
        n = self.kept(odd).index(mask)
        return pltpu.make_async_copy(
            self.source(self.at.masked(mask), odd), self.own.at[odd, n], self.local.at[odd, n]
        )

    def start(self):
        for odd in range(2):
            for n, mask in self.sent(odd, 0):
                self.copy(odd, 0, n, mask).start()
            if self.own is not None:
                for mask in self.kept(odd):
                    self.load(odd, mask).start()

    def step(self, i):
        for odd in range(2):
            if i == 0 and self.own is not None:
                for mask in self.kept(odd):
                    self.load(odd, mask).wait()
            bit = self.order(odd)[i]
            for n, mask in self.sent(odd, i):
                self.copy(odd, i, n, mask).wait_recv()
                block = self.block(odd, mask ^ bit)
                block[...] = (block[...].astype(F32) + self.recv[odd, n].astype(F32)).astype(BF16)
            if i + 1 < self.steps:
                for n, mask in self.sent(odd, i + 1):
                    self.copy(odd, i + 1, n, mask).start()

    def total(self, odd):
        return self.block(odd, 0)

    def finish(self):
        for odd in range(2):
            for i in range(self.steps):
                for n, mask in self.sent(odd, i):
                    self.copy(odd, i, n, mask).wait_send()


class ShardReduce:
    @staticmethod
    def scratch(dp, sp, shape, kept):
        return [dma(2, sp), dma(1)] + TreeReduce.scratch(dp, (sp // 2,) + shape, kept)

    def __init__(self, place, terms, out, kept, sems, local, *tree):
        self.at, self.out, self.sems, self.local = place, out, sems, local.at[0]
        self.size = place.sp // 2
        source = lambda p, odd: terms.at[p, pl.ds(odd * self.size, self.size)]
        self.tree = TreeReduce(place, source, kept, *tree)

    def sp_copy(self, slot):
        at = self.at
        src = self.tree.total(slot // self.size).at[slot % self.size]
        return remote(
            src, self.out.at[at.s], self.sems.at[0, slot], self.sems.at[1, at.s], at.along_sp(slot)
        )

    def back(self, slot):
        src = self.tree.total(slot // self.size).at[slot % self.size]
        return pltpu.make_async_copy(src, self.out.at[slot], self.local)

    def spread(self):
        for slot in range(self.at.sp):
            pl.when(self.at.s == slot)(lambda: self.back(slot).start())
            pl.when(self.at.s != slot)(lambda: self.sp_copy(slot).start())

    def finish(self):
        at = self.at
        self.tree.finish()
        for slot in range(at.sp):

            @pl.when(at.s == slot)
            def _():
                self.back(slot).wait()

            @pl.when(at.s != slot)
            def _():
                dst = self.out.at[slot]
                remote(dst, dst, self.sems.at[0, 0], self.sems.at[1, slot], at.along_sp(at.s)).wait_recv()
                self.sp_copy(slot).wait_send()


class OutReduce:
    @staticmethod
    def scratch(dp, sp, seqs, shape):
        each = sp // dp
        return [dma(each), dma(seqs), dma(1)] + TreeReduce.scratch(dp, (each // 2,) + shape, True)

    def __init__(self, place, terms, out, sent, got, local, *tree):
        self.at, self.out = place, out
        self.sent, self.got, self.local = sent, got, local.at[0]
        self.ways = Owners(place)
        self.size = self.ways.each // 2
        source = lambda p, odd: terms.at[pl.ds(self.ways.first(p) + odd * self.size, self.size)]
        self.tree = TreeReduce(place, source, True, *tree)

    def shard_copy(self, i):
        at = self.at
        device, mine = self.ways.owner(i)
        src = self.tree.total(i // self.size).at[i % self.size]
        return mine, remote(src, self.out.at[at.seq], self.sent.at[i], self.got.at[at.seq], device)

    def back(self, i):
        src = self.tree.total(i // self.size).at[i % self.size]
        return pltpu.make_async_copy(src, self.out.at[self.at.seq], self.local)

    def spread(self):
        for i in range(self.ways.each):
            mine, copy = self.shard_copy(i)
            pl.when(jnp.logical_not(mine))(copy.start)
            pl.when(mine)(lambda: self.back(i).start())

    def finish(self):
        at = self.at
        self.tree.finish()
        for i in range(self.ways.each):
            mine, copy = self.shard_copy(i)
            pl.when(jnp.logical_not(mine))(copy.wait_send)
            pl.when(mine)(lambda: self.back(i).wait())
        for seq in range(at.seqs):
            _, mine = self.ways.holder(seq)

            @pl.when(jnp.logical_not(mine))
            def _():
                dst = self.out.at[seq]
                remote(dst, dst, self.sent.at[0], self.got.at[seq], at.along_sp(at.s)).wait_recv()


class SmallReduce:
    @staticmethod
    def scratch(dp, sp, seqs, own, common):
        return [
            pltpu.VMEM((dp,) + own, F32), pltpu.VMEM((dp,) + common, F32),
            pltpu.VMEM((seqs,) + own, F32), pltpu.VMEM((sp,) + common, F32),
            dma(4, dp), dma(2, sp), dma(2, seqs),
        ]

    def __init__(self, place, own, common, own_buf, common_buf, out_own, out_common, dp_sems, sp_sems, own_sems):
        self.at = place
        self.parts = ((own, own_buf), (common, common_buf))
        self.out_own, self.out_common = out_own, out_common
        self.dp_sems, self.sp_sems, self.own_sems = dp_sems, sp_sems, own_sems

    def dp_copy(self, which, mask):
        at = self.at
        x, buf = self.parts[which]
        return remote(
            x, buf.at[mask], self.dp_sems.at[2 * which, mask], self.dp_sems.at[2 * which + 1, mask],
            at.along_dp(at.masked(mask)),
        )

    def own_copy(self, i):
        at = self.at
        target = at.group * at.seqs + i
        return target == at.s, remote(
            self.parts[0][1].at[0], self.out_own.at[at.seq], self.own_sems.at[0, i],
            self.own_sems.at[1, at.seq], at.along_sp(target),
        )

    def common_copy(self, i):
        at = self.at
        return remote(
            self.parts[1][1].at[0], self.out_common.at[at.s], self.sp_sems.at[0, i],
            self.sp_sems.at[1, at.s], at.along_sp(at.sp_peer(i)),
        )

    def start(self):
        for which in range(2):
            for mask in range(1, self.at.dp):
                self.dp_copy(which, mask).start()

    def add(self):
        at = self.at
        for which in range(2):
            x, buf = self.parts[which]
            total = x[...]
            for mask in range(1, at.dp):
                self.dp_copy(which, mask).wait_recv()
                total = total + buf[mask]
            buf[0] = total
        for i in range(at.seqs):
            mine, copy = self.own_copy(i)
            pl.when(jnp.logical_not(mine))(copy.start)

            @pl.when(mine)
            def _():
                self.out_own[at.seq] = self.parts[0][1][0]

        self.out_common[at.s] = self.parts[1][1][0]
        for i in range(1, at.sp):
            self.common_copy(i).start()

    def finish(self):
        at = self.at
        for which in range(2):
            for mask in range(1, at.dp):
                self.dp_copy(which, mask).wait_send()
        for i in range(at.seqs):
            mine, copy = self.own_copy(i)
            pl.when(jnp.logical_not(mine))(copy.wait_send)
            sender = i * at.groups + at.s // at.seqs

            @pl.when(sender != at.s)
            def _():
                dst = self.out_own.at[i]
                remote(dst, dst, self.own_sems.at[0, 0], self.own_sems.at[1, i], at.along_sp(at.s)).wait_recv()

        for i in range(1, at.sp):
            slot = at.sp_peer(i)
            dst = self.out_common.at[slot]
            remote(dst, dst, self.sp_sems.at[0, 0], self.sp_sems.at[1, slot], at.along_sp(at.s)).wait_recv()
            self.common_copy(i).wait_send()


def comm_params(number):
    return pltpu.CompilerParams(
        collective_id=number, has_side_effects=True, vmem_limit_bytes=VMEM_LIMIT
    )


class BlockGather:
    @staticmethod
    def scratch(dp, sp, seqs):
        return [dma(5, sp // 2)]

    def __init__(self, place, x, out, sems):
        self.at, self.x, self.out = place, x, out
        self.send, self.recv, self.cross_send, self.cross_recv, self.local = (
            sems.at[i] for i in range(5)
        )

    def chip_at(self, i):
        return lax.rem(self.at.chip + i, self.at.chips)

    def chip_copy(self, i):
        at = self.at
        chip = self.chip_at(i)
        return remote(
            self.x.at[chip // at.per], self.out.at[at.s], self.send.at[i], self.recv.at[at.chip],
            at.along_sp(chip * 2 + at.core),
        )

    def keep(self):
        return pltpu.make_async_copy(self.x.at[self.at.seq], self.out.at[self.at.s], self.local.at[0])

    def crossing(self, k, src):
        at = self.at
        return remote(
            src, self.out.at[k * 2 + at.core], self.cross_send.at[k], self.cross_recv.at[k],
            at.along_sp(at.chip * 2 + 1 - at.core),
        )

    def start(self):
        for i in range(1, self.at.chips):
            self.chip_copy(i).start()
        self.crossing(self.at.chip, self.x.at[self.at.seq]).start()
        self.keep().start()

    def arrive(self, i):
        at = self.at
        k = self.chip_at(i)
        dst = self.out.at[k * 2 + at.core]

        @pl.when(i == 0)
        def _():
            self.keep().wait()

        @pl.when(i != 0)
        def _():
            remote(dst, dst, self.send.at[0], self.recv.at[k], at.along_sp(at.s)).wait_recv()
            self.crossing(k, dst).start()

        return k * 2 + at.core

    def arrive_other(self, i):
        at = self.at
        k = self.chip_at(i)
        dst = self.out.at[k * 2 + 1 - at.core]
        remote(dst, dst, self.cross_send.at[0], self.cross_recv.at[k], at.along_sp(at.s)).wait_recv()
        return k * 2 + 1 - at.core

    def finish(self):
        for i in range(1, self.at.chips):
            self.chip_copy(i).wait_send()
        for k in range(self.at.chips):
            self.crossing(k, self.out.at[k * 2 + self.at.core]).wait_send()


class ColumnGather:
    @staticmethod
    def scratch(dp, sp, seqs):
        return [dma(2, sp), dma(1)] + DpTree.scratch(dp)

    def __init__(self, place, piece, out, along, local, *tree):
        self.at, self.piece, self.out = place, piece, out
        self.along, self.local = along, local.at[0]
        size = place.sp // 2
        self.tree = DpTree(place, lambda p, odd: out.at[p, pl.ds(odd * size, size)], *tree)

    def sp_copy(self, i):
        at = self.at
        target = at.sp_peer(i)
        return remote(
            self.piece(lax.rem(target, at.groups)), self.out.at[at.p, at.s],
            self.along.at[0, i], self.along.at[1, at.s], at.along_sp(target),
        )

    def keep(self):
        at = self.at
        return pltpu.make_async_copy(self.piece(at.group), self.out.at[at.p, at.s], self.local)

    def start(self):
        for i in range(1, self.at.sp):
            self.sp_copy(i).start()
        self.keep().start()

    def along_dp(self, odd):
        at = self.at
        size = at.sp // 2
        for slot in range(odd * size, (odd + 1) * size):

            @pl.when(at.s == slot)
            def _():
                self.keep().wait()

            @pl.when(at.s != slot)
            def _():
                dst = self.out.at[at.p, slot]
                remote(dst, dst, self.along.at[0, 0], self.along.at[1, slot], at.along_sp(at.s)).wait_recv()

        self.tree.start(odd)

    def forward(self):
        self.tree.forward()

    def complete(self):
        self.tree.complete()

    def finish(self):
        for i in range(1, self.at.sp):
            self.sp_copy(i).wait_send()
        self.tree.finish()


class CommonGather:
    @staticmethod
    def scratch(dp, sp, seqs):
        return [dma(2, sp // 2), dma(2, dp), dma(3)]

    def __init__(self, place, x, out, along, across, ends):
        self.at, self.x, self.out = place, x, out
        self.along, self.across, self.ends = along, across, ends

    def chip_copy(self, i):
        at = self.at
        chip = lax.rem(at.chip + i, at.chips)
        return remote(
            self.x, self.out.at[at.core, at.p, at.chip], self.along.at[0, i],
            self.along.at[1, at.chip], at.along_sp(chip * 2 + at.core),
        )

    def keep(self):
        at = self.at
        return pltpu.make_async_copy(self.x, self.out.at[at.core, at.p, at.chip], self.ends.at[0])

    def dp_copy(self, mask):
        at = self.at
        src = self.out.at[at.core, at.p]
        return remote(
            src, src, self.across.at[0, mask], self.across.at[1, mask], at.along_dp(at.masked(mask))
        )

    def crossing(self):
        at = self.at
        src = self.out.at[at.core]
        return remote(
            src, src, self.ends.at[1], self.ends.at[2], at.along_sp(at.chip * 2 + 1 - at.core)
        )

    def start(self):
        for i in range(1, self.at.chips):
            self.chip_copy(i).start()
        self.keep().start()

    def along_dp(self):
        at = self.at
        self.keep().wait()
        for i in range(1, at.chips):
            k = lax.rem(at.chip + i, at.chips)
            dst = self.out.at[at.core, at.p, k]
            remote(dst, dst, self.along.at[0, 0], self.along.at[1, k], at.along_sp(at.s)).wait_recv()
        for mask in range(1, at.dp):
            self.dp_copy(mask).start()

    def cross(self):
        at = self.at
        for mask in range(1, at.dp):
            dst = self.out.at[at.core, at.masked(mask)]
            remote(dst, dst, self.across.at[0, 0], self.across.at[1, mask], at.along_dp(at.p)).wait_recv()
        self.crossing().start()

    def complete(self):
        at = self.at
        dst = self.out.at[1 - at.core]
        remote(dst, dst, self.ends.at[1], self.ends.at[2], at.along_sp(at.s)).wait_recv()

    def finish(self):
        at = self.at
        self.crossing().wait_send()
        for mask in range(1, at.dp):
            self.dp_copy(mask).wait_send()
        for i in range(1, at.chips):
            self.chip_copy(i).wait_send()


def pack_kernel(
    w_bc, w_dt, norm, gate, bc_taps, bc_bias, x_taps, x_bias, dt_bias, a_log, d_skip, out, rows
):
    share, wide = w_bc.shape
    high = out.shape[0] - 16
    out[...] = jnp.zeros(out.shape, BF16)
    out[:share, :wide] = w_bc[...]
    out[:share, wide : wide + w_dt.shape[1]] = w_dt[...]
    rows[...] = jnp.zeros(rows.shape, F32)
    lines = ((0, norm), (1, gate), (6, bc_bias), (7, dt_bias), (8, a_log), (9, d_skip), (14, x_bias))
    for line, ref in lines:
        size = ref.shape[0]
        rows[line : line + 1, :size] = ref[...].astype(F32).reshape(1, size)
    for line, ref in ((2, bc_taps), (10, x_taps)):
        rows[line : line + 4, : ref.shape[1]] = ref[...].astype(F32)
    out[high:, :] = rows[...].astype(BF16)


def run_pack(w_bc, *args):
    share, wide = w_bc.shape
    shape = (-(-share // 16) * 16 + 16, wide + LANES)
    vmem = pl.BlockSpec(memory_space=pltpu.VMEM)
    return pl.pallas_call(
        pack_kernel,
        in_specs=[vmem] * (1 + len(args)),
        out_specs=vmem,
        out_shape=jax.ShapeDtypeStruct(shape, BF16),
        scratch_shapes=[pltpu.VMEM((16, shape[1]), F32)],
        name="pack",
    )(w_bc, *args)


def flatten(values, each, total):
    count, size = values.shape
    lane = iota((size, total), 1)
    place = (iota((size, total), 0) == lane - lane // each * each).astype(BF16)
    wide = dot(values.astype(BF16), place)
    keep = iota((count, total), 0) == iota((count, total), 1) // each
    return jnp.sum(jnp.where(keep, wide, 0.0), axis=0, keepdims=True)


def unpack(place, shards, misc, wb, dt_all, lines, norm, taps, heads, skip, gain):
    share, gate_share, bc_share, x_share, head_share = shards
    high = misc.shape[3] - 16
    wide = misc.shape[4] - LANES
    chans = gain.shape[1]
    count = place.dp * place.sp
    for index in range(count):
        p, s = index // place.sp, index % place.sp
        tile = misc[s % 2, p, s // 2]
        span = slice(index * share, (index + 1) * share)
        wb[span, :wide] = tile[:share, :wide]
        dt_all[span, :] = tile[:share, wide:].astype(F32)
        below = tile[high:, :].astype(F32)
        for line in range(7):
            lines[line, index : index + 1, :] = below[line : line + 1, :]
    own_heads = head_share * place.seqs
    turned = pltpu.roll(dt_all[...], lax.rem(LANES - place.group * own_heads, LANES), 1)
    wb[:, wide:] = jnp.where(iota(turned.shape, 1) < own_heads, turned, 0.0).astype(BF16)
    norm[0:1, :] = flatten(lines[0], share, norm.shape[1])
    mine = lines[1, pl.ds(place.group * place.sp, place.sp), :]
    gain[0:1, :] = flatten(mine, gate_share, chans)
    taps[...] = jnp.zeros(taps.shape, F32)
    for tap in range(5):
        taps[tap : tap + 1, chans:] = flatten(lines[2 + tap], bc_share, wide)
    found = []
    for i in range(place.seqs):
        holder = place.group * place.seqs + i
        tile = misc[lax.rem(holder, 2), place.p, holder // 2]
        below = tile[high:, :].astype(F32)
        taps[0:5, i * x_share : (i + 1) * x_share] = below[10:15, :x_share]
        found.append(below)
    rows = [
        flatten(jnp.concatenate([f[line : line + 1, :LANES] for f in found], axis=0), head_share, LANES)
        for line in (7, 8, 9)
    ]
    rows = [jnp.where(iota((1, LANES), 1) < own_heads, row, 0.0) for row in rows]
    heads[...] = jnp.zeros(heads.shape, F32)
    heads[0:1, :] = rows[0]
    heads[1:2, :] = jnp.exp(rows[1])
    owner = iota((LANES, chans), 0) == iota((LANES, chans), 1) // P_SIZE
    skip[...] = jnp.broadcast_to(dot(rows[2].astype(BF16), owner.astype(BF16)), skip.shape)


def scan_block(wide, chans, x, bd, taps, heads, skip, mixed, enter, ext, halo, state):
    rows = x.shape[0]
    pairs = chans // LANES
    low_half = iota((rows, LANES), 1) < P_SIZE
    ext[0:8, :] = halo[...]
    ext[8 : 8 + rows, :chans] = x.astype(F32)
    ext[8 : 8 + rows, chans:] = bd[:, :wide].astype(F32)
    halo[...] = ext[rows : rows + 8, :]
    pre = conv_pre(ext, rows, taps)
    act = (pre * jax.nn.sigmoid(pre)).astype(BF16)
    half = wide // 2
    bmat = act[:, chans : chans + half]
    cmat = act[:, chans + half :]
    _, steps, logs = steps_of(bd[:, wide:], heads)
    earlier = iota((rows, rows), 0) >= iota((rows, rows), 1)
    cumul = select_rows(earlier, logs)
    cumul_t = cumul.T
    last = cumul[rows - 1 :, :]
    scores = dot(cmat, bmat, ((1,), (1,)))
    grown = jnp.exp(cumul)
    to_end = steps * jnp.exp(last - cumul)
    final = jnp.exp(last)
    entering = state[...]
    entering_half = entering.astype(BF16)
    enter[...] = entering_half
    across = dot(cmat, entering_half)
    for pair in range(pairs):
        lanes = slice(pair * LANES, (pair + 1) * LANES)
        weights = []
        for head in (2 * pair, 2 * pair + 1):
            differ = cumul[:, head : head + 1] - cumul_t[head : head + 1, :]
            decay = jnp.where(earlier, jnp.exp(jnp.minimum(differ, 0.0)), 0.0)
            weights.append((decay * scores).astype(BF16))
        values = act[:, lanes].astype(F32)
        scaled = (values * spread(steps, pair, low_half)).astype(BF16)
        total = dot(jnp.concatenate(weights, axis=1), stack_heads(scaled, low_half))
        total = total + spread(grown, pair, low_half) * across[:, lanes]
        total = total + skip[0:1, lanes] * values
        mixed[:, lanes] = total.astype(BF16)
        ending = (values * spread(to_end, pair, low_half)).astype(BF16)
        state[:, lanes] = entering[:, lanes] * spread(final, pair, low_half[0:1, :]) + dot(
            bmat, ending, ((0,), (0,))
        )


def forward_kernel(
    dp, sp, seqs, wide, inner,
    shards, w_ref, misc_ref, hid_ref, o_ref, cot_ref,
    normed_out, x_out, bd_out, enter_out, dgate_out, dy_out, part_out, tg_out, to_out,
    wx_out, wg_out, wb_out, norm, taps, heads, skip,
    misc, dt_all, lines, gain, hid, wx_all, wb, rows_out, wg, cot, normed, x, bd, mixed, enter, gate, d_gated, gated, dgate, dy,
    part, tg, to, ext, halo, state, sums, mine, got, saves, sum_sems, *sems,
):
    place = Place(dp, sp, seqs)
    chans = gain.shape[1]
    chips = place.chips
    blocks, rows, width = hid.shape
    rest = list(sems)

    def take(scratch):
        taken = rest[: len(scratch)]
        del rest[: len(scratch)]
        return taken

    def columns(first):
        return lambda g: w_ref.at[:, pl.ds(pl.multiple_of(first + g * chans, LANES), chans)]

    half = ColumnGather.scratch(dp, sp, seqs)
    wx_comm = ColumnGather(place, columns(inner), wx_all, *take(half))
    wg_comm = ColumnGather(place, columns(0), wg, *take(half))
    misc_comm = CommonGather(place, misc_ref, misc, *take(CommonGather.scratch(dp, sp, seqs)))
    out_comm = OutGather(place, o_ref, rows_out, *take(OutGather.scratch(dp, sp, seqs)))
    hid_comm = BlockGather(place, hid_ref, hid, *take(BlockGather.scratch(dp, sp, seqs)))
    cot_comm = BlockGather(place, cot_ref, cot, *take(BlockGather.scratch(dp, sp, seqs)))
    place.meet(more=out_comm.ways.meet(True))
    misc_comm.start()
    wx_comm.start()
    halo[...] = jnp.zeros(halo.shape, F32)
    state[...] = jnp.zeros(state.shape, F32)
    sums[...] = jnp.zeros(sums.shape, F32)
    for odd in range(2):
        wx_comm.along_dp(odd)
    wg_comm.start()
    out_comm.start()
    misc_comm.along_dp()
    wx_comm.forward()
    misc_comm.cross()
    for odd in range(2):
        out_comm.along_dp(odd)
    hid_comm.start()
    for odd in range(2):
        wg_comm.along_dp(odd)
    hid_comm.arrive(0)
    misc_comm.complete()
    unpack(place, shards, misc, wb, dt_all, lines, norm, taps, heads, skip, gain)
    wg_comm.forward()
    hid_comm.arrive(1)
    cot_comm.start()
    for i in range(2, chips):
        hid_comm.arrive(i)
    out_comm.forward()
    for i in range(chips):
        hid_comm.arrive_other(i)
    wx_comm.complete()
    keeps = [
        pltpu.make_async_copy(src, dst, saves.at[7, i])
        for i, (src, dst) in enumerate(((wx_all, wx_out), (wb, wb_out)))
    ]
    for keep in keeps:
        keep.start()

    def save(src, dst, index, b):
        return pltpu.make_async_copy(src.at[b], dst.at[b], saves.at[index, b])

    early = ((normed, normed_out), (x, x_out), (bd, bd_out), (enter, enter_out))
    late = ((dgate, dgate_out), (dy, dy_out), (part, part_out))

    def first(b, carry):
        hidden = hid[b].astype(F32)
        scale = lax.rsqrt(jnp.mean(hidden * hidden, axis=-1, keepdims=True) + EPS)
        normed[b] = (hidden * scale * norm[0:1, :]).astype(BF16)
        x[b] = dot(normed[b], wx_all[...].reshape(width, chans)).astype(BF16)
        bd[b] = dot(normed[b], wb[...]).astype(BF16)
        scan_block(
            wide, chans, x[b], bd[b], taps, heads, skip, mixed.at[b], enter.at[b], ext, halo, state
        )
        for index, (src, dst) in enumerate(early):
            save(src, dst, index, b).start()
        return carry

    lax.fori_loop(0, blocks, first, 0)
    wg_comm.complete()
    keeps.append(pltpu.make_async_copy(wg, wg_out, saves.at[7, 2]))
    keeps[-1].start()
    lane = iota((rows, LANES), 1)

    def sum_copies(n):
        return [
            remote(
                mine.at[n], got.at[n, i], sum_sems.at[2 * n, i], sum_sems.at[2 * n + 1, i],
                place.along_sp(place.group_peer(i)),
            )
            for i in range(1, place.groups)
        ]

    def send_sums(n):
        mine[n] = sums[...].T[:blocks]
        for copy in sum_copies(n):
            copy.start()

    def take_sums(n):
        total = mine[n]
        for i, copy in enumerate(sum_copies(n)):
            copy.wait_recv()
            total = total + got[n, i + 1]
        sums[...] = jnp.concatenate([total, jnp.zeros((LANES - blocks, rows), F32)], axis=0).T

    def column(b):
        return jnp.sum(jnp.where(lane == b, sums[...], 0.0), axis=1, keepdims=True)

    def activated(b):
        gate_f = gate[b].astype(F32)
        sig = jax.nn.sigmoid(gate_f)
        return gate_f, sig, mixed[b].astype(F32) * gate_f * sig

    def second(b, carry):
        gate[b] = dot(normed[b], wg[...].reshape(width, chans)).astype(BF16)
        _, _, value = activated(b)
        square = jnp.sum(value * value, axis=1, keepdims=True)
        sums[...] = jnp.where(lane == b, square, sums[...])
        return carry

    lax.fori_loop(0, blocks, second, 0)
    send_sums(0)
    out_comm.complete()
    take_sums(0)
    scales = lax.rsqrt(sums[...] * (1.0 / inner) + EPS)
    sums[...] = scales

    def third(b, carry):
        _, _, value = activated(b)
        gated[b] = (value * column(b) * gain[0:1, :]).astype(BF16)
        part[b] = dot(gated[b], rows_out[...].reshape(chans, width)).astype(BF16)
        save(part, part_out, 6, b).start()
        return carry

    lax.fori_loop(0, blocks, third, 0)
    got[0, 0] = sums[...].T[:blocks]

    def fourth(b):
        d_gated[b] = dot(cot[b], rows_out[...].reshape(chans, width), ((1,), (1,)))
        _, _, value = activated(b)
        cross = jnp.sum(value * d_gated[b] * gain[0:1, :], axis=1, keepdims=True)
        sums[...] = jnp.where(lane == b, cross, sums[...])

    def own_core(i, carry):
        fourth(cot_comm.arrive(i))
        return carry

    def other_core(i, carry):
        fourth(cot_comm.arrive_other(i))
        return carry

    lax.fori_loop(0, chips, own_core, 0)
    lax.fori_loop(0, chips, other_core, 0)
    send_sums(1)
    everything = blocks * rows
    slots = sp // 2
    keep_to = []
    for half in range(2):
        size = chans // 2
        lanes = gated[:, :, half * size : (half + 1) * size].reshape(everything, size)
        value = dot(lanes, cot[...].reshape(everything, width), ((0,), (0,)))
        span = pl.ds(half * slots, slots)
        to[span] = value.astype(BF16).reshape((slots,) + to.shape[1:])
        keep_to.append(pltpu.make_async_copy(to.at[span], to_out.at[span], saves.at[8, half]))
        keep_to[-1].start()
    take_sums(1)
    crosses = sums[...]
    scales = jnp.concatenate([got[0, 0], jnp.zeros((LANES - blocks, rows), F32)], axis=0).T

    def fifth(b, carry):
        scale = jnp.sum(jnp.where(lane == b, scales, 0.0), axis=1, keepdims=True)
        mean = column(b) * scale * (1.0 / inner)
        gate_f, sig, value = activated(b)
        unit = value * scale
        back = scale * (d_gated[b] * gain[0:1, :] - unit * mean)
        dy[b] = (back * gate_f * sig).astype(BF16)
        dgate[b] = (
            back * mixed[b].astype(F32) * sig * (1.0 + gate_f * (1.0 - sig))
        ).astype(BF16)
        for index, (src, dst) in enumerate(late[:2]):
            save(src, dst, 4 + index, b).start()
        return carry

    lax.fori_loop(0, blocks, fifth, 0)
    tile = width // dp
    keep_tg = []
    for p in range(dp):
        lanes = normed[:, :, p * tile : (p + 1) * tile].reshape(everything, tile)
        value = dot(lanes, dgate[...].reshape(everything, chans), ((0,), (0,)))
        tg[p] = value.astype(BF16).reshape(tg.shape[1:])
        keep_tg.append(pltpu.make_async_copy(tg.at[p], tg_out.at[p], saves.at[7, 3 + p]))
        keep_tg[-1].start()
    for n in range(2):
        for copy in sum_copies(n):
            copy.wait_send()
    for comm in (misc_comm, wx_comm, wg_comm, out_comm, hid_comm, cot_comm):
        comm.finish()
    for keep in keeps + keep_tg + keep_to:
        keep.wait()
    for index, (src, dst) in enumerate(early + late):
        for b in range(blocks):
            save(src, dst, index, b).wait()


def run_forward(dp, sp, seqs, wide, inner, shards, w_zx, misc, hidden, w_out, cotangent):
    share = w_zx.shape[0]
    _, rows, width = hidden.shape
    blocks, chans, cols = sp, inner * seqs // sp, misc.shape[1]
    states = wide // 2
    columns = (dp, sp, share, chans)
    w_rows = (sp,) + w_out.shape
    tokens = lambda n: (blocks, rows, n)
    shapes = [
        tokens(width), tokens(chans), tokens(cols), (blocks, states, chans), tokens(chans),
        tokens(chans), tokens(width), columns, w_rows, columns, columns, (width, cols),
    ]
    params = [(8, width), (8, chans + wide), (8, LANES), (8, chans)]
    half = lambda shape: pltpu.VMEM(shape, BF16)
    full = lambda *shape: pltpu.VMEM(shape, F32)
    vmem = pl.BlockSpec(memory_space=pltpu.VMEM)
    return pl.pallas_call(
        functools.partial(forward_kernel, dp, sp, seqs, wide, inner, shards),
        in_specs=[ANY] * 5,
        out_specs=[ANY] * len(shapes) + [vmem] * len(params),
        out_shape=[jax.ShapeDtypeStruct(shape, BF16) for shape in shapes]
        + [jax.ShapeDtypeStruct(shape, F32) for shape in params],
        scratch_shapes=[
            half((2, dp, sp // 2) + misc.shape),
            full(width, LANES),
            full(7, dp * sp, cols),
            full(8, chans),
            half(tokens(width)),
            half(columns),
            half((width, cols)),
            half(w_rows),
            half(columns),
            half(tokens(width)),
            half(tokens(width)), half(tokens(chans)), half(tokens(cols)), half(tokens(chans)),
            half((blocks, states, chans)),
            half(tokens(chans)), full(*tokens(chans)), half(tokens(chans)), half(tokens(chans)),
            half(tokens(chans)), half(tokens(width)),
            half(columns),
            half(w_rows),
            full(rows + 8, chans + wide),
            full(8, chans + wide),
            full(states, chans),
            full(rows, LANES),
            full(2, blocks, rows),
            full(2, sp // seqs, blocks, rows),
            dma(9, max(blocks, dp + 3)),
            dma(4, sp // seqs),
        ]
        + ColumnGather.scratch(dp, sp, seqs) * 2
        + CommonGather.scratch(dp, sp, seqs)
        + OutGather.scratch(dp, sp, seqs)
        + BlockGather.scratch(dp, sp, seqs) * 2,
        compiler_params=comm_params(2),
        name="forward",
    )(w_zx, misc, hidden, w_out, cotangent)


def backward_kernel(
    dp, sp, seqs, wide, chans,
    dy, x, x_before, bd, bd_before, dgate, enter, taps, heads, skip, norm, wg_ref, wx_ref, wb_ref,
    normed_ref, out_part, terms_out, terms_gate, hid_ref, cot_ref, w_zx_ref, w_bc_ref, w_out_ref,
    hidden_out, grad_hidden, grad_zx, grad_bc, grad_dt, norm_sum, grad_out, gate_sum, own_small, common_small,
    ext, gext, halo, dstate, dtaps, dheads, dskip, dx, dbd, normed, part,
    hid, cot, w_zx, w_bc, w_out, wg, wx, wb, loads, tb, og, ob, oo, own, *scratch,
):
    step, steps = pl.program_id(0), pl.num_programs(0)
    chunk = steps - 1 - step
    place = Place(dp, sp, seqs)
    chips = place.chips
    blocks, rows, width = part.shape
    rest = list(scratch)

    def take(n):
        taken = rest[:n]
        del rest[:n]
        return taken

    out_red = BlockReduce(place, out_part, *take(6))
    dn_red = BlockReduce(place, part, None, *take(5))
    gate_red = ShardReduce(place, terms_gate, og, True, *take(5))
    b_red = ShardReduce(place, tb, ob, False, *take(4))
    out_grads = OutReduce(place, terms_out, oo, *take(6))
    few = SmallReduce(place, own, dtaps.at[:, pl.ds(chans, wide)], *take(7))
    x_reds, x_parts = [], []
    while rest:
        tx, landed = take(2)
        x_reds.append((tx, ShardReduce(place, tx, landed, False, *take(4))))
        x_parts.append(landed)
    weight_loads = [
        pltpu.make_async_copy(src, dst, loads.at[6 + i])
        for i, (src, dst) in enumerate(((wg_ref, wg), (wx_ref, wx), (wb_ref, wb)))
    ]
    last_loads = [
        pltpu.make_async_copy(src, dst, loads.at[i])
        for i, (src, dst) in enumerate(
            (
                (normed_ref, normed), (hid_ref, hid), (cot_ref, cot), (w_zx_ref, w_zx),
                (w_bc_ref, w_bc), (w_out_ref, w_out),
            )
        )
    ]

    @pl.when(step == 0)
    def _():
        for load in weight_loads:
            load.start()
        place.meet(more=out_grads.ways.meet(False))
        for k in range(chips):
            out_red.start(k)
        gate_red.tree.start()
        for load in last_loads:
            load.start()

    scan_backward(
        wide, chans, dy, x, x_before, bd, bd_before, taps, heads, skip, enter,
        dx.at[chunk], dbd.at[chunk], dtaps, dheads, dskip, ext, gext, halo, dstate,
    )

    @pl.when(step == 0)
    def _():
        for load in weight_loads:
            load.wait()

    across = ((1,), (1,))
    total = dot(dgate[...], wg[...], across) + dot(dx[chunk], wx[...], across)
    part[chunk] = (total + dot(dbd[chunk], wb[...], across)).astype(BF16)

    def both_ways(i, fn):
        for k in (place.chip + i, place.chip - i):
            pl.when((k >= 0) & (k < chips))(functools.partial(fn, k))

    for i in range(chips - 1, -1, -1):

        @pl.when(step == min(chips - 1 - i, chips - 2))
        def _():
            if i:
                both_ways(i, out_red.collect)
            else:
                out_red.collect(place.chip)

        @pl.when(step == min(chips + 2 - i, steps - 1))
        def _():
            if i:
                both_ways(i, out_red.settle)
            else:
                out_red.settle(place.chip)

    levels = len(place.bits)

    def at_step(when, fn):
        pl.when(step == min(when, steps - 1))(fn)

    at_step(1, out_grads.tree.start)
    for i in range(levels):
        at_step(3 + 2 * i, functools.partial(gate_red.tree.step, i))
        at_step(5 + i, functools.partial(out_grads.tree.step, i))
    at_step(1 + 2 * levels, gate_red.spread)
    at_step(4 + levels, out_grads.spread)

    @pl.when(lax.rem(step, 2) == 1)
    def _():
        dn_red.start(chunk // 2)

    @pl.when((lax.rem(step, 2) == 0) & (step >= 2))
    def _():
        dn_red.collect(chunk // 2 + 1)

    wait = 6

    @pl.when((lax.rem(step, 2) == 0) & (step >= wait))
    def _():
        dn_red.settle(chunk // 2 + wait // 2)

    @pl.when(step == steps - 1)
    def _():
        for load in last_loads:
            load.wait()
        rows_all = blocks * rows
        share_rows = tb.shape[1] * tb.shape[2]
        size = chans // len(x_reds)
        own[:, :chans] = dtaps[:, :chans]
        own[5:6, :chans] = dskip[0:1, :]
        own[:, chans:] = dheads[...]
        few.start()

        def terms(red, out, values):
            for p in range(dp):
                columns = normed[:, :, p * share_rows : (p + 1) * share_rows]
                value = dot(columns.reshape(rows_all, share_rows), values, ((0,), (0,)))
                out[p] = value.astype(BF16).reshape(out.shape[1:])
            red.tree.start()

        late = [
            (red, tx, lambda n=n: dx[:, :, n * size : (n + 1) * size].reshape(rows_all, size))
            for n, (tx, red) in enumerate(x_reds)
        ]
        late.append((b_red, tb, lambda: dbd[...].reshape(rows_all, -1)))
        settles = list(range(chips - 1 - (steps - 1 - wait) // 2 - 1, -1, -1))
        for turn in range(len(late) + levels):
            for place_in, (red, out, values) in enumerate(late):
                stage = turn - place_in
                if stage == 0:
                    terms(red, out, values())
                elif 0 < stage <= levels:
                    red.tree.step(stage - 1)
                    if stage == levels:
                        red.spread()
            if turn == 0:
                dn_red.collect(jnp.int32(0))
                dn_red.settle(jnp.int32(settles.pop(0)))
            elif turn == 2:
                few.add()
            if turn and settles:
                dn_red.settle(jnp.int32(settles.pop(0)))
        for k in settles:
            dn_red.settle(jnp.int32(k))
        out_red.finish()
        hidden_out[...] = (hid[...].astype(F32) + out_red.total[...].astype(F32)).astype(BF16)
        out_grads.finish()
        value = oo[0].astype(F32)
        for seq in range(1, seqs):
            value = value + oo[seq].astype(F32)
        grad_out[...] = value
        gate_sum[...] = jnp.broadcast_to(
            jnp.sum(value * w_out[...].astype(F32), axis=1, keepdims=True), gate_sum.shape
        )
        gate_red.finish()
        by_seq = lambda ref, g: functools.reduce(
            jnp.add, [ref[seq * place.groups + g].astype(F32) for seq in range(seqs)]
        )
        inner = grad_zx.shape[1] // 2
        norm_total = jnp.zeros((grad_zx.shape[0], 1), F32)

        def write(first, value):
            lanes = slice(first, first + value.shape[1])
            grad_zx[:, lanes] = value
            return jnp.sum(value * w_zx[:, lanes].astype(F32), axis=1, keepdims=True)

        for g in range(place.groups):
            norm_total = norm_total + write(g * chans, by_seq(og, g))
        dn_red.finish()
        for seq in range(seqs):
            value = hid[seq].astype(F32)
            scale = lax.rsqrt(jnp.mean(value * value, axis=-1, keepdims=True) + EPS)
            unit = value * scale
            weighted = dn_red.total[seq].astype(F32) * norm[0:1, :]
            weighted = weighted - unit * jnp.mean(weighted * unit, axis=-1, keepdims=True)
            grad_hidden[seq] = (cot[seq].astype(F32) + scale * weighted).astype(BF16)
        few.finish()
        own_small[...] = functools.reduce(jnp.add, [few.out_own[seq] for seq in range(seqs)])
        common_small[...] = functools.reduce(jnp.add, [few.out_common[slot] for slot in range(sp)])
        for n, landed in enumerate(x_parts):
            x_reds[n][1].finish()
            for g in range(place.groups):
                norm_total = norm_total + write(inner + g * chans + n * size, by_seq(landed, g))
        b_red.finish()
        value = functools.reduce(jnp.add, [ob[slot, :, :wide].astype(F32) for slot in range(sp)])
        grad_bc[...] = value
        norm_total = norm_total + jnp.sum(value * w_bc[...].astype(F32), axis=1, keepdims=True)
        norm_sum[...] = jnp.broadcast_to(norm_total, norm_sum.shape)
        for g in range(place.groups):
            grad_dt[g] = functools.reduce(
                jnp.add,
                [ob[seq * place.groups + g, :, wide:].astype(F32) for seq in range(seqs)],
            )


def run_backward(
    dp, sp, seqs, dy, x, bd, dgate, enter, taps, heads, skip, norm, wg, wx, wb,
    normed, out_part, terms_out, terms_gate, hidden, cotangent, w_zx, w_bc, w_out, wide,
):
    blocks, rows, chans = x.shape
    states = wide // 2
    cols, width = bd.shape[2], normed.shape[2]
    share = terms_gate.shape[2]
    groups = sp // seqs
    pieces = max(n for n in (1, 2, PIECES) if chans % (n * LANES) == 0)
    back = lambda i: blocks - 1 - i
    block = lambda n: pl.BlockSpec((None, rows, n), lambda i: (back(i), 0, 0))
    whole = lambda a: pl.BlockSpec(a.shape, lambda i: (0,) * a.ndim)
    before = lambda n: pl.BlockSpec(
        (None, 16, n), lambda i: (jnp.maximum(back(i) - 1, 0), rows // 16 - 1, 0)
    )
    outs = [
        jax.ShapeDtypeStruct(hidden.shape, BF16),
        jax.ShapeDtypeStruct(hidden.shape, BF16),
        jax.ShapeDtypeStruct(w_zx.shape, F32),
        jax.ShapeDtypeStruct(w_bc.shape, F32),
        jax.ShapeDtypeStruct((groups, share, LANES), F32),
        jax.ShapeDtypeStruct((share, LANES), F32),
        jax.ShapeDtypeStruct(w_out.shape, F32),
        jax.ShapeDtypeStruct((w_out.shape[0], LANES), F32),
        jax.ShapeDtypeStruct((8, chans + LANES), F32),
        jax.ShapeDtypeStruct((8, wide), F32),
    ]
    vmem = lambda a: pltpu.VMEM(a.shape, a.dtype)
    scratch = [
        pltpu.VMEM((rows + 8, chans + wide), F32),
        pltpu.VMEM((rows + 8, chans + wide), F32),
        pltpu.VMEM((8, chans + wide), F32),
        pltpu.VMEM((states, chans), F32),
        pltpu.VMEM((8, chans + wide), F32),
        pltpu.VMEM((8, LANES), F32),
        pltpu.VMEM((8, chans), F32),
        pltpu.VMEM((blocks, rows, chans), BF16),
        pltpu.VMEM((blocks, rows, cols), BF16),
        vmem(normed),
        pltpu.VMEM((blocks, rows, width), BF16),
        vmem(hidden), vmem(cotangent), vmem(w_zx), vmem(w_bc), vmem(w_out),
        vmem(wg), vmem(wx), vmem(wb),
        dma(9),
        pltpu.VMEM((dp, sp, share, cols), BF16),
        pltpu.VMEM((sp, share, chans), BF16),
        pltpu.VMEM((sp, share, cols), BF16),
        pltpu.VMEM((seqs,) + w_out.shape, BF16),
        pltpu.VMEM((8, chans + LANES), F32),
    ]
    scratch += BlockReduce.scratch(dp, sp, seqs, rows, width, True)
    scratch += BlockReduce.scratch(dp, sp, seqs, rows, width, False)
    scratch += ShardReduce.scratch(dp, sp, (share, chans), True)
    scratch += ShardReduce.scratch(dp, sp, (share, cols), False)
    scratch += OutReduce.scratch(dp, sp, seqs, w_out.shape)
    scratch += SmallReduce.scratch(dp, sp, seqs, (8, chans + LANES), (8, wide))
    for _ in range(pieces):
        shape = (share, chans // pieces)
        scratch += [pltpu.VMEM((dp, sp) + shape, BF16), pltpu.VMEM((sp,) + shape, BF16)]
        scratch += ShardReduce.scratch(dp, sp, shape, False)
    return pl.pallas_call(
        functools.partial(backward_kernel, dp, sp, seqs, wide, chans),
        grid=(blocks,),
        in_specs=[
            block(chans), block(chans), before(chans), block(cols), before(cols), block(chans),
            pl.BlockSpec((None, states, chans), lambda i: (back(i), 0, 0)),
            whole(taps), whole(heads), whole(skip), whole(norm),
        ]
        + [ANY] * 12,
        out_specs=[whole(out) for out in outs],
        out_shape=outs,
        scratch_shapes=scratch,
        compiler_params=comm_params(4),
        name="backward",
    )(
        dy, x, x, bd, bd, dgate, enter, taps, heads, skip, norm, wg, wx, wb,
        normed, out_part, terms_out, terms_gate, hidden, cotangent, w_zx, w_bc, w_out,
    )


def finish_kernel(
    dp, sp, seqs,
    hidden, grad, zx, bc, dt_parts, norm_sum, out, gate_sum, own, common, w_dt, norm_gain, gate_gain,
    hidden_to, grad_to, zx_to, bc_to, dt_to, norm_to, bc_taps, bc_bias, x_taps, x_bias, g_dt, g_log,
    g_skip, gate_to, out_to, tall,
):
    place = Place(dp, sp, seqs)
    for src, dst in ((hidden, hidden_to), (grad, grad_to), (zx, zx_to), (bc, bc_to), (out, out_to)):
        dst[...] = src[...]
    share, heads = w_dt.shape
    each = heads // place.groups
    lane = iota((share, LANES), 1)
    value = jnp.zeros((share, LANES), F32)
    for g in range(place.groups):
        part = jnp.where(lane < each, dt_parts[g], 0.0)
        value = value + (pltpu.roll(part, g * each, 1) if g else part)
    value = value[:, :heads]
    dt_to[...] = value
    dt_sum = jnp.sum(value * w_dt[...].astype(F32), axis=1, keepdims=True)

    def row(column):
        size = column.shape[0]
        wide = -(-size // LANES) * LANES
        tall[:size, :] = jnp.broadcast_to(column, (size, LANES))
        return tall[:wide, :].T[0:1, :size]

    share_sum = row(norm_sum[:, 0:1] + dt_sum)
    norm_to[...] = (share_sum / norm_gain[...].astype(F32).reshape(1, share)).reshape(share)
    size = gate_gain.shape[0]
    gate_to[...] = (row(gate_sum[:, 0:1]) / gate_gain[...].astype(F32).reshape(1, size)).reshape(size)
    x_share, bc_share = x_bias.shape[0], bc_bias.shape[0]
    chans = own.shape[1] - LANES
    place_in = lax.rem(place.s, place.seqs)
    mine = jnp.zeros((8, x_share), F32)
    for i in range(place.seqs):
        mine = mine + jnp.where(place_in == i, own[:, i * x_share : (i + 1) * x_share], 0.0)
    x_taps[...] = mine[0:4]
    x_bias[...] = mine[4:5].reshape(x_share)
    head_share = g_dt.shape[0]
    owner = (iota((x_share, LANES), 0) // P_SIZE == iota((x_share, LANES), 1)).astype(F32)
    skips = dot(mine, owner, precision=HIGH)[5:6, :head_share]
    g_skip[...] = skips.reshape(head_share)
    per_head = own[:, chans:]
    turned = per_head
    for i in range(1, place.seqs):
        turned = jnp.where(place_in == i, pltpu.roll(per_head, LANES - i * head_share, 1), turned)
    g_dt[...] = turned[0:1, :head_share].reshape(head_share)
    g_log[...] = turned[1:2, :head_share].reshape(head_share)
    wide = common.shape[1]
    index = place.p * sp + place.s
    pick = (iota((wide, LANES), 0) == iota((wide, LANES), 1) + index * bc_share).astype(F32)
    mine = dot(common[...], pick, precision=HIGH)[:, :bc_share]
    bc_taps[...] = mine[0:4]
    bc_bias[...] = mine[4:5].reshape(bc_share)


def run_finish(dp, sp, seqs, x_share, head_share, bc_share, *args):
    hidden, grad, zx, bc, _, _, out, _, _, _, w_dt, norm_gain, gate_gain = args
    vmem = pl.BlockSpec(memory_space=pltpu.VMEM)
    shapes = [
        hidden.shape, grad.shape, zx.shape, bc.shape, w_dt.shape, norm_gain.shape, (4, bc_share),
        (bc_share,), (4, x_share), (x_share,), (head_share,), (head_share,), (head_share,),
        gate_gain.shape, out.shape,
    ]
    kinds = [BF16, BF16] + [F32] * 13
    tall = max(-(-n // LANES) * LANES for n in (norm_gain.shape[0], gate_gain.shape[0]))
    return pl.pallas_call(
        functools.partial(finish_kernel, dp, sp, seqs),
        in_specs=[vmem] * len(args),
        out_specs=[vmem] * len(shapes),
        out_shape=[jax.ShapeDtypeStruct(s, k) for s, k in zip(shapes, kinds)],
        scratch_shapes=[pltpu.VMEM((tall, LANES), F32)],
        compiler_params=pltpu.CompilerParams(vmem_limit_bytes=VMEM_LIMIT),
        name="finish",
    )(*args)


def on_device(
    dp, sp,
    hidden_in, w_zx, w_bc, w_dt, norm_gain, conv_bc_weight, conv_bc_bias,
    conv_x_weight, conv_x_bias, dt_bias, a_log, d_skip, gate_gain, w_out, cotangent,
):
    seqs, width = hidden_in.shape[0], hidden_in.shape[2]
    wide, heads = w_bc.shape[1], w_dt.shape[1]
    inner = heads * P_SIZE
    chans = inner * seqs // sp
    x_share, head_share, bc_share = conv_x_bias.shape[0], dt_bias.shape[0], conv_bc_bias.shape[0]
    misc = run_pack(
        w_bc, w_dt, norm_gain, gate_gain, conv_bc_weight.T, conv_bc_bias, conv_x_weight.T,
        conv_x_bias, dt_bias, a_log, d_skip,
    )
    shards = (w_zx.shape[0], gate_gain.shape[0], bc_share, x_share, head_share)
    (normed, x, bd, entering, dgate, dy, out_part, terms_gate, terms_out, wx, wg, wb,
     norm, taps, head_rows, skip) = run_forward(
        dp, sp, seqs, wide, inner, shards, w_zx, misc, hidden_in, w_out, cotangent
    )
    grads = run_backward(
        dp, sp, seqs, dy, x, bd, dgate, entering, taps, head_rows, skip, norm,
        wg.reshape(width, chans), wx.reshape(width, chans), wb, normed, out_part, terms_out,
        terms_gate, hidden_in, cotangent, w_zx, w_bc, w_out, wide,
    )
    results = list(
        run_finish(dp, sp, seqs, x_share, head_share, bc_share, *grads, w_dt, norm_gain, gate_gain)
    )
    for taps_at in (6, 8):
        results[taps_at] = results[taps_at].T
    return tuple(results)


def solution(mesh):
    both = P(("dp", "sp"))
    rows = P(("dp", "sp"), None)
    tokens = P("dp", "sp", None)
    return jax.shard_map(
        functools.partial(on_device, mesh.shape["dp"], mesh.shape["sp"]),
        mesh=mesh,
        in_specs=(
            tokens, rows, rows, rows, both, rows, both, P("sp", None), P("sp"), P("sp"),
            P("sp"), P("sp"), both, rows, tokens,
        ),
        out_specs=(
            tokens, tokens, rows, rows, rows, both, rows, both, P("sp", None), P("sp"),
            P("sp"), P("sp"), P("sp"), both, rows,
        ),
        check_vma=False,
    )
```
